32 devices in a mesh: ctx: 2 (over core), seq: 16 (over z, y, x).
Axes of the slice: x: 2, y: 2, z: 4, core: 2. Of those that a mesh axis runs over, the one named last changes fastest.
Arguments:
- hidden: bfloat16 [2, 2048, 1024], P('ctx', 'seq'), may hold values from -6 to 6
- out_grad: bfloat16 [2, 2048, 1024], P('ctx', 'seq'), may hold values from -6 to 6
- resets: int32 [2, 2048], P('ctx', 'seq'), may hold values from 0 to 1, as said below
- valid: int32 [2], P('ctx'), may hold values from 256 to 2048, as said below
- norm_gain: bfloat16 [1024], P('seq'), may hold values from 0.099609375 to 1.8984375
- in_weight: bfloat16 [1024, 4096], P('seq'), may hold values from -0.1875 to 0.1875
- conv_weight: bfloat16 [2048, 4], P('seq'), may hold values from -0.5 to 0.5
- conv_bias: bfloat16 [2048], P('seq'), may hold values from -0.5 to 0.5
- x_weight: bfloat16 [2048, 96], P('seq'), may hold values from -0.125 to 0.125
- dt_weight: bfloat16 [2048, 64], P('seq'), may hold values from -0.75 to 0.75
- dt_bias: bfloat16 [2048], P('seq'), may hold values from -5 to -3
- a_log: bfloat16 [2048, 16], P('seq'), may hold values from -17 to 3
- skip_gain: bfloat16 [2048], P('seq'), may hold values from 0.5 to 1.5
- out_weight: bfloat16 [2048, 1024], P('seq'), may hold values from -0.0625 to 0.0625
Outputs:
- out: bfloat16 [2, 2048, 1024], P('ctx', 'seq')
- grad_hidden: float32 [2, 2048, 1024], P('ctx', 'seq')
- grad_norm_gain: float32 [1024], P('seq')
- grad_in_weight: float32 [1024, 4096], P('seq')
- grad_conv_weight: float32 [2048, 4], P('seq')
- grad_conv_bias: float32 [2048], P('seq')
- grad_x_weight: float32 [2048, 96], P('seq')
- grad_dt_weight: float32 [2048, 64], P('seq')
- grad_dt_bias: float32 [2048], P('seq')
- grad_a_log: float32 [2048, 16], P('seq')
- grad_skip_gain: float32 [2048], P('seq')
- grad_out_weight: float32 [2048, 1024], P('seq')
The draws below stay inside these ranges and needn't reach their ends.
Inputs may be any that keep to these rules, and one draw needn't show every extreme that they name: Tokens t >= valid[c] of context c are padding; one context, drawn from the seed, is full. `resets`: 1 marks the first token of a cluster. In the full context one cluster starts within the first 128 tokens and ends within the last 128.
All inputs are finite; a program needn't handle non-finite values.
Results may differ from the reference program's by a relative error of at most 0.0081.
Values may be sent and summed in bfloat16 or wider, within the bound.
A program may use at most 448 MiB of HBM per device.

```python
import jax
import jax.numpy as jnp
from jax import lax

D = 1024
INNER = 2048
STATE = 16
CONV = 4
DT_RANK = 64
TOK_DEV = 128
CLUSTER = 1024
L = 2048
N_CTX = 2


def full_context(key):
    return jax.random.randint(key, (), 0, N_CTX)


def draw_valid(key, part):
    chosen = full_context(key)
    key = jax.random.fold_in(key, 11)
    partial_len = jax.random.randint(key, (N_CTX,), L // 8, L // 2 + 1)
    return jnp.where(jnp.arange(N_CTX) == chosen, L, partial_len).astype(jnp.int32)


def draw_resets(key, part):
    chosen = full_context(key)
    key = jax.random.fold_in(key, 12)
    key_marks, key_first, key_last = jax.random.split(key, 3)
    marks = jax.random.randint(key_marks, (N_CTX, L), 0, CLUSTER) == 0
    first_pos = jax.random.randint(key_first, (), 1, TOK_DEV)
    last_pos = jax.random.randint(key_last, (), L - TOK_DEV + 1, L)
    places = jnp.arange(L)
    inside = (places > first_pos) & (places < last_pos)
    edges = (places == first_pos) | (places == last_pos)
    spanning = marks & jnp.logical_not(inside)[None, :] | edges[None, :]
    rows_full = (jnp.arange(N_CTX) == chosen)[:, None]
    return jnp.where(rows_full, spanning, marks).astype(jnp.int32)


def draw_a_log(key, part):
    key = jax.random.fold_in(key, 13)
    key_kind, key_rate = jax.random.split(key)
    slow_share = 5
    slow_rows = jax.random.randint(key_kind, (INNER, 1), 0, 10) < slow_share
    unit = jax.random.uniform(key_rate, (INNER, STATE), jnp.float32)
    fast_log = unit * jnp.log(16.0)
    slow_log = jnp.log(0.02 / L) + unit * jnp.log(25.0)
    return jnp.where(slow_rows, slow_log, fast_log).astype(jnp.bfloat16)


def block_scale(key, extent, shards, low, top_value):
    factor_of = 1.0
    for dim, blocks in shards:
        steps = jax.random.uniform(jax.random.fold_in(jax.random.fold_in(key, 6), dim), (blocks,), jnp.float32, low / len(shards), top_value / len(shards))
        factor_of = factor_of * jnp.repeat(jnp.exp(steps), extent[dim] // blocks).reshape((-1,) + (1,) * (len(extent) - 1 - dim))
    return factor_of


def gaussian(own_key, shape, deviation, reach, cuts=(), dtype=jnp.bfloat16):
    factor_of = block_scale(own_key, shape, cuts, -0.22, 0.18) if cuts else 1.0
    values = jax.random.normal(own_key, shape, jnp.float32) * deviation * factor_of
    return jnp.minimum(jnp.maximum(values, -reach), reach).astype(dtype)


def setup_inputs(seed: int = 0) -> dict:
    key_of = jax.random.split(jax.random.key(seed), 15)
    return {
        "hidden": gaussian(key_of[0], (N_CTX, L, D), 1.0, 6.0, ((0, 2), (1, 16))),
        "out_grad": gaussian(key_of[1], (N_CTX, L, D), 1.0, 6.0, ((0, 2), (1, 16))),
        "resets": draw_resets(jax.random.fold_in(key_of[14], 71), 0),
        "valid": draw_valid(jax.random.fold_in(key_of[14], 71), 0),
        "norm_gain": jnp.clip(1.0 + 0.18 * jax.random.normal(key_of[4], (D,), jnp.float32), 0.099609375, 1.8984375).astype(jnp.bfloat16),
        "in_weight": gaussian(key_of[5], (D, 2 * INNER), D ** -0.5, 0.1875, ((0, 16),)),
        "conv_weight": jnp.clip(jax.random.uniform(key_of[6], (INNER, CONV), jnp.float32, -0.5, 0.5) * block_scale(key_of[6], (INNER, CONV), ((0, 16),), -0.4, 0.0), -0.5, 0.5).astype(jnp.bfloat16),
        "conv_bias": jnp.clip(jax.random.uniform(key_of[7], (INNER,), jnp.float32, -0.5, 0.5) * block_scale(key_of[7], (INNER,), ((0, 16),), -0.4, 0.0), -0.5, 0.5).astype(jnp.bfloat16),
        "x_weight": gaussian(key_of[8], (INNER, DT_RANK + 2 * STATE), INNER ** -0.5, 0.125, ((0, 16),)),
        "dt_weight": gaussian(key_of[9], (INNER, DT_RANK), DT_RANK ** -0.5, 0.75, ((0, 16),)),
        "dt_bias": jnp.clip(-5.0 + 2.0 * jax.random.uniform(key_of[10], (INNER,), jnp.float32) ** block_scale(key_of[10], (INNER,), ((0, 16),), -0.2, 0.2), -5.0, -3.0).astype(jnp.bfloat16),
        "a_log": draw_a_log(jax.random.fold_in(key_of[14], 71), 0),
        "skip_gain": jnp.clip(0.5 + 1.0 * jax.random.uniform(key_of[12], (INNER,), jnp.float32) ** block_scale(key_of[12], (INNER,), ((0, 16),), -0.2, 0.2), 0.5, 1.5).astype(jnp.bfloat16),
        "out_weight": gaussian(key_of[13], (INNER, D), (4 * INNER) ** -0.5, 0.0625, ((0, 16),)),
    }


@jax.custom_vjp
def low(v):
    return lax.optimization_barrier(v.astype(jnp.bfloat16)).astype(jnp.float32)

@jax.custom_vjp
def low_back(v):
    return v

def low_keep(v):
    return (low(v), None)

def low_pass(kept, grad):
    return (grad,)

def back_keep(v):
    return (v, None)

def back_low(kept, grad):
    return (low(grad),)
low.defvjp(low_keep, low_pass)
low_back.defvjp(back_keep, back_low)
epsilon = 1e-05
highest = lax.Precision.HIGHEST

def selective(delta, drive, b_input, c_output, keep_mask, a_matrix):
    span_len = min(512, L)
    n_blocks = L // span_len

    def block_fn(state_in, inputs):

        def token_step(state_now, item):
            dt_step, drive_step, b_step, c_step, keep_step = item
            state_next = keep_step * jnp.exp(dt_step[:, None] * a_matrix) * state_now + drive_step[:, None] * b_step[None, :]
            return (state_next, jnp.dot(state_next, c_step, precision=highest))
        return lax.scan(token_step, state_in, inputs)
    stacked = tuple((value.reshape((n_blocks, span_len) + value.shape[1:]) for value in (delta, drive, b_input, c_output, keep_mask)))
    _, outputs = lax.scan(jax.checkpoint(block_fn), jnp.zeros((INNER, STATE), jnp.float32), stacked)
    return outputs.reshape(L, INNER)

def context(source, gain, w_in, w_conv, b_conv, w_x, w_dt, b_dt, a_logs, w_skip, w_out, live_mask, keep_mask):
    rscale = lax.rsqrt(lax.optimization_barrier(jnp.mean(source * source, axis=-1, keepdims=True)) + epsilon)
    normed = low(source * rscale * gain)
    projected = low_back(jnp.dot(normed, w_in, precision=highest, preferred_element_type=jnp.float32))
    x_part = low(projected[:, :INNER])
    z_part = projected[:, INNER:]
    extended = jnp.concatenate([jnp.zeros((CONV - 1, INNER), jnp.float32), x_part], 0)
    conv_out = b_conv + sum((w_conv[:, offset] * extended[offset:offset + L] for offset in range(CONV)))
    signal = low(jax.nn.silu(conv_out))
    x_dbl = low_back(jnp.dot(signal, w_x, precision=highest, preferred_element_type=jnp.float32))
    dt_low = low(x_dbl[:, :DT_RANK])
    b_input = x_dbl[:, DT_RANK:DT_RANK + STATE]
    c_output = x_dbl[:, DT_RANK + STATE:]
    dt_pre = low_back(jnp.dot(dt_low, w_dt.T, precision=highest, preferred_element_type=jnp.float32) + b_dt)
    delta = jax.nn.softplus(dt_pre)
    a_matrix = -jnp.exp(a_logs)
    scanned = selective(delta, delta * signal, b_input, c_output, keep_mask, a_matrix) + w_skip * signal
    mixed = low(scanned * jax.nn.silu(z_part))
    return source + live_mask[:, None] * jnp.dot(mixed, w_out, precision=highest, preferred_element_type=jnp.float32)

def reference(hidden, out_grad, resets, valid, norm_gain, in_weight, conv_weight, conv_bias, x_weight, dt_weight, dt_bias, a_log, skip_gain, out_weight):
    params = tuple((value.astype(jnp.float32) for value in (norm_gain, in_weight, conv_weight, conv_bias, x_weight, dt_weight, dt_bias, a_log, skip_gain, out_weight)))
    places = jnp.arange(L)

    def forward(source_all, *weights):
        results = []
        for index in range(N_CTX):
            live_mask = (places < valid[index]).astype(jnp.float32)
            keep_mask = 1.0 - resets[index].astype(jnp.float32)
            results.append(jax.checkpoint(context)(source_all[index], *weights, live_mask, keep_mask))
        return jnp.stack(results)
    result, pullback = jax.vjp(forward, hidden.astype(jnp.float32), *params)
    grads = pullback(out_grad.astype(jnp.float32))
    return (result.astype(jnp.bfloat16), grads[0], grads[1], grads[2], grads[3], grads[4], grads[5], grads[6], grads[7], grads[8], grads[9], grads[10])
```

```python
import functools

import jax
import jax.numpy as jnp
from jax import lax
from jax.experimental import pallas as pl
from jax.experimental.pallas import tpu as pltpu
from jax.sharding import PartitionSpec as P

epsilon = 1e-05
highest = lax.Precision.HIGHEST
contract_last = (((1,), (1,)), ((), ()))
contract_first = (((0,), (0,)), ((), ()))


def passed_along(block, axis, distance):
    devices = range(lax.axis_size(axis))
    route = [(i - distance, i) for i in devices if i - distance in devices]
    return lax.ppermute(block, axis, route)


def entering_2(part, axis, combine, identity, reverse):
    count = lax.axis_size(axis)
    place = lax.axis_index(axis)
    ahead = count - 1 - place if reverse else place
    gathered = jax.tree.map(lambda a: lax.all_gather(a, axis), part)
    state = jax.tree.map(lambda a, e: jnp.zeros_like(a) + jnp.asarray(e, a.dtype), part, identity)

    def one(hop, state):
        source = count - 1 - hop if reverse else hop
        return combine(
            state, jax.tree.map(lambda a: lax.dynamic_index_in_dim(a, source, 0, False), gathered)
        )

    return lax.fori_loop(0, ahead, one, state)


def silu_slope(value):
    sigma = jax.nn.sigmoid(value)
    return sigma * (1.0 + value * (1.0 - sigma))


def combine_pair(earlier, later):
    return (earlier[0] * later[0], later[0] * earlier[1] + later[1])


def decays_of(delta_blk, keep_blk, a_matrix):
    return keep_blk[:, None, None] * jnp.exp(delta_blk[:, :, None] * a_matrix[None])


def shards(
    hidden,
    out_grad,
    resets,
    valid,
    norm_gain,
    in_weight,
    conv_weight,
    conv_bias,
    x_weight,
    dt_weight,
    dt_bias,
    a_log,
    skip_gain,
    out_weight,
):
    gathered = (
        lax.all_gather(norm_gain, "seq", axis=0, tiled=True),
        lax.all_gather(in_weight, "seq", axis=0, tiled=True),
        lax.all_gather(conv_weight, "seq", axis=0, tiled=True),
        lax.all_gather(conv_bias, "seq", axis=0, tiled=True),
        lax.all_gather(x_weight, "seq", axis=0, tiled=True),
        lax.all_gather(dt_weight, "seq", axis=0, tiled=True),
        lax.all_gather(dt_bias, "seq", axis=0, tiled=True),
        lax.all_gather(a_log, "seq", axis=0, tiled=True),
        lax.all_gather(skip_gain, "seq", axis=0, tiled=True),
        lax.all_gather(out_weight, "seq", axis=0, tiled=True),
    )
    gain_full, w_in, w_conv, b_conv, w_x, w_dt, b_dt, a_logs, w_skip, w_out = gathered
    tokens = hidden.shape[1]
    inner = w_out.shape[0]
    rank = w_dt.shape[1]
    state = a_logs.shape[1]
    taps = w_conv.shape[1]
    places = lax.axis_index("seq") * tokens + jnp.arange(tokens, dtype=jnp.int32)
    live_mask = (places < valid[0]).astype(jnp.float32)
    reset_f = resets[0].astype(jnp.float32)
    keep_mask = 1.0 - reset_f
    source = hidden[0].astype(jnp.float32)
    rscale = lax.rsqrt(jnp.mean(source * source, axis=-1, keepdims=True) + epsilon)
    scaled = source * rscale
    gain_f = gain_full.astype(jnp.float32)
    normed = (scaled * gain_f).astype(jnp.bfloat16)
    projected = jnp.dot(normed, w_in, preferred_element_type=jnp.float32)
    x_part = projected[:, :inner].astype(jnp.bfloat16)
    z_part = projected[:, inner:]
    rim_rows = passed_along(x_part[tokens - (taps - 1) :], "seq", 1)
    extended = jnp.concatenate([rim_rows, x_part], 0).astype(jnp.float32)
    conv_taps = w_conv.astype(jnp.float32)
    conv_out = b_conv.astype(jnp.float32) + sum(
        (conv_taps[:, offset] * extended[offset : offset + tokens] for offset in range(taps))
    )
    signal_low = jax.nn.silu(conv_out).astype(jnp.bfloat16)
    signal = signal_low.astype(jnp.float32)
    x_dbl = jnp.dot(signal_low, w_x, preferred_element_type=jnp.float32)
    dt_low = x_dbl[:, :rank].astype(jnp.bfloat16)
    b_input = x_dbl[:, rank : rank + state]
    c_output = x_dbl[:, rank + state :]
    dt_pre = lax.dot_general(
        dt_low, w_dt, contract_last, preferred_element_type=jnp.float32
    ) + b_dt.astype(jnp.float32)
    delta = jax.nn.softplus(dt_pre)
    a_matrix = -jnp.exp(a_logs.astype(jnp.float32))
    drive = delta * signal
    reset_count = jnp.cumsum(reset_f)
    reset_before = reset_count - reset_f
    delta_sum = jnp.cumsum(delta, 0)
    delta_before = delta_sum - delta
    reset_total = reset_count[-1]
    delta_total = delta_sum[-1]
    alive_upto = (reset_count == 0.0).astype(jnp.float32)
    alive_before = (reset_before == 0.0).astype(jnp.float32)
    alive_after = (reset_total - reset_count == 0.0).astype(jnp.float32)
    span_len = min(64, tokens)
    n_blocks = tokens // span_len
    roll_by = min(16, span_len)

    def split_blocks(value):
        return value.reshape((n_blocks, span_len) + value.shape[1:])

    delta_b = split_blocks(delta)
    drive_b = split_blocks(drive)
    binput_b = split_blocks(b_input)
    coutput_b = split_blocks(c_output)
    keep_b = split_blocks(keep_mask)
    dsum_b = split_blocks(delta_sum)
    upto_b = split_blocks(alive_upto)
    after_b = split_blocks(alive_after)
    ones_state = jnp.ones((inner, state), jnp.float32)
    zero_state = jnp.zeros((inner, state), jnp.float32)
    group_prod = (reset_total == 0.0).astype(jnp.float32) * jnp.exp(delta_total[:, None] * a_matrix)

    def forward_step(state_now, blk):
        delta_blk, drive_blk, binput_blk, coutput_blk, keep_blk = blk
        decays = decays_of(delta_blk, keep_blk, a_matrix)

        def token_step(state_tok, item):
            decay_now, drive_now, binput_now, coutput_now = item
            state_next = decay_now * state_tok + drive_now[:, None] * binput_now[None, :]
            return (state_next, jnp.sum(state_next * coutput_now[None, :], -1))

        state_end, outputs = lax.scan(
            token_step, state_now, (decays, drive_blk, binput_blk, coutput_blk), unroll=roll_by
        )
        return (state_end, (state_now, outputs))

    group_state, (local_starts, scan_local) = lax.scan(
        forward_step, zero_state, (delta_b, drive_b, binput_b, coutput_b, keep_b)
    )
    entering = entering_2(
        (group_prod, group_state), "seq", combine_pair, (ones_state, zero_state), False
    )
    state_in = entering[1]

    def lift_block(blk):
        dsum_blk, upto_blk, coutput_blk = blk
        lifted = (
            upto_blk[:, None, None]
            * jnp.exp(dsum_blk[:, :, None] * a_matrix[None])
            * state_in[None]
        )
        return jnp.sum(lifted * coutput_blk[:, None, :], -1)

    lifted_out = lax.map(lift_block, (dsum_b, upto_b, coutput_b))
    scanned = (scan_local + lifted_out).reshape(tokens, inner) + w_skip.astype(jnp.float32) * signal
    gate_act = jax.nn.silu(z_part)
    mixed = (scanned * gate_act).astype(jnp.bfloat16)
    branch = jnp.dot(mixed, w_out, preferred_element_type=jnp.float32)
    result = (source + live_mask[:, None] * branch).astype(jnp.bfloat16)
    regathered = (
        lax.all_gather(norm_gain, "seq", axis=0, tiled=True),
        lax.all_gather(in_weight, "seq", axis=0, tiled=True),
        lax.all_gather(conv_weight, "seq", axis=0, tiled=True),
        lax.all_gather(conv_bias, "seq", axis=0, tiled=True),
        lax.all_gather(x_weight, "seq", axis=0, tiled=True),
        lax.all_gather(dt_weight, "seq", axis=0, tiled=True),
        lax.all_gather(dt_bias, "seq", axis=0, tiled=True),
        lax.all_gather(a_log, "seq", axis=0, tiled=True),
        lax.all_gather(skip_gain, "seq", axis=0, tiled=True),
        lax.all_gather(out_weight, "seq", axis=0, tiled=True),
    )
    gain_full, w_in, w_conv, b_conv, w_x, w_dt, b_dt, a_logs, w_skip, w_out = regathered
    gain_f = gain_full.astype(jnp.float32)
    conv_taps = w_conv.astype(jnp.float32)
    a_matrix = -jnp.exp(a_logs.astype(jnp.float32))
    cotangent = out_grad[0].astype(jnp.float32)
    g_branch = (live_mask[:, None] * cotangent).astype(jnp.bfloat16)
    g_mixed = lax.dot_general(g_branch, w_out, contract_last, preferred_element_type=jnp.float32)
    g_scan = g_mixed * gate_act
    g_zpart = g_mixed * scanned * silu_slope(z_part)
    g_skip_full = jnp.sum(g_scan * signal, 0)
    gscan_b = split_blocks(g_scan)

    def push_block(total, blk):
        dsum_blk, upto_blk, coutput_blk, gscan_blk = blk
        weight_blk = upto_blk[:, None, None] * jnp.exp(dsum_blk[:, :, None] * a_matrix[None])
        return (
            total + jnp.sum(weight_blk * gscan_blk[:, :, None] * coutput_blk[:, None, :], 0),
            None,
        )

    passed_local, _ = lax.scan(push_block, zero_state, (dsum_b, upto_b, coutput_b, gscan_b))
    leaving = entering_2(
        (group_prod, passed_local), "seq", combine_pair, (ones_state, zero_state), True
    )
    passed_in = leaving[1]
    start_rows = jnp.arange(n_blocks) * span_len
    start_alive = alive_before[start_rows]
    start_delta = delta_before[start_rows]
    block_starts = (
        local_starts
        + start_alive[:, None, None]
        * jnp.exp(start_delta[:, :, None] * a_matrix[None])
        * state_in[None]
    )

    def backward_step(carried, blk):
        passed, grad_amat = carried
        (
            start_state,
            delta_blk,
            drive_blk,
            binput_blk,
            coutput_blk,
            gscan_blk,
            keep_blk,
            dsum_blk,
            after_blk,
        ) = blk
        decays = decays_of(delta_blk, keep_blk, a_matrix)

        def ahead_step(state_tok, item):
            decay_now, drive_now, binput_now = item
            state_next = decay_now * state_tok + drive_now[:, None] * binput_now[None, :]
            return (state_next, state_next)

        _, states_blk = lax.scan(
            ahead_step, start_state, (decays, drive_blk, binput_blk), unroll=roll_by
        )
        before = jnp.concatenate([start_state[None], states_blk[:-1]], 0)

        def behind_step(passed_tok, item):
            decay_now, coutput_now, gscan_now = item
            adjoint = gscan_now[:, None] * coutput_now[None, :] + passed_tok
            return (decay_now * adjoint, adjoint)

        passed, adjoints_local = lax.scan(
            behind_step, passed, (decays, coutput_blk, gscan_blk), reverse=True, unroll=roll_by
        )
        reach = after_blk[:, None, None] * jnp.exp(
            (delta_total[None] - dsum_blk)[:, :, None] * a_matrix[None]
        )
        adjoints = adjoints_local + reach * passed_in[None]
        flow = adjoints * before * decays
        g_delta_decay = jnp.sum(flow * a_matrix[None], -1)
        grad_amat = grad_amat + jnp.sum(flow * delta_blk[:, :, None], 0)
        g_drive = jnp.einsum("qen,qn->qe", adjoints, binput_blk, precision=highest)
        g_binput = jnp.einsum("qen,qe->qn", adjoints, drive_blk, precision=highest)
        g_coutput = jnp.einsum("qen,qe->qn", states_blk, gscan_blk, precision=highest)
        return ((passed, grad_amat), (g_delta_decay, g_drive, g_binput, g_coutput))

    (_, grad_amat), pieces = lax.scan(
        backward_step,
        (zero_state, zero_state),
        (block_starts, delta_b, drive_b, binput_b, coutput_b, gscan_b, keep_b, dsum_b, after_b),
        reverse=True,
    )
    g_delta_decay = pieces[0].reshape(tokens, inner)
    g_drive = pieces[1].reshape(tokens, inner)
    g_binput = pieces[2].reshape(tokens, state)
    g_coutput = pieces[3].reshape(tokens, state)
    g_delta = g_delta_decay + g_drive * signal
    g_pre = (g_delta * jax.nn.sigmoid(dt_pre)).astype(jnp.bfloat16)
    g_dtlow = jnp.dot(g_pre, w_dt, preferred_element_type=jnp.float32)
    g_xdbl = jnp.concatenate([g_dtlow, g_binput, g_coutput], 1).astype(jnp.bfloat16)
    g_signal = (
        g_scan * w_skip.astype(jnp.float32)
        + g_drive * delta
        + lax.dot_general(g_xdbl, w_x, contract_last, preferred_element_type=jnp.float32)
    )
    g_conv = g_signal * silu_slope(conv_out)
    g_extended = sum(
        (
            jnp.pad(conv_taps[:, offset] * g_conv, ((offset, taps - 1 - offset), (0, 0)))
            for offset in range(taps)
        )
    )
    returned = passed_along(g_extended[: taps - 1], "seq", -1)
    g_xpart = g_extended[taps - 1 :] + jnp.pad(returned, ((tokens - (taps - 1), 0), (0, 0)))
    g_proj = jnp.concatenate([g_xpart, g_zpart], 1).astype(jnp.bfloat16)
    g_normed = lax.dot_general(g_proj, w_in, contract_last, preferred_element_type=jnp.float32)
    g_hat = g_normed * gain_f
    grad_source = (
        rscale * g_hat
        - source * rscale * rscale * rscale * jnp.mean(g_hat * source, axis=-1, keepdims=True)
        + cotangent
    )
    g_gain = jnp.sum(g_normed * scaled, 0)
    g_wconv = jnp.stack(
        [jnp.sum(g_conv * extended[offset : offset + tokens], 0) for offset in range(taps)], 1
    )
    g_bconv = jnp.sum(g_conv, 0)
    g_bdt = jnp.sum(g_pre.astype(jnp.float32), 0)
    g_alog = grad_amat * a_matrix
    weight_rows = lax.dot_general(
        normed, g_proj, contract_first, preferred_element_type=jnp.float32
    )
    g_win_rows, g_gain_rows = lax.psum_scatter(
        (weight_rows, g_gain), "seq", scatter_dimension=0, tiled=True
    )
    xw_rows = lax.dot_general(
        signal_low, g_xdbl, contract_first, preferred_element_type=jnp.float32
    )
    dtw_rows = lax.dot_general(g_pre, dt_low, contract_first, preferred_element_type=jnp.float32)
    outw_rows = lax.dot_general(mixed, g_branch, contract_first, preferred_element_type=jnp.float32)
    (
        g_wconv_rows,
        g_bconv_rows,
        g_wx_rows,
        g_wdt_rows,
        g_bdt_rows,
        g_alog_rows,
        g_skip_rows,
        g_wout_rows,
    ) = lax.psum_scatter(
        (g_wconv, g_bconv, xw_rows, dtw_rows, g_bdt, g_alog, g_skip_full, outw_rows),
        "seq",
        scatter_dimension=0,
        tiled=True,
    )
    totals = lax.psum(
        (
            g_gain_rows,
            g_win_rows,
            g_wconv_rows,
            g_bconv_rows,
            g_wx_rows,
            g_wdt_rows,
            g_bdt_rows,
            g_alog_rows,
            g_skip_rows,
            g_wout_rows,
        ),
        "ctx",
    )
    return (
        result[None],
        grad_source[None],
        totals[0],
        totals[1],
        totals[2],
        totals[3],
        totals[4],
        totals[5],
        totals[6],
        totals[7],
        totals[8],
        totals[9],
    )


MESH = pl.DeviceIdType.MESH
F32 = jnp.float32
BF16 = jnp.bfloat16
ROWS = 128
GROUPS = 8
LANES = 128
WIDE = 512
LOG2E = 1.4426950408889634


def place():
    seq = lax.axis_index("seq")
    return lax.axis_index("ctx"), seq, seq // 4, (seq // 2) % 2, seq % 2


def chip(z, y, x):
    return z * 4 + y * 2 + x


class Semaphores:
    def __init__(self, send, receive):
        self.send, self.receive = send, receive
        self.sends = self.receives = 0

    def new_send(self):
        self.sends += 1
        return self.send.at[self.sends - 1]

    def new_receive(self):
        self.receives += 1
        return self.receive.at[self.receives - 1]

    def copy(self, source, target, core, seq, send=None, receive=None):
        return pltpu.make_async_remote_copy(
            src_ref=source,
            dst_ref=target,
            send_sem=self.new_send() if send is None else send,
            recv_sem=self.new_receive() if receive is None else receive,
            device_id=(core, seq),
            device_id_type=MESH,
        )


def joint(region, copy_sems):
    c, _, z, y, x = place()
    send, receive = copy_sems
    return pltpu.make_async_remote_copy(
        src_ref=region,
        dst_ref=region,
        send_sem=send,
        recv_sem=receive,
        device_id=(c, chip(z, y, 1 - x)),
        device_id_type=MESH,
    )


def partner(z, j):
    return (z, z + 1 - 2 * (z % 2), (z + 2) % 4, 3 - z)[j]


class Gather:
    slots = 4

    def __init__(self, sems, buf):
        c, _, z, y, x = place()
        own = self.slot(0)
        self.first = [
            sems.copy(buf.at[:, own, y, x], buf.at[:, own, y, x], c, chip(partner(z, j), y, x))
            for j in (1, 2, 3)
        ]
        send2, send3 = sems.new_send(), sems.new_send()
        self.second, self.second_all, self.third, self.third_all = [], [], [], []
        for j in range(self.slots):
            s = self.slot(j)
            got = sems.new_receive()
            self.second.append(
                [
                    sems.copy(buf.at[0, s, y, x], buf.at[0, s, y, x], c, chip(z, 1 - y, x), send2, got),
                    sems.copy(buf.at[1, s, y, x], buf.at[1, s, y, x], c, chip(z, y, 1 - x), send2, got),
                ]
            )
            self.second_all.append(joint(buf.at[:, s, y, x], (send2, got)))
            got = sems.new_receive()
            self.third.append(
                [
                    sems.copy(buf.at[0, s, :, x], buf.at[0, s, :, x], c, chip(z, y, 1 - x), send3, got),
                    sems.copy(buf.at[1, s, y], buf.at[1, s, y], c, chip(z, 1 - y, x), send3, got),
                ]
            )
            self.third_all.append(joint(buf.at[:, s, :, x], (send3, got)))
        self.second_sent = joint(buf.at[:, :, y, x], (send2, got))
        self.third_sent = joint(buf.at[:, :, :, x], (send3, got))

    def slot(self, j):
        return partner(place()[2], j)

    def start(self):
        for copy in self.first:
            copy.start()

    def arrived(self, j):
        if j > 0:
            self.first[j - 1].wait_recv()

    def relay(self, j):
        self.arrived(j)
        for copy in self.second[j]:
            copy.start()

    def cross(self, j):
        self.second_all[j].wait_recv()
        for copy in self.third[j]:
            copy.start()

    def slot_done(self, j):
        self.third_all[j].wait_recv()

    def done(self):
        for j in range(self.slots):
            self.slot_done(j)

    def sent(self):
        for copy in self.first:
            copy.wait_send()
        self.sent_rest()

    def sent_rest(self):
        self.second_sent.wait_send()
        self.third_sent.wait_send()


def is_active():
    c, _, z, _, _ = place()
    return z // 2 == c


def is_passive():
    return jnp.logical_not(is_active())


def half_slot(j):
    z = place()[2]
    return z % 2 if j == 0 else 1 - z % 2


class HalfGather(Gather):
    slots = 2

    def slot(self, j):
        return half_slot(j)

    def start(self):
        @pl.when(is_active())
        def _():
            for copy in self.first:
                copy.start()

    def arrived(self, j):
        if j == 1:

            @pl.when(is_active())
            def _():
                self.first[0].wait_recv()

        @pl.when(is_passive())
        def _():
            self.first[1 + j].wait_recv()

    def sent(self):
        @pl.when(is_active())
        def _():
            for copy in self.first:
                copy.wait_send()

        self.sent_rest()


class SmallGather:
    def __init__(self, sems, buf):
        c, _, z, y, x = place()
        s = half_slot(0)
        self.first = sems.copy(buf.at[s, y, x], buf.at[s, y, x], c, chip(z, y, 1 - x))
        self.second = sems.copy(buf.at[s, y], buf.at[s, y], c, chip(z, 1 - y, x))
        self.third = [
            sems.copy(buf.at[s], buf.at[s], c, chip(partner(z, j), y, x)) for j in (1, 2, 3)
        ]

    def start(self):
        @pl.when(is_active())
        def _():
            self.first.start()

    def relay(self):
        @pl.when(is_active())
        def _():
            self.first.wait_recv()
            self.second.start()

    def cross(self):
        @pl.when(is_active())
        def _():
            self.second.wait_recv()
            for copy in self.third:
                copy.start()

    def done(self):
        @pl.when(is_active())
        def _():
            self.third[0].wait_recv()

        @pl.when(is_passive())
        def _():
            self.third[1].wait_recv()
            self.third[2].wait_recv()

    def sent(self):
        @pl.when(is_active())
        def _():
            for copy in [self.first, self.second] + self.third:
                copy.wait_send()


def add_into(total, part):
    total[...] = total[...] + part[...]


class Scatter:
    order = (2, 3, 1, 0)

    def __init__(self, sems, grad, came1, came2, came3):
        c, _, z, y, x = place()
        self.grad, self.came1, self.came2, self.came3 = grad, came1, came2, came3
        send1, send2 = sems.new_send(), sems.new_send()
        self.first, self.first_all, self.second, self.second_all = [], [], [], []
        for j in range(len(self.order)):
            s = self.slot(j)
            got = sems.new_receive()
            self.first.append(
                [
                    sems.copy(grad.at[0, s, :, 1 - x], came1.at[0, s], c, chip(z, y, 1 - x), send1, got),
                    sems.copy(grad.at[1, s, 1 - y], came1.at[1, s], c, chip(z, 1 - y, x), send1, got),
                ]
            )
            self.first_all.append(joint(came1.at[:, s], (send1, got)))
            got = sems.new_receive()
            self.second.append(
                [
                    sems.copy(grad.at[0, s, 1 - y, x], came2.at[0, s], c, chip(z, 1 - y, x), send2, got),
                    sems.copy(grad.at[1, s, y, 1 - x], came2.at[1, s], c, chip(z, y, 1 - x), send2, got),
                ]
            )
            self.second_all.append(joint(came2.at[:, s], (send2, got)))
        self.first_sent = joint(came1, (send1, got))
        self.second_sent = joint(came2, (send2, got))
        got = sems.new_receive()
        self.third = [
            sems.copy(
                grad.at[:, self.slot(self.third_slot(j)), y, x],
                came3.at[j - 1],
                c,
                chip(partner(z, j), y, x),
                None,
                got,
            )
            for j in (1, 2, 3)
        ]
        self.third_all = joint(came3, (send2, got))

    def slot(self, j):
        return partner(place()[2], j)

    def third_slot(self, j):
        return j

    def push1(self, j):
        for copy in self.first[j]:
            copy.start()

    def push2(self, j):
        _, _, _, y, x = place()
        s = self.slot(j)
        self.first_all[j].wait_recv()
        add_into(self.grad.at[0, s, 1 - y, x], self.came1.at[0, s, 1 - y])
        self.second[j][0].start()
        add_into(self.grad.at[1, s, y, 1 - x], self.came1.at[1, s, 1 - x])
        self.second[j][1].start()
        add_into(self.grad.at[0, s, y, x], self.came1.at[0, s, y])
        add_into(self.grad.at[1, s, y, x], self.came1.at[1, s, x])

    def push3(self, j):
        _, _, _, y, x = place()
        s = self.slot(j)
        self.second_all[j].wait_recv()
        for half in (0, 1):
            add_into(self.grad.at[half, s, y, x], self.came2.at[half, s])
        self.send_on(j)

    def send_on(self, j):
        if j > 0:
            self.third[j - 1].start()

    def all1(self):
        for j in self.order:
            self.push1(j)

    def all2(self):
        for j in self.order:
            self.push2(j)

    def all3(self):
        for j in self.order:
            self.push3(j)

    def done(self):
        self.third_all.wait_recv()

    def sent(self):
        for copy in self.third:
            copy.wait_send()
        self.sent_rest()

    def sent_rest(self):
        self.first_sent.wait_send()
        self.second_sent.wait_send()

    def result(self, half):
        _, _, _, y, x = place()
        total = self.grad[half, self.slot(0), y, x].astype(F32)
        for k in range(3):
            total = total + self.came3[k, half].astype(F32)
        return total


class HalfScatter(Scatter):
    order = (1, 0)

    def slot(self, j):
        return half_slot(j)

    def third_slot(self, j):
        return j % 2

    def send_on(self, j):
        if j == 1:

            @pl.when(is_active())
            def _():
                self.third[0].start()

        @pl.when(is_passive())
        def _():
            self.third[1 + j].start()

    def done(self):
        @pl.when(is_active())
        def _():
            self.third_all.wait_recv()

    def sent(self):
        @pl.when(is_active())
        def _():
            self.third[0].wait_send()

        @pl.when(is_passive())
        def _():
            self.third[1].wait_send()
            self.third[2].wait_send()

        self.sent_rest()


class SmallScatter:
    def __init__(self, sems, grad, came_z, came_y, came_x):
        c, _, z, y, x = place()
        self.grad, self.came_z, self.came_y, self.came_x = grad, came_z, came_y, came_x
        got = sems.new_receive()
        self.first = [
            sems.copy(
                grad.at[half_slot(j % 2)],
                came_z.at[j - 1],
                c,
                chip(partner(z, j), y, x),
                None,
                got,
            )
            for j in (1, 2, 3)
        ]
        self.first_all = joint(came_z, (sems.new_send(), got))
        s = half_slot(0)
        self.second = sems.copy(grad.at[s, 1 - y], came_y, c, chip(z, 1 - y, x))
        self.third = sems.copy(grad.at[s, y, 1 - x], came_x, c, chip(z, y, 1 - x))

    def push1(self):
        @pl.when(is_active())
        def _():
            self.first[0].start()

        @pl.when(is_passive())
        def _():
            self.first[1].start()
            self.first[2].start()

    def push2(self):
        _, _, _, y, _ = place()
        s = half_slot(0)

        @pl.when(is_active())
        def _():
            self.first_all.wait_recv()
            for row in (1 - y, y):
                total = self.grad[s, row].astype(F32)
                for k in range(3):
                    total = total + self.came_z[k, row].astype(F32)
                self.grad[s, row] = total.astype(BF16)
            self.second.start()

    def push3(self):
        _, _, _, y, _ = place()
        s = half_slot(0)

        @pl.when(is_active())
        def _():
            self.second.wait_recv()
            add_into(self.grad.at[s, y], self.came_y)
            self.third.start()

    def result(self):
        _, _, _, y, x = place()
        self.third.wait_recv()
        return self.grad[half_slot(0), y, x].astype(F32) + self.came_x[...].astype(F32)

    def sent(self):
        @pl.when(is_active())
        def _():
            for copy in (self.first[0], self.second, self.third):
                copy.wait_send()

        @pl.when(is_passive())
        def _():
            self.first[1].wait_send()
            self.first[2].wait_send()


class Transpose:
    def __init__(self, sems, source, target):
        c, seq, _, _, _ = place()
        self.source, self.target = source, target
        pair = (sems.new_send(), sems.new_receive())
        self.copies = [
            sems.copy(source.at[(seq + k) % 16], target.at[seq], c, (seq + k) % 16, *pair)
            for k in range(1, 16)
        ]
        self.all = joint(target.at[pl.ds(0, 15)], pair)

    def start(self):
        _, seq, _, _, _ = place()
        for copy in self.copies:
            copy.start()
        self.target[seq] = self.source[seq]

    def done(self):
        self.all.wait()


def wide(tile, count=WIDE // LANES):
    return jnp.concatenate([tile] * count, axis=1)


def rows_of(ref, base):
    return jnp.broadcast_to(ref[pl.ds(base, 1), :], (16, LANES))


def spread(slab, j):
    return jnp.broadcast_to(slab[j : j + 1, :], (16, slab.shape[1]))


def put_partial(ref, j, value):
    folded = value[:8] + value[8:]
    for g in range(WIDE // LANES):
        ref[pl.ds(g * 64 + 8 * j, 8), :] = folded[:, g * LANES : (g + 1) * LANES]


def take_partial(ref):
    out = []
    for g in range(WIDE // LANES):
        total = ref[pl.ds(g * 64, 8, stride=8), :]
        for j in range(1, 8):
            total = total + ref[pl.ds(g * 64 + j, 8, stride=8), :]
        out.append(total)
    return jnp.concatenate(out, axis=1)


def fold_lanes(value):
    total = value[:, :LANES]
    for g in range(1, value.shape[1] // LANES):
        total = total + value[:, g * LANES : (g + 1) * LANES]
    return total


def dot_nn(a, b):
    return jnp.dot(a, b, preferred_element_type=F32)


def dot_nt(a, b):
    return lax.dot_general(a, b, contract_last, preferred_element_type=F32)


def dot_tn(a, b):
    return lax.dot_general(a, b, contract_first, preferred_element_type=F32)


def for_each(count, body):
    def step(i, carry):
        body(i)
        return carry

    lax.fori_loop(0, count, step, 0)


def lanes_at(i, width):
    return pl.ds(pl.multiple_of(i * width, width), width)


def fused_kernel(
    valid,
    hid,
    out_g,
    resets,
    in_w,
    out_w,
    x_w,
    dt_w,
    a_log,
    conv_w,
    vectors,
    o_out,
    o_gh,
    o_gin,
    o_gout,
    o_small,
    o_gain,
    hidb,
    gbr,
    kb,
    gain_b,
    nrm,
    nrm_t,
    xext,
    sig,
    delta,
    zz,
    gs,
    yy,
    bb,
    cb,
    a2,
    prm,
    hs,
    qb,
    qc,
    part1,
    part2,
    part3,
    gbc,
    low,
    mid,
    mid_t,
    gz,
    wx,
    wz,
    wo,
    wp,
    gx_w,
    gz_w,
    go_w,
    gp_w,
    x1,
    x2,
    x3,
    z1,
    z2,
    z3,
    o1,
    o2,
    o3,
    p1,
    p2,
    p3,
    hp,
    hpr,
    hret,
    hin,
    lp,
    lpr,
    xd_out,
    xd_in,
    gext,
    gedge,
    rowx,
    rowx_in,
    fin,
    fin_in,
    fsm,
    send_sems,
    recv_sems,
):
    c, seq, z, y, x = place()
    mate = 1 - c
    after = (seq + 1) % 16
    before = (seq + 15) % 16
    sems = Semaphores(send_sems, recv_sems)

    barrier = pltpu.get_barrier_semaphore()
    for k in range(1, 16):
        pl.semaphore_signal(
            barrier, inc=1, device_id=(c, (seq + k) % 16), device_id_type=MESH
        )
    pl.semaphore_signal(barrier, inc=1, device_id=(mate, seq), device_id_type=MESH)
    pl.semaphore_signal(barrier, inc=1, device_id=(mate, after), device_id_type=MESH)
    pl.semaphore_signal(barrier, inc=1, device_id=(mate, before), device_id_type=MESH)

    for half in (0, 1):
        wx[half, z, y, x] = in_w[:, pl.ds(pl.multiple_of(c * 1024 + half * 512, 512), 512)]
        wz[half, z, y, x] = in_w[
            :, pl.ds(pl.multiple_of(2048 + c * 1024 + half * 512, 512), 512)
        ]

    @pl.when(z // 2 == c)
    def _():
        for half in (0, 1):
            wo[half, z % 2, y, x] = out_w[:, half * 512 : (half + 1) * 512]
        wp[z % 2, y, x, 0:96, :] = x_w[...]
        wp[z % 2, y, x, 96:160, :] = dt_w[...]
        wp[z % 2, y, x, 160:176, :] = a_log[...]
        wp[z % 2, y, x, 176:192, :] = jnp.concatenate(
            [conv_w[...].astype(F32), vectors[0:3, :], jnp.zeros((9, LANES), F32)], axis=0
        ).astype(BF16)

    lane = lax.broadcasted_iota(jnp.int32, (8, LANES), 1)
    gain_mine = jnp.where(lane // 64 == x, jnp.broadcast_to(vectors[3:4, :], (8, LANES)), 0.0)
    gain_b[seq] = gain_mine
    kb[c] = jnp.transpose(
        jnp.broadcast_to(1.0 - resets[...].astype(F32), (ROWS, LANES))
    )
    row_place = seq * ROWS + lax.broadcasted_iota(jnp.int32, (ROWS, LANES), 0)
    live = (row_place < valid[0]).astype(F32)
    hidb[c, pl.ds(16, ROWS), :] = hid[...]
    for g in range(GROUPS):
        at = slice(g * LANES, (g + 1) * LANES)
        gbr[c, :, at] = (live * out_g[:, at].astype(F32)).astype(BF16)

    pl.semaphore_wait(barrier, 18)

    gather_x = Gather(sems, wx)
    gather_z = Gather(sems, wz)
    gather_o = HalfGather(sems, wo)
    gather_p = SmallGather(sems, wp)
    gain_sems = (sems.new_send(), sems.new_receive())
    gain_copies = [
        sems.copy(gain_b.at[seq], gain_b.at[seq], c, (seq + k) % 16, *gain_sems)
        for k in range(1, 16)
    ]
    gain_all = joint(gain_b.at[pl.ds(0, 15)], gain_sems)
    hid_copies = [
        sems.copy(hidb.at[c, pl.ds(16, ROWS), :], hidb.at[c, pl.ds(16, ROWS), :], mate, seq),
        sems.copy(hidb.at[c, pl.ds(128, 16), :], hidb.at[c, pl.ds(0, 16), :], c, after),
        sems.copy(hidb.at[c, pl.ds(128, 16), :], hidb.at[c, pl.ds(0, 16), :], mate, after),
        sems.copy(kb.at[c], kb.at[c], mate, seq),
    ]
    gbr_copy = sems.copy(gbr.at[c], gbr.at[c], mate, seq)
    for copy in hid_copies:
        copy.start()
    for copy in gain_copies:
        copy.start()
    gather_p.start()
    gather_x.start()
    gather_x.relay(0)

    for copy in hid_copies:
        copy.wait()
    gather_p.relay()
    gain_all.wait()
    gain_row = jnp.concatenate(
        [gain_b[2 * g][0:1, :] + gain_b[2 * g + 1][0:1, :] for g in range(GROUPS)], axis=1
    )
    for ctx in (0, 1):

        def norm_rows(i):
            at = pl.ds(pl.multiple_of(i * 16, 16), 16)
            rows = hidb[ctx, at, :].astype(F32)
            r = lax.rsqrt(jnp.mean(rows * rows, axis=1, keepdims=True) + epsilon)
            nrm[ctx, at, :] = (rows * r * gain_row).astype(BF16)

        for_each(9, norm_rows)
    gather_p.cross()
    gather_z.start()
    for ctx in (0, 1):
        for g in range(GROUPS):
            at = slice(g * LANES, (g + 1) * LANES)
            nrm_t[at, ctx * ROWS : (ctx + 1) * ROWS] = jnp.transpose(
                nrm[ctx, 16:144, at].astype(F32)
            ).astype(BF16)

    gather_x.relay(1)
    gather_x.cross(0)
    gather_x.relay(2)
    gather_x.cross(1)
    gather_x.relay(3)
    gather_o.start()
    gather_x.cross(2)
    gather_x.cross(3)
    gbr_copy.start()
    gather_z.relay(0)
    gather_x.done()
    gather_z.relay(1)
    gather_z.cross(0)
    first_chip = (seq > 0).astype(F32)
    for half in (0, 1):

        def x_columns(i):
            rows = nrm[...].reshape(288, 1024)
            w = wx[half, :, :, :, :, lanes_at(i, 256)].reshape(1024, 256)
            got = dot_nn(rows, w).astype(BF16).astype(F32)
            at = pl.ds(pl.multiple_of(half * 512 + i * 256, 256), 256)
            for ctx in (0, 1):
                xext[ctx, 0:16, at] = got[ctx * 144 : ctx * 144 + 16] * first_chip
                xext[ctx, 16:144, at] = got[ctx * 144 + 16 : ctx * 144 + 144]

        for_each(2, x_columns)

    gather_z.relay(2)
    gather_z.cross(1)
    gather_p.done()
    for j in range(GROUPS):
        prm[:, j * LANES : (j + 1) * LANES] = wp[
            j // 4, (j // 2) % 2, j % 2, 160:192, :
        ].astype(F32)
    a2[...] = -jnp.exp(prm[0:16, :]) * LOG2E

    def conv_rows(ctx, at):
        total = prm[20:21, at] + prm[16:17, at] * xext[ctx, 13:141, at]
        for k in range(1, 4):
            total = total + prm[16 + k : 17 + k, at] * xext[ctx, 13 + k : 141 + k, at]
        return total

    for ctx in (0, 1):

        def conv_columns(i):
            at = lanes_at(i, LANES)
            total = conv_rows(ctx, at)
            rows = slice(ctx * ROWS, (ctx + 1) * ROWS)
            sig[rows, at] = (total * jax.nn.sigmoid(total)).astype(BF16)

        for_each(GROUPS, conv_columns)

    total = jnp.zeros((256, LANES), F32)
    for j in range(GROUPS):
        total = total + dot_nt(
            sig[:, j * LANES : (j + 1) * LANES], wp[j // 4, (j // 2) % 2, j % 2, 0:128, :]
        )
    xd_out[...] = total
    xd_copy = sems.copy(xd_out, xd_in, mate, seq)
    xd_copy.start()
    gather_z.relay(3)
    gather_z.cross(2)
    xd_copy.wait()
    xd = xd_out[...] + xd_in[...]
    low[...] = xd[:, 0:64].astype(BF16)
    for n in range(16):
        bb[pl.ds(n, 256, stride=16), :] = jnp.broadcast_to(xd[:, 64 + n : 65 + n], (256, LANES))
        cb[pl.ds(n, 256, stride=16), :] = jnp.broadcast_to(xd[:, 80 + n : 81 + n], (256, LANES))
    for j in range(GROUPS):
        at = slice(j * LANES, (j + 1) * LANES)
        pre = dot_nn(low[...], wp[j // 4, (j // 2) % 2, j % 2, 96:160, :]) + prm[21:22, at]
        delta[:, at] = jnp.maximum(pre, 0.0) + jnp.log1p(jnp.exp(-jnp.abs(pre)))

    gather_z.cross(3)
    gather_o.relay(0)
    gather_o.relay(1)

    def decay(slab, j, a, base):
        return jnp.exp2(spread(slab, j) * a) * wide(rows_of(kb2, base))

    kb2 = kb.reshape(256, LANES)

    def tile16(ref, t):
        return ref[pl.ds(pl.multiple_of(t * 16, 16), 16), :]

    def forward_ends(q):
        ctx, block = q // 2, q % 2
        at = lanes_at(block, WIDE)
        a = a2[:, at]

        def eight(i, h):
            t0 = pl.multiple_of(ctx * ROWS + i * 8, 8)
            d = delta[pl.ds(t0, 8), at]
            u = d * slab_of(sig, t0, at)
            for j in range(8):
                h = decay(d, j, a, t0 + j) * h + spread(u, j) * wide(tile16(bb, t0 + j))
            return h

        h = lax.fori_loop(0, 16, eight, jnp.zeros((16, WIDE), F32))
        rows = pl.ds(pl.multiple_of(ctx * ROWS, ROWS), ROWS)
        summed = jnp.sum(delta[rows, at], axis=0, keepdims=True)
        kept = jnp.min(kb[ctx], axis=0, keepdims=True)
        decays = jnp.exp2(jnp.broadcast_to(summed, (16, WIDE)) * a) * wide(
            jnp.broadcast_to(kept, (16, LANES))
        )
        for g in range(4):
            piece = ctx * GROUPS + block * 4 + g
            hp[piece, 0] = h[:, g * LANES : (g + 1) * LANES]
            hp[piece, 1] = decays[:, g * LANES : (g + 1) * LANES]

    def slab_of(ref, t0, at):
        base = pl.multiple_of((t0 // 16) * 16, 16)
        both = ref[pl.ds(base, 16), at].astype(F32)
        return jnp.where(t0 % 16 == 0, both[:8], both[8:])

    for_each(4, forward_ends)
    send_ends = Transpose(sems, hp, hpr)
    send_ends.start()
    gather_z.done()

    def z_columns(i):
        rows = nrm_rows()
        for half in (0, 1):
            w = wz[half, :, :, :, :, lanes_at(i, 256)].reshape(1024, 256)
            at = pl.ds(pl.multiple_of(half * 512 + i * 256, 256), 256)
            zz[:, at] = dot_nn(rows, w)

    def nrm_rows():
        return jnp.concatenate([nrm[0, 16:144, :], nrm[1, 16:144, :]], axis=0)

    for_each(2, z_columns)
    gather_o.cross(0)
    send_ends.done()
    state = jnp.zeros((16, LANES), F32)
    for s in range(16):
        hret[s] = state
        state = hpr[s, 1] * state + hpr[s, 0]
    return_states = Transpose(sems, hret, hin)
    return_states.start()
    gather_o.cross(1)
    return_states.done()

    def forward(q):
        ctx, block = q // 2, q % 2
        at = lanes_at(block, WIDE)
        a = a2[:, at]
        h0 = jnp.concatenate([hin[ctx * GROUPS + block * 4 + g] for g in range(4)], axis=1)
        hs[ctx * 129, :, at] = h0

        def eight(i, h):
            t0 = pl.multiple_of(ctx * ROWS + i * 8, 8)
            d = delta[pl.ds(t0, 8), at]
            s8 = slab_of(sig, t0, at)
            u = d * s8
            for j in range(8):
                h = decay(d, j, a, t0 + j) * h + spread(u, j) * wide(tile16(bb, t0 + j))
                hs[t0 + ctx + j + 1, :, at] = h
                put_partial(part1, j, h * wide(tile16(cb, t0 + j)))
            yy[pl.ds(t0, 8), at] = take_partial(part1) + prm[22:23, at] * s8
            return h

        lax.fori_loop(0, 16, eight, h0)

    for_each(4, forward)

    for ctx in (0, 1):
        for g in range(GROUPS):
            at = slice(g * LANES, (g + 1) * LANES)
            rows = slice(ctx * ROWS, (ctx + 1) * ROWS)
            zv = zz[rows, at]
            val = (yy[rows, at] * zv * jax.nn.sigmoid(zv)).astype(BF16)
            mid[rows, at] = val
            mid_t[at, rows] = jnp.transpose(val.astype(F32)).astype(BF16)

    gbr_copy.wait()

    def out_grads(i):
        e = pl.ds(pl.multiple_of(i * 256, 256), 256)
        branch = gbr[...].reshape(256, 1024)
        for half in (0, 1):
            got = dot_nn(mid_t[e, :], branch[:, half * 512 : (half + 1) * 512])
            go_w[half, i // 2, i % 2] = got.astype(BF16).reshape(2, 128, 512)

    for_each(4, out_grads)
    scatter_o = HalfScatter(sems, go_w, o1, o2, o3)
    scatter_o.push1(1)

    def branch_back(i):
        branch = gbr[...].reshape(256, 1024)
        w0 = wo[0, i // 2, i % 2].reshape(256, 512)
        w1 = wo[1, i // 2, i % 2].reshape(256, 512)
        gm = dot_nt(branch[:, :512], w0) + dot_nt(branch[:, 512:], w1)
        at = lanes_at(i, 256)
        zv = zz[:, at]
        sigma = jax.nn.sigmoid(zv)
        gs[:, at] = gm * (zv * sigma)
        gz[:, at] = (gm * yy[:, at] * (sigma * (1.0 + zv * (1.0 - sigma)))).astype(BF16)


    def z_grads(i):
        d = pl.ds(pl.multiple_of(i * 128, 128), 128)
        for half in (0, 1):
            got = dot_nn(nrm_t[d, :], gz[:, half * 512 : (half + 1) * 512])
            gz_w[half, i // 2, i % 2] = got.astype(BF16).reshape(2, 64, 512)

    scatter_z = Scatter(sems, gz_w, z1, z2, z3)

    def backward_ends(q):
        ctx, block = q // 2, q % 2
        at = lanes_at(block, WIDE)
        a = a2[:, at]

        def eight(i, adj):
            t0 = pl.multiple_of(ctx * ROWS + (15 - i) * 8, 8)
            d = delta[pl.ds(t0, 8), at]
            u = gs[pl.ds(t0, 8), at]
            for j in range(7, -1, -1):
                adj = decay(d, j, a, t0 + j) * (adj + spread(u, j) * wide(tile16(cb, t0 + j)))
            return adj

        adj = lax.fori_loop(0, 16, eight, jnp.zeros((16, WIDE), F32))
        for g in range(4):
            lp[ctx * GROUPS + block * 4 + g] = adj[:, g * LANES : (g + 1) * LANES]

    for j in (0, 1):
        gather_o.slot_done(j)
        block = half_slot(j)
        branch_back(2 * block)
        branch_back(2 * block + 1)
        backward_ends(block)
        backward_ends(2 + block)
    send_adj = Transpose(sems, lp, lpr)
    send_adj.start()
    for_each(8, z_grads)
    send_adj.done()
    state = jnp.zeros((16, LANES), F32)
    for s in range(15, -1, -1):
        hret[s] = state
        state = hpr[s, 1] * state + lpr[s]
    return_adj = Transpose(sems, hret, hin)
    return_adj.start()
    scatter_o.push1(0)
    scatter_z.push1(2)
    scatter_z.push1(3)
    for half in (0, 1):
        got = dot_nn(mid[...], wo[half].reshape(1024, 512))
        for ctx in (0, 1):
            rowx[ctx, :, half * 512 : (half + 1) * 512] = got[ctx * ROWS : (ctx + 1) * ROWS]
    rows_copy = sems.copy(rowx.at[mate], rowx_in.at[0], mate, seq)
    rows_copy.start()
    rows_copy.wait()
    for g in range(GROUPS):
        at = slice(g * LANES, (g + 1) * LANES)
        o_out[:, at] = (
            hid[:, at].astype(F32) + live * (rowx[c, :, at] + rowx_in[0, :, at])
        ).astype(BF16)
    return_adj.done()

    sub = lax.broadcasted_iota(jnp.int32, (8, LANES), 0)
    pick_b = [(lane == 64 + 8 * k + sub).astype(F32) for k in (0, 1)]
    pick_c = [(lane == 80 + 8 * k + sub).astype(F32) for k in (0, 1)]
    all_ones = jnp.ones((LANES, LANES), BF16)
    def backward(ctx, block):
        at = slice(block * WIDE, (block + 1) * WIDE)
        a = a2[:, at]

        def eight(i, carry):
            adj, grad_a = carry
            t0 = pl.multiple_of(ctx * ROWS + (15 - i) * 8, 8)
            d = delta[pl.ds(t0, 8), at]
            g8 = gs[pl.ds(t0, 8), at]
            u = d * slab_of(sig, t0, at)
            h_next = hs[t0 + ctx + 8, :, at]
            for j in range(7, -1, -1):
                t = t0 + j
                dj = spread(d, j)
                gj = spread(g8, j)
                lam = adj + gj * wide(tile16(cb, t))
                adj = jnp.exp2(dj * a) * wide(rows_of(kb2, t)) * lam
                h_prev = hs[t + ctx, :, at]
                flow = adj * h_prev
                grad_a = grad_a + flow * dj
                put_partial(part1, j, flow * a)
                put_partial(part2, j, lam * wide(tile16(bb, t)))
                to = pl.ds(pl.multiple_of((t - ctx * ROWS) * 16, 16), 16)
                qb[block, to, :] = fold_lanes(lam * spread(u, j)).astype(BF16)
                qc[block, to, :] = fold_lanes(gj * h_next).astype(BF16)
                h_next = h_prev
            yy[pl.ds(t0, 8), at] = take_partial(part1) * (1.0 / LOG2E)
            zz[pl.ds(t0, 8), at] = take_partial(part2)
            return adj, grad_a

        adj0 = jnp.concatenate([hin[ctx * GROUPS + block * 4 + g] for g in range(4)], axis=1)
        _, grad_a = lax.fori_loop(0, 16, eight, (adj0, jnp.zeros((16, WIDE), F32)))
        hs[ctx * 129, :, at] = grad_a

    def sum_lanes(ctx, i):
        for k in range(2):
            t0 = pl.multiple_of(i * 32 + k * 16, 16)
            at = pl.ds(pl.multiple_of(t0 * 16, 256), 256)
            sum_b = dot_nn(qb[0, at, :], all_ones) + dot_nn(qb[1, at, :], all_ones)
            sum_c = dot_nn(qc[0, at, :], all_ones) + dot_nn(qc[1, at, :], all_ones)
            for j in range(16):
                got = sum_b[16 * j : 16 * j + 8] * pick_b[0]
                got = got + sum_b[16 * j + 8 : 16 * j + 16] * pick_b[1]
                got = got + sum_c[16 * j : 16 * j + 8] * pick_c[0]
                got = got + sum_c[16 * j + 8 : 16 * j + 16] * pick_c[1]
                part3[k * 128 + 8 * j : k * 128 + 8 * j + 8, :] = got
            for j in range(2):
                got = part3[pl.ds(k * 128 + j * 64, 8, stride=8), :]
                for n in range(1, 8):
                    got = got + part3[pl.ds(k * 128 + j * 64 + n, 8, stride=8), :]
                gbc[pl.ds(pl.multiple_of(ctx * ROWS + t0 + 8 * j, 8), 8), :] = got

    backward(0, 0)
    scatter_o.push2(1)
    scatter_z.push1(1)
    scatter_z.push1(0)
    backward(0, 1)
    scatter_o.push2(0)
    for_each(4, functools.partial(sum_lanes, 0))
    backward(1, 0)
    scatter_o.push3(1)
    backward(1, 1)
    scatter_z.push2(2)
    for_each(4, functools.partial(sum_lanes, 1))

    ones = []
    for j in range(GROUPS):
        at = slice(j * LANES, (j + 1) * LANES)
        sv = sig[:, at].astype(F32)
        g_pre = ((yy[:, at] + zz[:, at] * sv) * (1.0 - jnp.exp(-delta[:, at]))).astype(BF16)
        mid[:, at] = g_pre
        ones.append(jnp.sum(g_pre.astype(F32), axis=0, keepdims=True))
    g_bdt = jnp.concatenate(ones, axis=1)

    total = jnp.zeros((256, 64), F32)
    for j in range(GROUPS):
        total = total + dot_nt(
            mid[:, j * LANES : (j + 1) * LANES], wp[j // 4, (j // 2) % 2, j % 2, 96:160, :]
        )
    xd_out[:, 0:64] = total
    xd_out[:, 64:128] = gbc[:, 64:128]
    gd_copy = sems.copy(xd_out, xd_in, mate, seq)
    gd_copy.start()
    scatter_z.push2(3)
    gd_copy.wait()
    g_dbl = (xd_out[...] + xd_in[...]).astype(BF16)

    for ctx in (0, 1):
        for j in range(GROUPS):
            at = slice(j * LANES, (j + 1) * LANES)
            rows = slice(ctx * ROWS, (ctx + 1) * ROWS)
            back = dot_nn(g_dbl[rows, :], wp[j // 4, (j // 2) % 2, j % 2, 0:128, :])
            g_sig = gs[rows, at] * prm[22:23, at] + zz[rows, at] * delta[rows, at] + back
            v = conv_rows(ctx, at)
            sigma = jax.nn.sigmoid(v)
            gext[ctx, 0:128, at] = g_sig * (sigma * (1.0 + v * (1.0 - sigma)))
    edge_copies = [
        sems.copy(gext.at[ctx, pl.ds(0, 8), :], gedge.at[ctx], c, before) for ctx in (0, 1)
    ]
    for copy in edge_copies:
        copy.start()
    scatter_z.push2(1)
    scatter_o.push3(0)

    def small_grads():
        a_rows = -jnp.exp(prm[0:16, :])
        g_alog = (hs[0] + hs[129]) * a_rows
        g_t = jnp.transpose(g_dbl.astype(F32))[0:96].astype(BF16)
        low_t = jnp.transpose(
            jnp.concatenate([low[...].astype(F32), jnp.zeros((256, 64), F32)], axis=1)
        )[0:64].astype(BF16)
        for j in range(GROUPS):
            at = slice(j * LANES, (j + 1) * LANES)
            to = (j // 4, (j // 2) % 2, j % 2)
            sv = sig[:, at].astype(F32)
            gp_w[to + (slice(0, 96),)] = dot_nn(g_t, sig[:, at]).astype(BF16)
            g_dtw = dot_nn(low_t, mid[:, at])
            taps = []
            for k in range(4):
                term = jnp.zeros((1, LANES), F32)
                for ctx in (0, 1):
                    term = term + jnp.sum(
                        gext[ctx, 0:128, at] * xext[ctx, 13 + k : 141 + k, at],
                        axis=0,
                        keepdims=True,
                    )
                taps.append(term)
            bias = jnp.sum(gext[0, 0:128, at] + gext[1, 0:128, at], axis=0, keepdims=True)
            skip = jnp.sum(gs[:, at] * sv, axis=0, keepdims=True)
            rest = jnp.concatenate(
                [g_dtw, g_alog[:, at]]
                + taps
                + [bias, g_bdt[:, at], skip, jnp.zeros((9, LANES), F32)],
                axis=0,
            )
            gp_w[to + (slice(96, 192),)] = rest.astype(BF16)

    small_grads()
    scatter_p = SmallScatter(sems, gp_w, p1, p2, p3)
    scatter_p.push1()

    for copy in edge_copies:
        copy.wait()
    last_chip = (seq < 15).astype(F32)
    for ctx in (0, 1):
        gext[ctx, 128:136, :] = gedge[ctx] * last_chip

    for ctx in (0, 1):

        def x_back(i):
            at = lanes_at(i, LANES)
            total = prm[19:20, at] * gext[ctx, 0:128, at]
            for k in range(3):
                total = total + prm[16 + k : 17 + k, at] * gext[ctx, 3 - k : 131 - k, at]
            mid[ctx * ROWS : (ctx + 1) * ROWS, at] = total.astype(BF16)

        for_each(GROUPS, x_back)

    def x_grads(i):
        d = pl.ds(pl.multiple_of(i * 128, 128), 128)
        for half in (0, 1):
            got = dot_nn(nrm_t[d, :], mid[:, half * 512 : (half + 1) * 512])
            gx_w[half, i // 2, i % 2] = got.astype(BF16).reshape(2, 64, 512)

    scatter_x = Scatter(sems, gx_w, x1, x2, x3)
    scatter_z.push2(0)
    for j in scatter_x.order:
        zj = partner(z, j)
        x_grads(2 * zj)
        x_grads(2 * zj + 1)
        scatter_x.push1(j)
        scatter_z.push3(j)
    def normed_back(i):
        total = jnp.zeros((256, 128), F32)
        for half in (0, 1):
            at = slice(half * 512, (half + 1) * 512)
            total = total + dot_nt(mid[:, at], wx[half, i // 2, i % 2].reshape(128, 512))
            total = total + dot_nt(gz[:, at], wz[half, i // 2, i % 2].reshape(128, 512))
        to = lanes_at(i, 128)
        for ctx in (0, 1):
            rowx[ctx, :, to] = total[ctx * ROWS : (ctx + 1) * ROWS]

    for i in range(4):
        normed_back(i)
    scatter_x.push2(2)
    for i in range(4, 8):
        normed_back(i)
    back_copy = sems.copy(rowx.at[mate], rowx_in.at[1], mate, seq)
    back_copy.start()
    scatter_x.push2(3)
    scatter_x.push2(1)

    def hidden_rows(i):
        at = pl.ds(pl.multiple_of(i * 16, 16), 16)
        rows = hid[at, :].astype(F32)
        r = lax.rsqrt(jnp.mean(rows * rows, axis=1, keepdims=True) + epsilon)
        g_hat = (rowx[c, at, :] + rowx_in[1, at, :]) * gain_row
        inner = jnp.mean(g_hat * rows, axis=1, keepdims=True)
        o_gh[at, :] = r * g_hat - rows * (r * r * r * inner) + out_g[at, :].astype(F32)

    back_copy.wait()
    for_each(8, hidden_rows)
    scatter_x.push3(2)
    scatter_x.push2(0)
    scatter_x.push3(3)
    scatter_x.push3(1)
    scatter_p.push2()
    scatter_x.push3(0)
    scatter_o.done()
    out_copy = sems.copy(o_gout, o_gout, mate, seq)

    @pl.when(is_active())
    def _():
        for half in (0, 1):
            o_gout[:, half * 512 : (half + 1) * 512] = scatter_o.result(half)
        out_copy.start()

    scatter_z.done()
    for half in (0, 1):
        fin[2 + half] = scatter_z.result(half)
    z_copy = sems.copy(fin.at[pl.ds(2, 2)], fin_in.at[pl.ds(2, 2)], mate, seq)
    z_copy.start()
    scatter_p.push3()
    small_copy = sems.copy(fsm, fsm, mate, seq)

    @pl.when(is_active())
    def _():
        fsm[...] = scatter_p.result()
        small_copy.start()

    def weight_rows(part, gain_sum):
        for half in (0, 1):
            for core, ref in ((c, fin), (mate, fin_in)):
                at = pl.ds(pl.multiple_of(part * 2048 + core * 1024 + half * 512, 512), 512)
                rows = ref[part * 2 + half]
                o_gin[:, at] = rows
                gain_sum = gain_sum + fold_lanes(rows * in_w[:, at].astype(F32))
        return gain_sum

    z_copy.wait()
    gain_sum = weight_rows(1, jnp.zeros((64, LANES), F32))
    for group in (gather_x, gather_z, gather_o, gather_p, scatter_z, scatter_o):
        group.sent()

    scatter_x.done()
    for half in (0, 1):
        fin[half] = scatter_x.result(half)
    x_copy = sems.copy(fin.at[pl.ds(0, 2)], fin_in.at[pl.ds(0, 2)], mate, seq)
    x_copy.start()

    @pl.when(is_active())
    def _():
        out_copy.wait_send()
        small_copy.wait_send()

    @pl.when(is_passive())
    def _():
        out_copy.wait_recv()
        small_copy.wait_recv()

    o_small[...] = fsm[...]
    scatter_x.sent()
    scatter_p.sent()
    x_copy.wait()
    o_gain[...] = weight_rows(0, gain_sum)


def fused_shards(
    hidden,
    out_grad,
    resets,
    valid,
    norm_gain,
    in_weight,
    conv_weight,
    conv_bias,
    x_weight,
    dt_weight,
    dt_bias,
    a_log,
    skip_gain,
    out_weight,
):
    norm_row = norm_gain.astype(F32)
    vectors = jnp.stack(
        [
            conv_bias.astype(F32),
            dt_bias.astype(F32),
            skip_gain.astype(F32),
            jnp.concatenate([norm_row, norm_row]),
        ]
    )
    vmem = pltpu.VMEM
    count = 88
    scratch = [
        vmem((2, 144, 1024), BF16),
        vmem((2, 128, 1024), BF16),
        vmem((2, 128, LANES), F32),
        vmem((16, 8, LANES), F32),
        vmem((2, 144, 1024), BF16),
        vmem((1024, 256), BF16),
        vmem((2, 144, 1024), F32),
        vmem((256, 1024), BF16),
        vmem((256, 1024), F32),
        vmem((256, 1024), F32),
        vmem((256, 1024), F32),
        vmem((256, 1024), F32),
        vmem((4096, LANES), F32),
        vmem((4096, LANES), F32),
        vmem((16, 1024), F32),
        vmem((32, 1024), F32),
        vmem((258, 16, 1024), F32),
        vmem((2, 2048, LANES), BF16),
        vmem((2, 2048, LANES), BF16),
        vmem((256, LANES), F32),
        vmem((256, LANES), F32),
        vmem((256, LANES), F32),
        vmem((256, LANES), F32),
        vmem((256, 64), BF16),
        vmem((256, 1024), BF16),
        vmem((1024, 256), BF16),
        vmem((256, 1024), BF16),
        vmem((2, 4, 2, 2, 64, 512), BF16),
        vmem((2, 4, 2, 2, 64, 512), BF16),
        vmem((2, 2, 2, 2, 128, 512), BF16),
        vmem((2, 2, 2, 192, LANES), BF16),
        vmem((2, 4, 2, 2, 64, 512), BF16),
        vmem((2, 4, 2, 2, 64, 512), BF16),
        vmem((2, 2, 2, 2, 128, 512), BF16),
        vmem((2, 2, 2, 192, LANES), BF16),
    ]
    for z_count, rows, columns in ((4, 64, 512), (4, 64, 512), (2, 128, 512)):
        scratch += [
            vmem((2, z_count, 2, rows, columns), BF16),
            vmem((2, z_count, rows, columns), BF16),
            vmem((3, 2, rows, columns), BF16),
        ]
    scratch += [
        vmem((3, 2, 2, 192, LANES), BF16),
        vmem((2, 192, LANES), BF16),
        vmem((192, LANES), BF16),
        vmem((16, 2, 16, LANES), F32),
        vmem((16, 2, 16, LANES), F32),
        vmem((16, 16, LANES), F32),
        vmem((16, 16, LANES), F32),
        vmem((16, 16, LANES), F32),
        vmem((16, 16, LANES), F32),
        vmem((256, LANES), F32),
        vmem((256, LANES), F32),
        vmem((2, 136, 1024), F32),
        vmem((2, 8, 1024), F32),
        vmem((2, 128, 1024), F32),
        vmem((2, 128, 1024), F32),
        vmem((4, 64, 512), F32),
        vmem((4, 64, 512), F32),
        vmem((192, LANES), F32),
        pltpu.SemaphoreType.DMA((count,)),
        pltpu.SemaphoreType.DMA((count,)),
    ]
    whole = pl.BlockSpec(memory_space=pltpu.VMEM)
    parts = pl.pallas_call(
        fused_kernel,
        out_shape=(
            jax.ShapeDtypeStruct((128, 1024), BF16),
            jax.ShapeDtypeStruct((128, 1024), F32),
            jax.ShapeDtypeStruct((64, 4096), F32),
            jax.ShapeDtypeStruct((128, 1024), F32),
            jax.ShapeDtypeStruct((192, LANES), F32),
            jax.ShapeDtypeStruct((64, LANES), F32),
        ),
        in_specs=[pl.BlockSpec(memory_space=pltpu.SMEM)] + [whole] * 10,
        out_specs=(whole,) * 6,
        scratch_shapes=scratch,
        compiler_params=pltpu.CompilerParams(
            collective_id=0, has_side_effects=True, vmem_limit_bytes=64 * 2**20
        ),
    )(
        valid,
        hidden[0],
        out_grad[0],
        resets,
        in_weight,
        out_weight,
        x_weight.T,
        dt_weight.T,
        a_log.T,
        conv_weight.T,
        vectors,
    )
    got = pl.pallas_call(
        place_outputs,
        out_shape=tuple(
            jax.ShapeDtypeStruct(shape, dtype)
            for shape, dtype in (
                ((128, 1024), BF16),
                ((128, 1024), F32),
                ((1, 64), F32),
                ((64, 4096), F32),
                ((4, LANES), F32),
                ((1, LANES), F32),
                ((96, LANES), F32),
                ((64, LANES), F32),
                ((1, LANES), F32),
                ((16, LANES), F32),
                ((1, LANES), F32),
                ((128, 1024), F32),
            )
        ),
        in_specs=[whole] * 7,
        out_specs=(whole,) * 12,
        compiler_params=pltpu.CompilerParams(vmem_limit_bytes=64 * 2**20),
    )(*parts, vectors)
    return (
        got[0][None],
        got[1][None],
        got[2][0],
        got[3],
        got[4].T,
        got[5][0],
        got[6].T,
        got[7].T,
        got[8][0],
        got[9].T,
        got[10][0],
        got[11],
    )


def place_outputs(
    out,
    g_hidden,
    g_in,
    g_out,
    small,
    gain,
    vectors,
    o_out,
    o_hidden,
    o_gain,
    o_in,
    o_taps,
    o_bias,
    o_xw,
    o_dtw,
    o_dtb,
    o_alog,
    o_skip,
    o_outw,
):
    o_out[...] = out[...]
    o_hidden[...] = g_hidden[...]
    o_in[...] = g_in[...]
    o_outw[...] = g_out[...]
    o_xw[...] = small[0:96, :]
    o_dtw[...] = small[96:160, :]
    o_alog[...] = small[160:176, :]
    o_taps[...] = small[176:180, :]
    o_bias[...] = small[180:181, :]
    o_dtb[...] = small[181:182, :]
    o_skip[...] = small[182:183, :]
    turned = jnp.transpose(jnp.concatenate([gain[...], jnp.zeros((64, LANES), F32)], axis=0))
    o_gain[...] = (jnp.sum(turned, axis=0, keepdims=True) / vectors[3:4, :])[:, 0:64]


def solution(mesh):
    sizes = dict(mesh.shape)
    body = fused_shards if sizes == {"ctx": 2, "seq": 16} else shards
    return jax.shard_map(
        body,
        mesh=mesh,
        in_specs=(
            P("ctx", "seq", None),
            P("ctx", "seq", None),
            P("ctx", "seq"),
            P("ctx"),
            P("seq"),
            P("seq", None),
            P("seq", None),
            P("seq"),
            P("seq", None),
            P("seq", None),
            P("seq"),
            P("seq", None),
            P("seq"),
            P("seq", None),
        ),
        out_specs=(
            P("ctx", "seq", None),
            P("ctx", "seq", None),
            P("seq"),
            P("seq", None),
            P("seq", None),
            P("seq"),
            P("seq", None),
            P("seq", None),
            P("seq"),
            P("seq", None),
            P("seq"),
            P("seq", None),
        ),
        check_vma=False,
    )
```

```python
import functools

import jax
import jax.numpy as jnp
from jax import lax
from jax.experimental import pallas as pl
from jax.experimental.pallas import tpu as pltpu
from jax.sharding import PartitionSpec as P

epsilon = 1e-05
highest = lax.Precision.HIGHEST
contract_last = (((1,), (1,)), ((), ()))
contract_first = (((0,), (0,)), ((), ()))


def passed_along(block, axis, distance):
    devices = range(lax.axis_size(axis))
    route = [(i - distance, i) for i in devices if i - distance in devices]
    return lax.ppermute(block, axis, route)


def entering_2(part, axis, combine, identity, reverse):
    count = lax.axis_size(axis)
    place = lax.axis_index(axis)
    ahead = count - 1 - place if reverse else place
    gathered = jax.tree.map(lambda a: lax.all_gather(a, axis), part)
    state = jax.tree.map(lambda a, e: jnp.zeros_like(a) + jnp.asarray(e, a.dtype), part, identity)

    def one(hop, state):
        source = count - 1 - hop if reverse else hop
        return combine(
            state, jax.tree.map(lambda a: lax.dynamic_index_in_dim(a, source, 0, False), gathered)
        )

    return lax.fori_loop(0, ahead, one, state)


def silu_slope(value):
    sigma = jax.nn.sigmoid(value)
    return sigma * (1.0 + value * (1.0 - sigma))


def combine_pair(earlier, later):
    return (earlier[0] * later[0], later[0] * earlier[1] + later[1])


def decays_of(delta_blk, keep_blk, a_matrix):
    return keep_blk[:, None, None] * jnp.exp(delta_blk[:, :, None] * a_matrix[None])


def shards(
    hidden,
    out_grad,
    resets,
    valid,
    norm_gain,
    in_weight,
    conv_weight,
    conv_bias,
    x_weight,
    dt_weight,
    dt_bias,
    a_log,
    skip_gain,
    out_weight,
):
    gathered = (
        lax.all_gather(norm_gain, "seq", axis=0, tiled=True),
        lax.all_gather(in_weight, "seq", axis=0, tiled=True),
        lax.all_gather(conv_weight, "seq", axis=0, tiled=True),
        lax.all_gather(conv_bias, "seq", axis=0, tiled=True),
        lax.all_gather(x_weight, "seq", axis=0, tiled=True),
        lax.all_gather(dt_weight, "seq", axis=0, tiled=True),
        lax.all_gather(dt_bias, "seq", axis=0, tiled=True),
        lax.all_gather(a_log, "seq", axis=0, tiled=True),
        lax.all_gather(skip_gain, "seq", axis=0, tiled=True),
        lax.all_gather(out_weight, "seq", axis=0, tiled=True),
    )
    gain_full, w_in, w_conv, b_conv, w_x, w_dt, b_dt, a_logs, w_skip, w_out = gathered
    tokens = hidden.shape[1]
    inner = w_out.shape[0]
    rank = w_dt.shape[1]
    state = a_logs.shape[1]
    taps = w_conv.shape[1]
    places = lax.axis_index("seq") * tokens + jnp.arange(tokens, dtype=jnp.int32)
    live_mask = (places < valid[0]).astype(jnp.float32)
    reset_f = resets[0].astype(jnp.float32)
    keep_mask = 1.0 - reset_f
    source = hidden[0].astype(jnp.float32)
    rscale = lax.rsqrt(jnp.mean(source * source, axis=-1, keepdims=True) + epsilon)
    scaled = source * rscale
    gain_f = gain_full.astype(jnp.float32)
    normed = (scaled * gain_f).astype(jnp.bfloat16)
    projected = jnp.dot(normed, w_in, preferred_element_type=jnp.float32)
    x_part = projected[:, :inner].astype(jnp.bfloat16)
    z_part = projected[:, inner:]
    rim_rows = passed_along(x_part[tokens - (taps - 1) :], "seq", 1)
    extended = jnp.concatenate([rim_rows, x_part], 0).astype(jnp.float32)
    conv_taps = w_conv.astype(jnp.float32)
    conv_out = b_conv.astype(jnp.float32) + sum(
        (conv_taps[:, offset] * extended[offset : offset + tokens] for offset in range(taps))
    )
    signal_low = jax.nn.silu(conv_out).astype(jnp.bfloat16)
    signal = signal_low.astype(jnp.float32)
    x_dbl = jnp.dot(signal_low, w_x, preferred_element_type=jnp.float32)
    dt_low = x_dbl[:, :rank].astype(jnp.bfloat16)
    b_input = x_dbl[:, rank : rank + state]
    c_output = x_dbl[:, rank + state :]
    dt_pre = lax.dot_general(
        dt_low, w_dt, contract_last, preferred_element_type=jnp.float32
    ) + b_dt.astype(jnp.float32)
    delta = jax.nn.softplus(dt_pre)
    a_matrix = -jnp.exp(a_logs.astype(jnp.float32))
    drive = delta * signal
    reset_count = jnp.cumsum(reset_f)
    reset_before = reset_count - reset_f
    delta_sum = jnp.cumsum(delta, 0)
    delta_before = delta_sum - delta
    reset_total = reset_count[-1]
    delta_total = delta_sum[-1]
    alive_upto = (reset_count == 0.0).astype(jnp.float32)
    alive_before = (reset_before == 0.0).astype(jnp.float32)
    alive_after = (reset_total - reset_count == 0.0).astype(jnp.float32)
    span_len = min(64, tokens)
    n_blocks = tokens // span_len
    roll_by = min(16, span_len)

    def split_blocks(value):
        return value.reshape((n_blocks, span_len) + value.shape[1:])

    delta_b = split_blocks(delta)
    drive_b = split_blocks(drive)
    binput_b = split_blocks(b_input)
    coutput_b = split_blocks(c_output)
    keep_b = split_blocks(keep_mask)
    dsum_b = split_blocks(delta_sum)
    upto_b = split_blocks(alive_upto)
    after_b = split_blocks(alive_after)
    ones_state = jnp.ones((inner, state), jnp.float32)
    zero_state = jnp.zeros((inner, state), jnp.float32)
    group_prod = (reset_total == 0.0).astype(jnp.float32) * jnp.exp(delta_total[:, None] * a_matrix)

    def forward_step(state_now, blk):
        delta_blk, drive_blk, binput_blk, coutput_blk, keep_blk = blk
        decays = decays_of(delta_blk, keep_blk, a_matrix)

        def token_step(state_tok, item):
            decay_now, drive_now, binput_now, coutput_now = item
            state_next = decay_now * state_tok + drive_now[:, None] * binput_now[None, :]
            return (state_next, jnp.sum(state_next * coutput_now[None, :], -1))

        state_end, outputs = lax.scan(
            token_step, state_now, (decays, drive_blk, binput_blk, coutput_blk), unroll=roll_by
        )
        return (state_end, (state_now, outputs))

    group_state, (local_starts, scan_local) = lax.scan(
        forward_step, zero_state, (delta_b, drive_b, binput_b, coutput_b, keep_b)
    )
    entering = entering_2(
        (group_prod, group_state), "seq", combine_pair, (ones_state, zero_state), False
    )
    state_in = entering[1]

    def lift_block(blk):
        dsum_blk, upto_blk, coutput_blk = blk
        lifted = (
            upto_blk[:, None, None]
            * jnp.exp(dsum_blk[:, :, None] * a_matrix[None])
            * state_in[None]
        )
        return jnp.sum(lifted * coutput_blk[:, None, :], -1)

    lifted_out = lax.map(lift_block, (dsum_b, upto_b, coutput_b))
    scanned = (scan_local + lifted_out).reshape(tokens, inner) + w_skip.astype(jnp.float32) * signal
    gate_act = jax.nn.silu(z_part)
    mixed = (scanned * gate_act).astype(jnp.bfloat16)
    branch = jnp.dot(mixed, w_out, preferred_element_type=jnp.float32)
    result = (source + live_mask[:, None] * branch).astype(jnp.bfloat16)
    regathered = (
        lax.all_gather(norm_gain, "seq", axis=0, tiled=True),
        lax.all_gather(in_weight, "seq", axis=0, tiled=True),
        lax.all_gather(conv_weight, "seq", axis=0, tiled=True),
        lax.all_gather(conv_bias, "seq", axis=0, tiled=True),
        lax.all_gather(x_weight, "seq", axis=0, tiled=True),
        lax.all_gather(dt_weight, "seq", axis=0, tiled=True),
        lax.all_gather(dt_bias, "seq", axis=0, tiled=True),
        lax.all_gather(a_log, "seq", axis=0, tiled=True),
        lax.all_gather(skip_gain, "seq", axis=0, tiled=True),
        lax.all_gather(out_weight, "seq", axis=0, tiled=True),
    )
    gain_full, w_in, w_conv, b_conv, w_x, w_dt, b_dt, a_logs, w_skip, w_out = regathered
    gain_f = gain_full.astype(jnp.float32)
    conv_taps = w_conv.astype(jnp.float32)
    a_matrix = -jnp.exp(a_logs.astype(jnp.float32))
    cotangent = out_grad[0].astype(jnp.float32)
    g_branch = (live_mask[:, None] * cotangent).astype(jnp.bfloat16)
    g_mixed = lax.dot_general(g_branch, w_out, contract_last, preferred_element_type=jnp.float32)
    g_scan = g_mixed * gate_act
    g_zpart = g_mixed * scanned * silu_slope(z_part)
    g_skip_full = jnp.sum(g_scan * signal, 0)
    gscan_b = split_blocks(g_scan)

    def push_block(total, blk):
        dsum_blk, upto_blk, coutput_blk, gscan_blk = blk
        weight_blk = upto_blk[:, None, None] * jnp.exp(dsum_blk[:, :, None] * a_matrix[None])
        return (
            total + jnp.sum(weight_blk * gscan_blk[:, :, None] * coutput_blk[:, None, :], 0),
            None,
        )

    passed_local, _ = lax.scan(push_block, zero_state, (dsum_b, upto_b, coutput_b, gscan_b))
    leaving = entering_2(
        (group_prod, passed_local), "seq", combine_pair, (ones_state, zero_state), True
    )
    passed_in = leaving[1]
    start_rows = jnp.arange(n_blocks) * span_len
    start_alive = alive_before[start_rows]
    start_delta = delta_before[start_rows]
    block_starts = (
        local_starts
        + start_alive[:, None, None]
        * jnp.exp(start_delta[:, :, None] * a_matrix[None])
        * state_in[None]
    )

    def backward_step(carried, blk):
        passed, grad_amat = carried
        (
            start_state,
            delta_blk,
            drive_blk,
            binput_blk,
            coutput_blk,
            gscan_blk,
            keep_blk,
            dsum_blk,
            after_blk,
        ) = blk
        decays = decays_of(delta_blk, keep_blk, a_matrix)

        def ahead_step(state_tok, item):
            decay_now, drive_now, binput_now = item
            state_next = decay_now * state_tok + drive_now[:, None] * binput_now[None, :]
            return (state_next, state_next)

        _, states_blk = lax.scan(
            ahead_step, start_state, (decays, drive_blk, binput_blk), unroll=roll_by
        )
        before = jnp.concatenate([start_state[None], states_blk[:-1]], 0)

        def behind_step(passed_tok, item):
            decay_now, coutput_now, gscan_now = item
            adjoint = gscan_now[:, None] * coutput_now[None, :] + passed_tok
            return (decay_now * adjoint, adjoint)

        passed, adjoints_local = lax.scan(
            behind_step, passed, (decays, coutput_blk, gscan_blk), reverse=True, unroll=roll_by
        )
        reach = after_blk[:, None, None] * jnp.exp(
            (delta_total[None] - dsum_blk)[:, :, None] * a_matrix[None]
        )
        adjoints = adjoints_local + reach * passed_in[None]
        flow = adjoints * before * decays
        g_delta_decay = jnp.sum(flow * a_matrix[None], -1)
        grad_amat = grad_amat + jnp.sum(flow * delta_blk[:, :, None], 0)
        g_drive = jnp.einsum("qen,qn->qe", adjoints, binput_blk, precision=highest)
        g_binput = jnp.einsum("qen,qe->qn", adjoints, drive_blk, precision=highest)
        g_coutput = jnp.einsum("qen,qe->qn", states_blk, gscan_blk, precision=highest)
        return ((passed, grad_amat), (g_delta_decay, g_drive, g_binput, g_coutput))

    (_, grad_amat), pieces = lax.scan(
        backward_step,
        (zero_state, zero_state),
        (block_starts, delta_b, drive_b, binput_b, coutput_b, gscan_b, keep_b, dsum_b, after_b),
        reverse=True,
    )
    g_delta_decay = pieces[0].reshape(tokens, inner)
    g_drive = pieces[1].reshape(tokens, inner)
    g_binput = pieces[2].reshape(tokens, state)
    g_coutput = pieces[3].reshape(tokens, state)
    g_delta = g_delta_decay + g_drive * signal
    g_pre = (g_delta * jax.nn.sigmoid(dt_pre)).astype(jnp.bfloat16)
    g_dtlow = jnp.dot(g_pre, w_dt, preferred_element_type=jnp.float32)
    g_xdbl = jnp.concatenate([g_dtlow, g_binput, g_coutput], 1).astype(jnp.bfloat16)
    g_signal = (
        g_scan * w_skip.astype(jnp.float32)
        + g_drive * delta
        + lax.dot_general(g_xdbl, w_x, contract_last, preferred_element_type=jnp.float32)
    )
    g_conv = g_signal * silu_slope(conv_out)
    g_extended = sum(
        (
            jnp.pad(conv_taps[:, offset] * g_conv, ((offset, taps - 1 - offset), (0, 0)))
            for offset in range(taps)
        )
    )
    returned = passed_along(g_extended[: taps - 1], "seq", -1)
    g_xpart = g_extended[taps - 1 :] + jnp.pad(returned, ((tokens - (taps - 1), 0), (0, 0)))
    g_proj = jnp.concatenate([g_xpart, g_zpart], 1).astype(jnp.bfloat16)
    g_normed = lax.dot_general(g_proj, w_in, contract_last, preferred_element_type=jnp.float32)
    g_hat = g_normed * gain_f
    grad_source = (
        rscale * g_hat
        - source * rscale * rscale * rscale * jnp.mean(g_hat * source, axis=-1, keepdims=True)
        + cotangent
    )
    g_gain = jnp.sum(g_normed * scaled, 0)
    g_wconv = jnp.stack(
        [jnp.sum(g_conv * extended[offset : offset + tokens], 0) for offset in range(taps)], 1
    )
    g_bconv = jnp.sum(g_conv, 0)
    g_bdt = jnp.sum(g_pre.astype(jnp.float32), 0)
    g_alog = grad_amat * a_matrix
    weight_rows = lax.dot_general(
        normed, g_proj, contract_first, preferred_element_type=jnp.float32
    )
    g_win_rows, g_gain_rows = lax.psum_scatter(
        (weight_rows, g_gain), "seq", scatter_dimension=0, tiled=True
    )
    xw_rows = lax.dot_general(
        signal_low, g_xdbl, contract_first, preferred_element_type=jnp.float32
    )
    dtw_rows = lax.dot_general(g_pre, dt_low, contract_first, preferred_element_type=jnp.float32)
    outw_rows = lax.dot_general(mixed, g_branch, contract_first, preferred_element_type=jnp.float32)
    (
        g_wconv_rows,
        g_bconv_rows,
        g_wx_rows,
        g_wdt_rows,
        g_bdt_rows,
        g_alog_rows,
        g_skip_rows,
        g_wout_rows,
    ) = lax.psum_scatter(
        (g_wconv, g_bconv, xw_rows, dtw_rows, g_bdt, g_alog, g_skip_full, outw_rows),
        "seq",
        scatter_dimension=0,
        tiled=True,
    )
    totals = lax.psum(
        (
            g_gain_rows,
            g_win_rows,
            g_wconv_rows,
            g_bconv_rows,
            g_wx_rows,
            g_wdt_rows,
            g_bdt_rows,
            g_alog_rows,
            g_skip_rows,
            g_wout_rows,
        ),
        "ctx",
    )
    return (
        result[None],
        grad_source[None],
        totals[0],
        totals[1],
        totals[2],
        totals[3],
        totals[4],
        totals[5],
        totals[6],
        totals[7],
        totals[8],
        totals[9],
    )


MESH = pl.DeviceIdType.MESH
F32 = jnp.float32
BF16 = jnp.bfloat16
ROWS = 128
GROUPS = 8
LANES = 128
WIDE = 512
LOG2E = 1.4426950408889634


def place():
    seq = lax.axis_index("seq")
    return lax.axis_index("ctx"), seq, seq // 4, (seq // 2) % 2, seq % 2


def chip(z, y, x):
    return z * 4 + y * 2 + x


class Semaphores:
    def __init__(self, send, receive):
        self.send, self.receive = send, receive
        self.sends = self.receives = 0

    def new_send(self):
        self.sends += 1
        return self.send.at[self.sends - 1]

    def new_receive(self):
        self.receives += 1
        return self.receive.at[self.receives - 1]

    def copy(self, source, target, core, seq, send=None, receive=None):
        return pltpu.make_async_remote_copy(
            src_ref=source,
            dst_ref=target,
            send_sem=self.new_send() if send is None else send,
            recv_sem=self.new_receive() if receive is None else receive,
            device_id=(core, seq),
            device_id_type=MESH,
        )


def joint(region, copy_sems):
    c, _, z, y, x = place()
    send, receive = copy_sems
    return pltpu.make_async_remote_copy(
        src_ref=region,
        dst_ref=region,
        send_sem=send,
        recv_sem=receive,
        device_id=(c, chip(z, y, 1 - x)),
        device_id_type=MESH,
    )


def partner(z, j):
    return (z, z + 1 - 2 * (z % 2), (z + 2) % 4, 3 - z)[j]


class Gather:
    slots = 4

    def __init__(self, sems, buf):
        c, _, z, y, x = place()
        own = self.slot(0)
        self.first = [
            sems.copy(buf.at[:, own, y, x], buf.at[:, own, y, x], c, chip(partner(z, j), y, x))
            for j in (1, 2, 3)
        ]
        send2, send3 = sems.new_send(), sems.new_send()
        self.second, self.second_all, self.third, self.third_all = [], [], [], []
        for j in range(self.slots):
            s = self.slot(j)
            got = sems.new_receive()
            self.second.append(
                [
                    sems.copy(buf.at[0, s, y, x], buf.at[0, s, y, x], c, chip(z, 1 - y, x), send2, got),
                    sems.copy(buf.at[1, s, y, x], buf.at[1, s, y, x], c, chip(z, y, 1 - x), send2, got),
                ]
            )
            self.second_all.append(joint(buf.at[:, s, y, x], (send2, got)))
            got = sems.new_receive()
            self.third.append(
                [
                    sems.copy(buf.at[0, s, :, x], buf.at[0, s, :, x], c, chip(z, y, 1 - x), send3, got),
                    sems.copy(buf.at[1, s, y], buf.at[1, s, y], c, chip(z, 1 - y, x), send3, got),
                ]
            )
            self.third_all.append(joint(buf.at[:, s, :, x], (send3, got)))
        self.second_sent = joint(buf.at[:, :, y, x], (send2, got))
        self.third_sent = joint(buf.at[:, :, :, x], (send3, got))

    def slot(self, j):
        return partner(place()[2], j)

    def start(self):
        for copy in self.first:
            copy.start()

    def arrived(self, j):
        if j > 0:
            self.first[j - 1].wait_recv()

    def relay(self, j):
        self.arrived(j)
        for copy in self.second[j]:
            copy.start()

    def cross(self, j):
        self.second_all[j].wait_recv()
        for copy in self.third[j]:
            copy.start()

    def slot_done(self, j):
        self.third_all[j].wait_recv()

    def done(self):
        for j in range(self.slots):
            self.slot_done(j)

    def sent(self):
        for copy in self.first:
            copy.wait_send()
        self.sent_rest()

    def sent_rest(self):
        self.second_sent.wait_send()
        self.third_sent.wait_send()


def is_active():
    c, _, z, _, _ = place()
    return z // 2 == c


def is_passive():
    return jnp.logical_not(is_active())


def half_slot(j):
    z = place()[2]
    return z % 2 if j == 0 else 1 - z % 2


class HalfGather(Gather):
    slots = 2

    def slot(self, j):
        return half_slot(j)

    def start(self):
        @pl.when(is_active())
        def _():
            for copy in self.first:
                copy.start()

    def arrived(self, j):
        if j == 1:

            @pl.when(is_active())
            def _():
                self.first[0].wait_recv()

        @pl.when(is_passive())
        def _():
            self.first[1 + j].wait_recv()

    def sent(self):
        @pl.when(is_active())
        def _():
            for copy in self.first:
                copy.wait_send()

        self.sent_rest()


def add_into(total, part):
    total[...] = total[...] + part[...]


class Scatter:
    order = (2, 3, 1, 0)

    def __init__(self, sems, grad, came1, came2, came3):
        c, _, z, y, x = place()
        self.grad, self.came1, self.came2, self.came3 = grad, came1, came2, came3
        send1, send2 = sems.new_send(), sems.new_send()
        self.first, self.first_all, self.second, self.second_all = [], [], [], []
        for j in range(len(self.order)):
            s = self.slot(j)
            got = sems.new_receive()
            self.first.append(
                [
                    sems.copy(grad.at[0, s, :, 1 - x], came1.at[0, s], c, chip(z, y, 1 - x), send1, got),
                    sems.copy(grad.at[1, s, 1 - y], came1.at[1, s], c, chip(z, 1 - y, x), send1, got),
                ]
            )
            self.first_all.append(joint(came1.at[:, s], (send1, got)))
            got = sems.new_receive()
            self.second.append(
                [
                    sems.copy(grad.at[0, s, 1 - y, x], came2.at[0, s], c, chip(z, 1 - y, x), send2, got),
                    sems.copy(grad.at[1, s, y, 1 - x], came2.at[1, s], c, chip(z, y, 1 - x), send2, got),
                ]
            )
            self.second_all.append(joint(came2.at[:, s], (send2, got)))
        self.first_sent = joint(came1, (send1, got))
        self.second_sent = joint(came2, (send2, got))
        got = sems.new_receive()
        self.third = [
            sems.copy(
                grad.at[:, self.slot(self.third_slot(j)), y, x],
                came3.at[j - 1],
                c,
                chip(partner(z, j), y, x),
                None,
                got,
            )
            for j in (1, 2, 3)
        ]
        self.third_all = joint(came3, (send2, got))

    def slot(self, j):
        return partner(place()[2], j)

    def third_slot(self, j):
        return j

    def push1(self, j):
        for copy in self.first[j]:
            copy.start()

    def push2(self, j):
        _, _, _, y, x = place()
        s = self.slot(j)
        self.first_all[j].wait_recv()
        add_into(self.grad.at[0, s, 1 - y, x], self.came1.at[0, s, 1 - y])
        self.second[j][0].start()
        add_into(self.grad.at[1, s, y, 1 - x], self.came1.at[1, s, 1 - x])
        self.second[j][1].start()
        add_into(self.grad.at[0, s, y, x], self.came1.at[0, s, y])
        add_into(self.grad.at[1, s, y, x], self.came1.at[1, s, x])

    def push3(self, j):
        _, _, _, y, x = place()
        s = self.slot(j)
        self.second_all[j].wait_recv()
        for half in (0, 1):
            add_into(self.grad.at[half, s, y, x], self.came2.at[half, s])
        self.send_on(j)

    def send_on(self, j):
        if j > 0:
            self.third[j - 1].start()

    def all1(self):
        for j in self.order:
            self.push1(j)

    def all2(self):
        for j in self.order:
            self.push2(j)

    def all3(self):
        for j in self.order:
            self.push3(j)

    def done(self):
        self.third_all.wait_recv()

    def sent(self):
        for copy in self.third:
            copy.wait_send()
        self.sent_rest()

    def sent_rest(self):
        self.first_sent.wait_send()
        self.second_sent.wait_send()

    def result(self, half):
        _, _, _, y, x = place()
        total = self.grad[half, self.slot(0), y, x].astype(F32)
        for k in range(3):
            total = total + self.came3[k, half].astype(F32)
        return total


class HalfScatter(Scatter):
    order = (1, 0)

    def slot(self, j):
        return half_slot(j)

    def third_slot(self, j):
        return j % 2

    def send_on(self, j):
        if j == 1:

            @pl.when(is_active())
            def _():
                self.third[0].start()

        @pl.when(is_passive())
        def _():
            self.third[1 + j].start()

    def done(self):
        @pl.when(is_active())
        def _():
            self.third_all.wait_recv()

    def sent(self):
        @pl.when(is_active())
        def _():
            self.third[0].wait_send()

        @pl.when(is_passive())
        def _():
            self.third[1].wait_send()
            self.third[2].wait_send()

        self.sent_rest()


class Transpose:
    def __init__(self, sems, source, target):
        c, seq, _, _, _ = place()
        self.source, self.target = source, target
        pair = (sems.new_send(), sems.new_receive())
        self.copies = [
            sems.copy(source.at[(seq + k) % 16], target.at[seq], c, (seq + k) % 16, *pair)
            for k in range(1, 16)
        ]
        self.all = joint(target.at[pl.ds(0, 15)], pair)

    def start(self):
        _, seq, _, _, _ = place()
        for copy in self.copies:
            copy.start()
        self.target[seq] = self.source[seq]

    def done(self):
        self.all.wait_recv()

    def sent(self):
        self.all.wait_send()


def wide(tile, count=WIDE // LANES):
    return jnp.concatenate([tile] * count, axis=1)


def rows_of(ref, base):
    return jnp.broadcast_to(ref[pl.ds(base, 1), :], (16, LANES))


def spread(slab, j):
    return jnp.broadcast_to(slab[j : j + 1, :], (16, slab.shape[1]))


def put_partial(ref, j, value):
    folded = value[:8] + value[8:]
    for g in range(WIDE // LANES):
        ref[pl.ds(g * 64 + 8 * j, 8), :] = folded[:, g * LANES : (g + 1) * LANES]


def take_partial(ref):
    out = []
    for g in range(WIDE // LANES):
        total = ref[pl.ds(g * 64, 8, stride=8), :]
        for j in range(1, 8):
            total = total + ref[pl.ds(g * 64 + j, 8, stride=8), :]
        out.append(total)
    return jnp.concatenate(out, axis=1)


def fold_lanes(value):
    total = value[:, :LANES]
    for g in range(1, value.shape[1] // LANES):
        total = total + value[:, g * LANES : (g + 1) * LANES]
    return total


def dot_nn(a, b):
    return jnp.dot(a, b, preferred_element_type=F32)


def dot_nt(a, b):
    return lax.dot_general(a, b, contract_last, preferred_element_type=F32)


def dot_tn(a, b):
    return lax.dot_general(a, b, contract_first, preferred_element_type=F32)


def for_each(count, body):
    def step(i, carry):
        body(i)
        return carry

    lax.fori_loop(0, count, step, 0)


def lanes_at(i, width):
    return pl.ds(pl.multiple_of(i * width, width), width)


def fused_kernel(
    valid,
    hid,
    out_g,
    resets,
    in_w,
    out_w,
    x_w,
    dt_w,
    a_log,
    conv_w,
    vectors,
    o_out,
    o_gh,
    o_gin,
    o_gout,
    o_small,
    o_gain,
    hidb,
    gbr,
    kb,
    gain_b,
    nrm,
    nrm_t,
    xext,
    sig,
    delta,
    zz,
    gs,
    yy,
    bb,
    cb,
    a2,
    prm,
    hs,
    qb,
    qc,
    part1,
    part2,
    part3,
    gbc,
    low,
    mid,
    mid_t,
    gz,
    wx,
    wz,
    wo,
    wp,
    gx_w,
    gz_w,
    go_w,
    gp_w,
    x1,
    x2,
    x3,
    z1,
    z2,
    z3,
    o1,
    o2,
    o3,
    p1,
    p2,
    p3,
    hp,
    hpr,
    hret,
    hin,
    lret,
    lin,
    lp,
    lpr,
    xd_out,
    xd_in,
    gext,
    gedge,
    rowx,
    rowx_in,
    fin,
    fin_in,
    fsm,
    send_sems,
    recv_sems,
):
    c, seq, z, y, x = place()
    mate = 1 - c
    after = (seq + 1) % 16
    before = (seq + 15) % 16
    sems = Semaphores(send_sems, recv_sems)

    barrier = pltpu.get_barrier_semaphore()
    for k in range(1, 16):
        pl.semaphore_signal(
            barrier, inc=1, device_id=(c, (seq + k) % 16), device_id_type=MESH
        )
    pl.semaphore_signal(barrier, inc=1, device_id=(mate, seq), device_id_type=MESH)
    pl.semaphore_signal(barrier, inc=1, device_id=(mate, after), device_id_type=MESH)
    pl.semaphore_signal(barrier, inc=1, device_id=(mate, before), device_id_type=MESH)

    for half in (0, 1):
        wx[half, z, y, x] = in_w[:, pl.ds(pl.multiple_of(c * 1024 + half * 512, 512), 512)]
        wz[half, z, y, x] = in_w[
            :, pl.ds(pl.multiple_of(2048 + c * 1024 + half * 512, 512), 512)
        ]

    @pl.when(z // 2 == c)
    def _():
        for half in (0, 1):
            wo[half, z % 2, y, x] = out_w[:, half * 512 : (half + 1) * 512]
        wp[0, z % 2, y, x] = x_w[...]
        wp[1, z % 2, y, x, 0:64, :] = dt_w[...]
        wp[1, z % 2, y, x, 64:80, :] = a_log[...]
        wp[1, z % 2, y, x, 80:96, :] = jnp.concatenate(
            [conv_w[...].astype(F32), vectors[0:3, :], jnp.zeros((9, LANES), F32)], axis=0
        ).astype(BF16)

    lane = lax.broadcasted_iota(jnp.int32, (8, LANES), 1)
    gain_mine = jnp.where(lane // 64 == x, jnp.broadcast_to(vectors[3:4, :], (8, LANES)), 0.0)
    gain_b[seq] = gain_mine
    kb[c] = jnp.transpose(
        jnp.broadcast_to(1.0 - resets[...].astype(F32), (ROWS, LANES))
    )
    row_place = seq * ROWS + lax.broadcasted_iota(jnp.int32, (ROWS, LANES), 0)
    live = (row_place < valid[0]).astype(F32)
    hidb[c, pl.ds(16, ROWS), :] = hid[...]
    for g in range(GROUPS):
        at = slice(g * LANES, (g + 1) * LANES)
        gbr[c, :, at] = (live * out_g[:, at].astype(F32)).astype(BF16)

    pl.semaphore_wait(barrier, 18)

    gather_x = Gather(sems, wx)
    gather_z = Gather(sems, wz)
    gather_o = HalfGather(sems, wo)
    gather_p = HalfGather(sems, wp)
    gain_sems = (sems.new_send(), sems.new_receive())
    gain_copies = [
        sems.copy(gain_b.at[seq], gain_b.at[seq], c, (seq + k) % 16, *gain_sems)
        for k in range(1, 16)
    ]
    gain_all = joint(gain_b.at[pl.ds(0, 15)], gain_sems)
    hid_copies = [
        sems.copy(hidb.at[c, pl.ds(16, ROWS), :], hidb.at[c, pl.ds(16, ROWS), :], mate, seq),
        sems.copy(hidb.at[c, pl.ds(128, 16), :], hidb.at[c, pl.ds(0, 16), :], c, after),
        sems.copy(hidb.at[c, pl.ds(128, 16), :], hidb.at[c, pl.ds(0, 16), :], mate, after),
        sems.copy(kb.at[c], kb.at[c], mate, seq),
    ]
    gbr_copy = sems.copy(gbr.at[c], gbr.at[c], mate, seq)
    for copy in hid_copies:
        copy.start()
    for copy in gain_copies:
        copy.start()
    gather_p.start()
    gather_x.start()
    gather_x.relay(0)

    for copy in hid_copies:
        copy.wait_recv()
    gather_p.relay(0)
    gather_p.relay(1)
    gain_all.wait_recv()
    gain_row = jnp.concatenate(
        [gain_b[2 * g][0:1, :] + gain_b[2 * g + 1][0:1, :] for g in range(GROUPS)], axis=1
    )
    for ctx in (0, 1):

        def norm_rows(i):
            at = pl.ds(pl.multiple_of(i * 16, 16), 16)
            rows = hidb[ctx, at, :].astype(F32)
            r = lax.rsqrt(jnp.mean(rows * rows, axis=1, keepdims=True) + epsilon)
            nrm[ctx, at, :] = (rows * r * gain_row).astype(BF16)

        for_each(9, norm_rows)
    gather_p.cross(0)
    gather_p.cross(1)
    gather_z.start()
    for ctx in (0, 1):
        for g in range(GROUPS):
            at = slice(g * LANES, (g + 1) * LANES)
            nrm_t[at, ctx * ROWS : (ctx + 1) * ROWS] = jnp.transpose(
                nrm[ctx, 16:144, at].astype(F32)
            ).astype(BF16)

    gather_x.relay(1)
    gather_x.cross(0)
    gather_x.relay(2)
    gather_x.cross(1)
    gather_x.relay(3)
    gather_o.start()
    gather_x.cross(2)
    gather_x.cross(3)
    gbr_copy.start()
    gather_z.relay(0)
    gather_x.done()
    gather_z.relay(1)
    gather_z.cross(0)
    first_chip = (seq > 0).astype(F32)
    for half in (0, 1):

        def x_columns(i):
            rows = nrm[...].reshape(288, 1024)
            w = wx[half, :, :, :, :, lanes_at(i, 256)].reshape(1024, 256)
            got = dot_nn(rows, w).astype(BF16).astype(F32)
            at = pl.ds(pl.multiple_of(half * 512 + i * 256, 256), 256)
            for ctx in (0, 1):
                xext[ctx, 0:16, at] = got[ctx * 144 : ctx * 144 + 16] * first_chip
                xext[ctx, 16:144, at] = got[ctx * 144 + 16 : ctx * 144 + 144]

        for_each(2, x_columns)

    gather_z.relay(2)
    gather_z.cross(1)
    gather_p.done()
    for j in range(GROUPS):
        prm[:, j * LANES : (j + 1) * LANES] = wp[
            1, j // 4, (j // 2) % 2, j % 2, 64:96, :
        ].astype(F32)
    a2[...] = -jnp.exp(prm[0:16, :]) * LOG2E

    def conv_rows(ctx, at):
        total = prm[20:21, at] + prm[16:17, at] * xext[ctx, 13:141, at]
        for k in range(1, 4):
            total = total + prm[16 + k : 17 + k, at] * xext[ctx, 13 + k : 141 + k, at]
        return total

    for ctx in (0, 1):

        def conv_columns(i):
            at = lanes_at(i, LANES)
            total = conv_rows(ctx, at)
            rows = slice(ctx * ROWS, (ctx + 1) * ROWS)
            sig[rows, at] = (total * jax.nn.sigmoid(total)).astype(BF16)

        for_each(GROUPS, conv_columns)

    total = jnp.zeros((256, 96), F32)
    for j in range(GROUPS):
        total = total + dot_nt(
            sig[:, j * LANES : (j + 1) * LANES], wp[0, j // 4, (j // 2) % 2, j % 2]
        )
    xd_out[:, 0:96] = total
    xd_out[:, 96:128] = jnp.zeros((256, 32), F32)
    xd_copy = sems.copy(xd_out, xd_in, mate, seq)
    xd_copy.start()
    gather_z.relay(3)
    gather_z.cross(2)
    xd_copy.wait()
    xd = xd_out[...] + xd_in[...]
    low[...] = xd[:, 0:64].astype(BF16)
    for n in range(16):
        bb[pl.ds(n, 256, stride=16), :] = jnp.broadcast_to(xd[:, 64 + n : 65 + n], (256, LANES))
        cb[pl.ds(n, 256, stride=16), :] = jnp.broadcast_to(xd[:, 80 + n : 81 + n], (256, LANES))
    for j in range(GROUPS):
        at = slice(j * LANES, (j + 1) * LANES)
        pre = dot_nn(low[...], wp[1, j // 4, (j // 2) % 2, j % 2, 0:64, :]) + prm[21:22, at]
        delta[:, at] = jnp.maximum(pre, 0.0) + jnp.log1p(jnp.exp(-jnp.abs(pre)))

    gather_z.cross(3)

    def decay(slab, j, a, base):
        return jnp.exp2(spread(slab, j) * a) * wide(rows_of(kb2, base))

    kb2 = kb.reshape(256, LANES)

    def tile16(ref, t):
        return ref[pl.ds(pl.multiple_of(t * 16, 16), 16), :]

    def forward_ends(q):
        ctx, block = q // 2, q % 2
        at = lanes_at(block, WIDE)
        a = a2[:, at]

        def eight(i, h):
            t0 = pl.multiple_of(ctx * ROWS + i * 8, 8)
            d = delta[pl.ds(t0, 8), at]
            u = d * slab_of(sig, t0, at)
            for j in range(8):
                h = decay(d, j, a, t0 + j) * h + spread(u, j) * wide(tile16(bb, t0 + j))
            return h

        h = lax.fori_loop(0, 16, eight, jnp.zeros((16, WIDE), F32))
        rows = pl.ds(pl.multiple_of(ctx * ROWS, ROWS), ROWS)
        summed = jnp.sum(delta[rows, at], axis=0, keepdims=True)
        kept = jnp.min(kb[ctx], axis=0, keepdims=True)
        decays = jnp.exp2(jnp.broadcast_to(summed, (16, WIDE)) * a) * wide(
            jnp.broadcast_to(kept, (16, LANES))
        )
        for g in range(4):
            piece = ctx * GROUPS + block * 4 + g
            hp[piece, 0] = h[:, g * LANES : (g + 1) * LANES]
            hp[piece, 1] = decays[:, g * LANES : (g + 1) * LANES]

    def slab_of(ref, t0, at):
        base = pl.multiple_of((t0 // 16) * 16, 16)
        both = ref[pl.ds(base, 16), at].astype(F32)
        return jnp.where(t0 % 16 == 0, both[:8], both[8:])

    for_each(4, forward_ends)
    send_ends = Transpose(sems, hp, hpr)
    send_ends.start()
    gather_o.relay(0)
    gather_o.relay(1)
    gather_z.done()

    def z_columns(i):
        rows = nrm_rows()
        for half in (0, 1):
            w = wz[half, :, :, :, :, lanes_at(i, 256)].reshape(1024, 256)
            at = pl.ds(pl.multiple_of(half * 512 + i * 256, 256), 256)
            zz[:, at] = dot_nn(rows, w)

    def nrm_rows():
        return jnp.concatenate([nrm[0, 16:144, :], nrm[1, 16:144, :]], axis=0)

    for_each(2, z_columns)
    send_ends.done()
    state = jnp.zeros((16, LANES), F32)
    for s in range(16):
        hret[s] = state
        state = hpr[s, 1] * state + hpr[s, 0]
    return_states = Transpose(sems, hret, hin)
    return_states.start()
    gather_o.cross(0)
    gather_o.cross(1)

    def forward(q):
        ctx, block = q // 2, q % 2
        at = lanes_at(block, WIDE)
        a = a2[:, at]
        h0 = jnp.concatenate([hin[ctx * GROUPS + block * 4 + g] for g in range(4)], axis=1)
        hs[ctx * 129, :, at] = h0

        def eight(i, h):
            t0 = pl.multiple_of(ctx * ROWS + i * 8, 8)
            d = delta[pl.ds(t0, 8), at]
            s8 = slab_of(sig, t0, at)
            u = d * s8
            for j in range(8):
                h = decay(d, j, a, t0 + j) * h + spread(u, j) * wide(tile16(bb, t0 + j))
                hs[t0 + ctx + j + 1, :, at] = h
                put_partial(part1, j, h * wide(tile16(cb, t0 + j)))
            yy[pl.ds(t0, 8), at] = take_partial(part1) + prm[22:23, at] * s8
            return h

        lax.fori_loop(0, 16, eight, h0)

    gbr_copy.wait_recv()

    def branch_back(i):
        branch = gbr[...].reshape(256, 1024)
        w0 = wo[0, i // 2, i % 2].reshape(256, 512)
        w1 = wo[1, i // 2, i % 2].reshape(256, 512)
        gm = dot_nt(branch[:, :512], w0) + dot_nt(branch[:, 512:], w1)
        at = lanes_at(i, 256)
        zv = zz[:, at]
        sigma = jax.nn.sigmoid(zv)
        gs[:, at] = gm * (zv * sigma)
        gz[:, at] = (gm * yy[:, at] * (sigma * (1.0 + zv * (1.0 - sigma)))).astype(BF16)

    def z_grads(i):
        d = pl.ds(pl.multiple_of(i * 128, 128), 128)
        for half in (0, 1):
            got = dot_nn(nrm_t[d, :], gz[:, half * 512 : (half + 1) * 512])
            gz_w[half, i // 2, i % 2] = got.astype(BF16).reshape(2, 64, 512)

    def backward_ends(q):
        ctx, block = q // 2, q % 2
        at = lanes_at(block, WIDE)
        a = a2[:, at]

        def eight(i, adj):
            t0 = pl.multiple_of(ctx * ROWS + (15 - i) * 8, 8)
            d = delta[pl.ds(t0, 8), at]
            u = gs[pl.ds(t0, 8), at]
            for j in range(7, -1, -1):
                adj = decay(d, j, a, t0 + j) * (adj + spread(u, j) * wide(tile16(cb, t0 + j)))
            return adj

        adj = lax.fori_loop(0, 16, eight, jnp.zeros((16, WIDE), F32))
        for g in range(4):
            lp[ctx * GROUPS + block * 4 + g] = adj[:, g * LANES : (g + 1) * LANES]

    return_states.done()
    for_each(4, forward)
    for ctx in (0, 1):
        for g in range(GROUPS):
            at = slice(g * LANES, (g + 1) * LANES)
            rows = slice(ctx * ROWS, (ctx + 1) * ROWS)
            zv = zz[rows, at]
            val = (yy[rows, at] * zv * jax.nn.sigmoid(zv)).astype(BF16)
            mid[rows, at] = val
            mid_t[at, rows] = jnp.transpose(val.astype(F32)).astype(BF16)

    def out_grads(i):
        e = pl.ds(pl.multiple_of(i * 256, 256), 256)
        branch = gbr[...].reshape(256, 1024)
        for half in (0, 1):
            got = dot_nn(mid_t[e, :], branch[:, half * 512 : (half + 1) * 512])
            go_w[half, i // 2, i % 2] = got.astype(BF16).reshape(2, 128, 512)

    for_each(4, out_grads)
    scatter_o = HalfScatter(sems, go_w, o1, o2, o3)
    scatter_o.push1(1)

    for j in (0, 1):
        gather_o.slot_done(j)
        block = half_slot(j)
        branch_back(2 * block)
        branch_back(2 * block + 1)
        backward_ends(block)
        backward_ends(2 + block)
    send_adj = Transpose(sems, lp, lpr)
    send_adj.start()
    for_each(8, z_grads)
    scatter_z = Scatter(sems, gz_w, z1, z2, z3)
    send_adj.done()
    state = jnp.zeros((16, LANES), F32)
    for s in range(15, -1, -1):
        lret[s] = state
        state = hpr[s, 1] * state + lpr[s]
    return_adj = Transpose(sems, lret, lin)
    return_adj.start()
    scatter_o.push1(0)
    scatter_z.push1(2)
    scatter_z.push1(3)
    for half in (0, 1):
        got = dot_nn(mid[...], wo[half].reshape(1024, 512))
        for ctx in (0, 1):
            rowx[ctx, :, half * 512 : (half + 1) * 512] = got[ctx * ROWS : (ctx + 1) * ROWS]
    rows_copy = sems.copy(rowx.at[mate], rowx_in.at[0], mate, seq)
    rows_copy.start()
    return_adj.done()

    sub = lax.broadcasted_iota(jnp.int32, (8, LANES), 0)
    pick_b = [(lane == 64 + 8 * k + sub).astype(F32) for k in (0, 1)]
    pick_c = [(lane == 80 + 8 * k + sub).astype(F32) for k in (0, 1)]
    all_ones = jnp.ones((LANES, LANES), BF16)
    def backward(ctx, block):
        at = slice(block * WIDE, (block + 1) * WIDE)
        a = a2[:, at]

        def eight(i, carry):
            adj, grad_a = carry
            t0 = pl.multiple_of(ctx * ROWS + (15 - i) * 8, 8)
            d = delta[pl.ds(t0, 8), at]
            g8 = gs[pl.ds(t0, 8), at]
            u = d * slab_of(sig, t0, at)
            h_next = hs[t0 + ctx + 8, :, at]
            for j in range(7, -1, -1):
                t = t0 + j
                dj = spread(d, j)
                gj = spread(g8, j)
                lam = adj + gj * wide(tile16(cb, t))
                adj = jnp.exp2(dj * a) * wide(rows_of(kb2, t)) * lam
                h_prev = hs[t + ctx, :, at]
                flow = adj * h_prev
                grad_a = grad_a + flow * dj
                put_partial(part1, j, flow * a)
                put_partial(part2, j, lam * wide(tile16(bb, t)))
                to = pl.ds(pl.multiple_of((t - ctx * ROWS) * 16, 16), 16)
                qb[block, to, :] = fold_lanes(lam * spread(u, j)).astype(BF16)
                qc[block, to, :] = fold_lanes(gj * h_next).astype(BF16)
                h_next = h_prev
            yy[pl.ds(t0, 8), at] = take_partial(part1) * (1.0 / LOG2E)
            zz[pl.ds(t0, 8), at] = take_partial(part2)
            return adj, grad_a

        adj0 = jnp.concatenate([lin[ctx * GROUPS + block * 4 + g] for g in range(4)], axis=1)
        _, grad_a = lax.fori_loop(0, 16, eight, (adj0, jnp.zeros((16, WIDE), F32)))
        hs[ctx * 129, :, at] = grad_a

    def sum_lanes(ctx, i):
        for k in range(2):
            t0 = pl.multiple_of(i * 32 + k * 16, 16)
            at = pl.ds(pl.multiple_of(t0 * 16, 256), 256)
            sum_b = dot_nn(qb[0, at, :], all_ones) + dot_nn(qb[1, at, :], all_ones)
            sum_c = dot_nn(qc[0, at, :], all_ones) + dot_nn(qc[1, at, :], all_ones)
            for j in range(16):
                got = sum_b[16 * j : 16 * j + 8] * pick_b[0]
                got = got + sum_b[16 * j + 8 : 16 * j + 16] * pick_b[1]
                got = got + sum_c[16 * j : 16 * j + 8] * pick_c[0]
                got = got + sum_c[16 * j + 8 : 16 * j + 16] * pick_c[1]
                part3[k * 128 + 8 * j : k * 128 + 8 * j + 8, :] = got
            for j in range(2):
                got = part3[pl.ds(k * 128 + j * 64, 8, stride=8), :]
                for n in range(1, 8):
                    got = got + part3[pl.ds(k * 128 + j * 64 + n, 8, stride=8), :]
                gbc[pl.ds(pl.multiple_of(ctx * ROWS + t0 + 8 * j, 8), 8), :] = got

    backward(0, 0)
    scatter_o.push2(1)
    scatter_z.push1(1)
    backward(0, 1)
    scatter_o.push2(0)
    scatter_z.push1(0)
    for_each(4, functools.partial(sum_lanes, 0))
    backward(1, 0)
    scatter_z.push2(2)
    backward(1, 1)
    scatter_o.push3(1)
    scatter_z.push2(3)
    for_each(4, functools.partial(sum_lanes, 1))

    ones = []
    for j in range(GROUPS):
        at = slice(j * LANES, (j + 1) * LANES)
        sv = sig[:, at].astype(F32)
        g_pre = ((yy[:, at] + zz[:, at] * sv) * (1.0 - jnp.exp(-delta[:, at]))).astype(BF16)
        mid[:, at] = g_pre
        ones.append(jnp.sum(g_pre.astype(F32), axis=0, keepdims=True))
    g_bdt = jnp.concatenate(ones, axis=1)

    total = jnp.zeros((256, 64), F32)
    for j in range(GROUPS):
        total = total + dot_nt(
            mid[:, j * LANES : (j + 1) * LANES], wp[1, j // 4, (j // 2) % 2, j % 2, 0:64, :]
        )
    xd_out[:, 0:64] = total
    xd_out[:, 64:128] = gbc[:, 64:128]
    gd_copy = sems.copy(xd_out, xd_in, mate, seq)
    rows_copy.wait()
    gd_copy.start()
    for g in range(GROUPS):
        at = slice(g * LANES, (g + 1) * LANES)
        o_out[:, at] = (
            hid[:, at].astype(F32) + live * (rowx[c, :, at] + rowx_in[0, :, at])
        ).astype(BF16)
    scatter_z.push2(1)
    gd_copy.wait()
    g_dbl = (xd_out[...] + xd_in[...]).astype(BF16)

    for ctx in (0, 1):
        for j in range(GROUPS):
            at = slice(j * LANES, (j + 1) * LANES)
            rows = slice(ctx * ROWS, (ctx + 1) * ROWS)
            back = dot_nn(g_dbl[rows, 0:96], wp[0, j // 4, (j // 2) % 2, j % 2])
            g_sig = gs[rows, at] * prm[22:23, at] + zz[rows, at] * delta[rows, at] + back
            v = conv_rows(ctx, at)
            sigma = jax.nn.sigmoid(v)
            gext[ctx, 0:128, at] = g_sig * (sigma * (1.0 + v * (1.0 - sigma)))
    edge_copies = [
        sems.copy(gext.at[ctx, pl.ds(0, 8), :], gedge.at[ctx], c, before) for ctx in (0, 1)
    ]
    for copy in edge_copies:
        copy.start()
    scatter_z.push2(0)
    scatter_o.push3(0)

    def small_grads():
        a_rows = -jnp.exp(prm[0:16, :])
        g_alog = (hs[0] + hs[129]) * a_rows
        g_t = jnp.transpose(g_dbl.astype(F32))[0:96].astype(BF16)
        low_t = jnp.transpose(
            jnp.concatenate([low[...].astype(F32), jnp.zeros((256, 64), F32)], axis=1)
        )[0:64].astype(BF16)
        for j in range(GROUPS):
            at = slice(j * LANES, (j + 1) * LANES)
            to = (j // 4, (j // 2) % 2, j % 2)
            sv = sig[:, at].astype(F32)
            gp_w[(0,) + to] = dot_nn(g_t, sig[:, at]).astype(BF16)
            g_dtw = dot_nn(low_t, mid[:, at])
            taps = []
            for k in range(4):
                term = jnp.zeros((1, LANES), F32)
                for ctx in (0, 1):
                    term = term + jnp.sum(
                        gext[ctx, 0:128, at] * xext[ctx, 13 + k : 141 + k, at],
                        axis=0,
                        keepdims=True,
                    )
                taps.append(term)
            bias = jnp.sum(gext[0, 0:128, at] + gext[1, 0:128, at], axis=0, keepdims=True)
            skip = jnp.sum(gs[:, at] * sv, axis=0, keepdims=True)
            rest = jnp.concatenate(
                [g_dtw, g_alog[:, at]]
                + taps
                + [bias, g_bdt[:, at], skip, jnp.zeros((9, LANES), F32)],
                axis=0,
            )
            gp_w[(1,) + to] = rest.astype(BF16)

    small_grads()
    scatter_p = HalfScatter(sems, gp_w, p1, p2, p3)
    scatter_p.all1()

    for copy in edge_copies:
        copy.wait_recv()
    last_chip = (seq < 15).astype(F32)
    for ctx in (0, 1):
        gext[ctx, 128:136, :] = gedge[ctx] * last_chip

    for ctx in (0, 1):

        def x_back(i):
            at = lanes_at(i, LANES)
            total = prm[19:20, at] * gext[ctx, 0:128, at]
            for k in range(3):
                total = total + prm[16 + k : 17 + k, at] * gext[ctx, 3 - k : 131 - k, at]
            mid[ctx * ROWS : (ctx + 1) * ROWS, at] = total.astype(BF16)

        for_each(GROUPS, x_back)

    def x_grads(i):
        d = pl.ds(pl.multiple_of(i * 128, 128), 128)
        for half in (0, 1):
            got = dot_nn(nrm_t[d, :], mid[:, half * 512 : (half + 1) * 512])
            gx_w[half, i // 2, i % 2] = got.astype(BF16).reshape(2, 64, 512)

    scatter_x = Scatter(sems, gx_w, x1, x2, x3)
    for j in scatter_x.order:
        zj = partner(z, j)
        x_grads(2 * zj)
        x_grads(2 * zj + 1)
        scatter_x.push1(j)
        scatter_z.push3(j)
    def normed_back(i):
        total = jnp.zeros((256, 128), F32)
        for half in (0, 1):
            at = slice(half * 512, (half + 1) * 512)
            total = total + dot_nt(mid[:, at], wx[half, i // 2, i % 2].reshape(128, 512))
            total = total + dot_nt(gz[:, at], wz[half, i // 2, i % 2].reshape(128, 512))
        to = lanes_at(i, 128)
        for ctx in (0, 1):
            rowx[ctx, :, to] = total[ctx * ROWS : (ctx + 1) * ROWS]

    for i in range(4):
        normed_back(i)
    scatter_p.all2()
    scatter_x.push2(2)
    for i in range(4, 8):
        normed_back(i)
    back_copy = sems.copy(rowx.at[mate], rowx_in.at[1], mate, seq)
    back_copy.start()
    scatter_x.push2(3)
    scatter_p.all3()
    scatter_x.push2(1)

    def hidden_rows(i):
        at = pl.ds(pl.multiple_of(i * 16, 16), 16)
        rows = hid[at, :].astype(F32)
        r = lax.rsqrt(jnp.mean(rows * rows, axis=1, keepdims=True) + epsilon)
        g_hat = (rowx[c, at, :] + rowx_in[1, at, :]) * gain_row
        inner = jnp.mean(g_hat * rows, axis=1, keepdims=True)
        o_gh[at, :] = r * g_hat - rows * (r * r * r * inner) + out_g[at, :].astype(F32)

    back_copy.wait()
    for_each(8, hidden_rows)
    scatter_x.push3(2)
    scatter_x.push2(0)
    scatter_x.push3(3)
    scatter_x.push3(1)
    scatter_x.push3(0)
    scatter_o.done()
    out_copy = sems.copy(o_gout, o_gout, mate, seq)

    @pl.when(is_active())
    def _():
        for half in (0, 1):
            o_gout[:, half * 512 : (half + 1) * 512] = scatter_o.result(half)
        out_copy.start()

    scatter_z.done()
    for half in (0, 1):
        fin[2 + half] = scatter_z.result(half)
    z_copy = sems.copy(fin.at[pl.ds(2, 2)], fin_in.at[pl.ds(2, 2)], mate, seq)
    z_copy.start()
    scatter_p.done()
    small_copy = sems.copy(fsm, fsm, mate, seq)

    @pl.when(is_active())
    def _():
        for half in (0, 1):
            fsm[half * 96 : (half + 1) * 96, :] = scatter_p.result(half)
        small_copy.start()

    def weight_rows(part, gain_sum):
        for half in (0, 1):
            for core, ref in ((c, fin), (mate, fin_in)):
                at = pl.ds(pl.multiple_of(part * 2048 + core * 1024 + half * 512, 512), 512)
                rows = ref[part * 2 + half]
                o_gin[:, at] = rows
                gain_sum = gain_sum + fold_lanes(rows * in_w[:, at].astype(F32))
        return gain_sum

    z_copy.wait()
    gain_sum = weight_rows(1, jnp.zeros((64, LANES), F32))
    for group in (gather_x, gather_z, gather_o, gather_p, scatter_z, scatter_o):
        group.sent()
    for group in (send_ends, return_states, send_adj, return_adj):
        group.sent()
    for copy in hid_copies + edge_copies + [gbr_copy, gain_all]:
        copy.wait_send()

    scatter_x.done()
    for half in (0, 1):
        fin[half] = scatter_x.result(half)
    x_copy = sems.copy(fin.at[pl.ds(0, 2)], fin_in.at[pl.ds(0, 2)], mate, seq)
    x_copy.start()

    @pl.when(is_active())
    def _():
        out_copy.wait_send()
        small_copy.wait_send()

    @pl.when(is_passive())
    def _():
        out_copy.wait_recv()
        small_copy.wait_recv()

    o_small[...] = fsm[...]
    scatter_x.sent()
    scatter_p.sent()
    x_copy.wait()
    o_gain[...] = weight_rows(0, gain_sum)


def fused_shards(
    hidden,
    out_grad,
    resets,
    valid,
    norm_gain,
    in_weight,
    conv_weight,
    conv_bias,
    x_weight,
    dt_weight,
    dt_bias,
    a_log,
    skip_gain,
    out_weight,
):
    norm_row = norm_gain.astype(F32)
    vectors = jnp.stack(
        [
            conv_bias.astype(F32),
            dt_bias.astype(F32),
            skip_gain.astype(F32),
            jnp.concatenate([norm_row, norm_row]),
        ]
    )
    vmem = pltpu.VMEM
    count = 88
    scratch = [
        vmem((2, 144, 1024), BF16),
        vmem((2, 128, 1024), BF16),
        vmem((2, 128, LANES), F32),
        vmem((16, 8, LANES), F32),
        vmem((2, 144, 1024), BF16),
        vmem((1024, 256), BF16),
        vmem((2, 144, 1024), F32),
        vmem((256, 1024), BF16),
        vmem((256, 1024), F32),
        vmem((256, 1024), F32),
        vmem((256, 1024), F32),
        vmem((256, 1024), F32),
        vmem((4096, LANES), F32),
        vmem((4096, LANES), F32),
        vmem((16, 1024), F32),
        vmem((32, 1024), F32),
        vmem((258, 16, 1024), F32),
        vmem((2, 2048, LANES), BF16),
        vmem((2, 2048, LANES), BF16),
        vmem((256, LANES), F32),
        vmem((256, LANES), F32),
        vmem((256, LANES), F32),
        vmem((256, LANES), F32),
        vmem((256, 64), BF16),
        vmem((256, 1024), BF16),
        vmem((1024, 256), BF16),
        vmem((256, 1024), BF16),
        vmem((2, 4, 2, 2, 64, 512), BF16),
        vmem((2, 4, 2, 2, 64, 512), BF16),
        vmem((2, 2, 2, 2, 128, 512), BF16),
        vmem((2, 2, 2, 2, 96, LANES), BF16),
        vmem((2, 4, 2, 2, 64, 512), BF16),
        vmem((2, 4, 2, 2, 64, 512), BF16),
        vmem((2, 2, 2, 2, 128, 512), BF16),
        vmem((2, 2, 2, 2, 96, LANES), BF16),
    ]
    for z_count, rows, columns in ((4, 64, 512), (4, 64, 512), (2, 128, 512)):
        scratch += [
            vmem((2, z_count, 2, rows, columns), BF16),
            vmem((2, z_count, rows, columns), BF16),
            vmem((3, 2, rows, columns), BF16),
        ]
    scratch += [
        vmem((2, 2, 2, 96, LANES), BF16),
        vmem((2, 2, 96, LANES), BF16),
        vmem((3, 2, 96, LANES), BF16),
        vmem((16, 2, 16, LANES), F32),
        vmem((16, 2, 16, LANES), F32),
        vmem((16, 16, LANES), F32),
        vmem((16, 16, LANES), F32),
        vmem((16, 16, LANES), F32),
        vmem((16, 16, LANES), F32),
        vmem((16, 16, LANES), F32),
        vmem((16, 16, LANES), F32),
        vmem((256, LANES), F32),
        vmem((256, LANES), F32),
        vmem((2, 136, 1024), F32),
        vmem((2, 8, 1024), F32),
        vmem((2, 128, 1024), F32),
        vmem((2, 128, 1024), F32),
        vmem((4, 64, 512), F32),
        vmem((4, 64, 512), F32),
        vmem((192, LANES), F32),
        pltpu.SemaphoreType.DMA((count,)),
        pltpu.SemaphoreType.DMA((count,)),
    ]
    whole = pl.BlockSpec(memory_space=pltpu.VMEM)
    parts = pl.pallas_call(
        fused_kernel,
        out_shape=(
            jax.ShapeDtypeStruct((128, 1024), BF16),
            jax.ShapeDtypeStruct((128, 1024), F32),
            jax.ShapeDtypeStruct((64, 4096), F32),
            jax.ShapeDtypeStruct((128, 1024), F32),
            jax.ShapeDtypeStruct((192, LANES), F32),
            jax.ShapeDtypeStruct((64, LANES), F32),
        ),
        in_specs=[pl.BlockSpec(memory_space=pltpu.SMEM)] + [whole] * 10,
        out_specs=(whole,) * 6,
        scratch_shapes=scratch,
        compiler_params=pltpu.CompilerParams(
            collective_id=0, has_side_effects=True, vmem_limit_bytes=64 * 2**20
        ),
    )(
        valid,
        hidden[0],
        out_grad[0],
        resets,
        in_weight,
        out_weight,
        x_weight.T,
        dt_weight.T,
        a_log.T,
        conv_weight.T,
        vectors,
    )
    got = pl.pallas_call(
        place_outputs,
        out_shape=tuple(
            jax.ShapeDtypeStruct(shape, dtype)
            for shape, dtype in (
                ((128, 1024), BF16),
                ((128, 1024), F32),
                ((1, 64), F32),
                ((64, 4096), F32),
                ((4, LANES), F32),
                ((1, LANES), F32),
                ((96, LANES), F32),
                ((64, LANES), F32),
                ((1, LANES), F32),
                ((16, LANES), F32),
                ((1, LANES), F32),
                ((128, 1024), F32),
            )
        ),
        in_specs=[whole] * 7,
        out_specs=(whole,) * 12,
        compiler_params=pltpu.CompilerParams(vmem_limit_bytes=64 * 2**20),
    )(*parts, vectors)
    return (
        got[0][None],
        got[1][None],
        got[2][0],
        got[3],
        got[4].T,
        got[5][0],
        got[6].T,
        got[7].T,
        got[8][0],
        got[9].T,
        got[10][0],
        got[11],
    )


def place_outputs(
    out,
    g_hidden,
    g_in,
    g_out,
    small,
    gain,
    vectors,
    o_out,
    o_hidden,
    o_gain,
    o_in,
    o_taps,
    o_bias,
    o_xw,
    o_dtw,
    o_dtb,
    o_alog,
    o_skip,
    o_outw,
):
    o_out[...] = out[...]
    o_hidden[...] = g_hidden[...]
    o_in[...] = g_in[...]
    o_outw[...] = g_out[...]
    o_xw[...] = small[0:96, :]
    o_dtw[...] = small[96:160, :]
    o_alog[...] = small[160:176, :]
    o_taps[...] = small[176:180, :]
    o_bias[...] = small[180:181, :]
    o_dtb[...] = small[181:182, :]
    o_skip[...] = small[182:183, :]
    turned = jnp.transpose(jnp.concatenate([gain[...], jnp.zeros((64, LANES), F32)], axis=0))
    o_gain[...] = (jnp.sum(turned, axis=0, keepdims=True) / vectors[3:4, :])[:, 0:64]


def solution(mesh):
    sizes = dict(mesh.shape)
    body = fused_shards if sizes == {"ctx": 2, "seq": 16} else shards
    return jax.shard_map(
        body,
        mesh=mesh,
        in_specs=(
            P("ctx", "seq", None),
            P("ctx", "seq", None),
            P("ctx", "seq"),
            P("ctx"),
            P("seq"),
            P("seq", None),
            P("seq", None),
            P("seq"),
            P("seq", None),
            P("seq", None),
            P("seq"),
            P("seq", None),
            P("seq"),
            P("seq", None),
        ),
        out_specs=(
            P("ctx", "seq", None),
            P("ctx", "seq", None),
            P("seq"),
            P("seq", None),
            P("seq", None),
            P("seq"),
            P("seq", None),
            P("seq", None),
            P("seq"),
            P("seq", None),
            P("seq"),
            P("seq", None),
        ),
        check_vma=False,
    )
```

```python
import functools

import jax
import jax.numpy as jnp
from jax import lax
from jax.experimental import pallas as pl
from jax.experimental.pallas import tpu as pltpu
from jax.sharding import PartitionSpec as P

epsilon = 1e-05
highest = lax.Precision.HIGHEST
contract_last = (((1,), (1,)), ((), ()))
contract_first = (((0,), (0,)), ((), ()))


def passed_along(block, axis, distance):
    devices = range(lax.axis_size(axis))
    route = [(i - distance, i) for i in devices if i - distance in devices]
    return lax.ppermute(block, axis, route)


def entering_2(part, axis, combine, identity, reverse):
    count = lax.axis_size(axis)
    place = lax.axis_index(axis)
    ahead = count - 1 - place if reverse else place
    gathered = jax.tree.map(lambda a: lax.all_gather(a, axis), part)
    state = jax.tree.map(lambda a, e: jnp.zeros_like(a) + jnp.asarray(e, a.dtype), part, identity)

    def one(hop, state):
        source = count - 1 - hop if reverse else hop
        return combine(
            state, jax.tree.map(lambda a: lax.dynamic_index_in_dim(a, source, 0, False), gathered)
        )

    return lax.fori_loop(0, ahead, one, state)


def silu_slope(value):
    sigma = jax.nn.sigmoid(value)
    return sigma * (1.0 + value * (1.0 - sigma))


def combine_pair(earlier, later):
    return (earlier[0] * later[0], later[0] * earlier[1] + later[1])


def decays_of(delta_blk, keep_blk, a_matrix):
    return keep_blk[:, None, None] * jnp.exp(delta_blk[:, :, None] * a_matrix[None])


def shards(
    hidden,
    out_grad,
    resets,
    valid,
    norm_gain,
    in_weight,
    conv_weight,
    conv_bias,
    x_weight,
    dt_weight,
    dt_bias,
    a_log,
    skip_gain,
    out_weight,
):
    gathered = (
        lax.all_gather(norm_gain, "seq", axis=0, tiled=True),
        lax.all_gather(in_weight, "seq", axis=0, tiled=True),
        lax.all_gather(conv_weight, "seq", axis=0, tiled=True),
        lax.all_gather(conv_bias, "seq", axis=0, tiled=True),
        lax.all_gather(x_weight, "seq", axis=0, tiled=True),
        lax.all_gather(dt_weight, "seq", axis=0, tiled=True),
        lax.all_gather(dt_bias, "seq", axis=0, tiled=True),
        lax.all_gather(a_log, "seq", axis=0, tiled=True),
        lax.all_gather(skip_gain, "seq", axis=0, tiled=True),
        lax.all_gather(out_weight, "seq", axis=0, tiled=True),
    )
    gain_full, w_in, w_conv, b_conv, w_x, w_dt, b_dt, a_logs, w_skip, w_out = gathered
    tokens = hidden.shape[1]
    inner = w_out.shape[0]
    rank = w_dt.shape[1]
    state = a_logs.shape[1]
    taps = w_conv.shape[1]
    places = lax.axis_index("seq") * tokens + jnp.arange(tokens, dtype=jnp.int32)
    live_mask = (places < valid[0]).astype(jnp.float32)
    reset_f = resets[0].astype(jnp.float32)
    keep_mask = 1.0 - reset_f
    source = hidden[0].astype(jnp.float32)
    rscale = lax.rsqrt(jnp.mean(source * source, axis=-1, keepdims=True) + epsilon)
    scaled = source * rscale
    gain_f = gain_full.astype(jnp.float32)
    normed = (scaled * gain_f).astype(jnp.bfloat16)
    projected = jnp.dot(normed, w_in, preferred_element_type=jnp.float32)
    x_part = projected[:, :inner].astype(jnp.bfloat16)
    z_part = projected[:, inner:]
    rim_rows = passed_along(x_part[tokens - (taps - 1) :], "seq", 1)
    extended = jnp.concatenate([rim_rows, x_part], 0).astype(jnp.float32)
    conv_taps = w_conv.astype(jnp.float32)
    conv_out = b_conv.astype(jnp.float32) + sum(
        (conv_taps[:, offset] * extended[offset : offset + tokens] for offset in range(taps))
    )
    signal_low = jax.nn.silu(conv_out).astype(jnp.bfloat16)
    signal = signal_low.astype(jnp.float32)
    x_dbl = jnp.dot(signal_low, w_x, preferred_element_type=jnp.float32)
    dt_low = x_dbl[:, :rank].astype(jnp.bfloat16)
    b_input = x_dbl[:, rank : rank + state]
    c_output = x_dbl[:, rank + state :]
    dt_pre = lax.dot_general(
        dt_low, w_dt, contract_last, preferred_element_type=jnp.float32
    ) + b_dt.astype(jnp.float32)
    delta = jax.nn.softplus(dt_pre)
    a_matrix = -jnp.exp(a_logs.astype(jnp.float32))
    drive = delta * signal
    reset_count = jnp.cumsum(reset_f)
    reset_before = reset_count - reset_f
    delta_sum = jnp.cumsum(delta, 0)
    delta_before = delta_sum - delta
    reset_total = reset_count[-1]
    delta_total = delta_sum[-1]
    alive_upto = (reset_count == 0.0).astype(jnp.float32)
    alive_before = (reset_before == 0.0).astype(jnp.float32)
    alive_after = (reset_total - reset_count == 0.0).astype(jnp.float32)
    span_len = min(64, tokens)
    n_blocks = tokens // span_len
    roll_by = min(16, span_len)

    def split_blocks(value):
        return value.reshape((n_blocks, span_len) + value.shape[1:])

    delta_b = split_blocks(delta)
    drive_b = split_blocks(drive)
    binput_b = split_blocks(b_input)
    coutput_b = split_blocks(c_output)
    keep_b = split_blocks(keep_mask)
    dsum_b = split_blocks(delta_sum)
    upto_b = split_blocks(alive_upto)
    after_b = split_blocks(alive_after)
    ones_state = jnp.ones((inner, state), jnp.float32)
    zero_state = jnp.zeros((inner, state), jnp.float32)
    group_prod = (reset_total == 0.0).astype(jnp.float32) * jnp.exp(delta_total[:, None] * a_matrix)

    def forward_step(state_now, blk):
        delta_blk, drive_blk, binput_blk, coutput_blk, keep_blk = blk
        decays = decays_of(delta_blk, keep_blk, a_matrix)

        def token_step(state_tok, item):
            decay_now, drive_now, binput_now, coutput_now = item
            state_next = decay_now * state_tok + drive_now[:, None] * binput_now[None, :]
            return (state_next, jnp.sum(state_next * coutput_now[None, :], -1))

        state_end, outputs = lax.scan(
            token_step, state_now, (decays, drive_blk, binput_blk, coutput_blk), unroll=roll_by
        )
        return (state_end, (state_now, outputs))

    group_state, (local_starts, scan_local) = lax.scan(
        forward_step, zero_state, (delta_b, drive_b, binput_b, coutput_b, keep_b)
    )
    entering = entering_2(
        (group_prod, group_state), "seq", combine_pair, (ones_state, zero_state), False
    )
    state_in = entering[1]

    def lift_block(blk):
        dsum_blk, upto_blk, coutput_blk = blk
        lifted = (
            upto_blk[:, None, None]
            * jnp.exp(dsum_blk[:, :, None] * a_matrix[None])
            * state_in[None]
        )
        return jnp.sum(lifted * coutput_blk[:, None, :], -1)

    lifted_out = lax.map(lift_block, (dsum_b, upto_b, coutput_b))
    scanned = (scan_local + lifted_out).reshape(tokens, inner) + w_skip.astype(jnp.float32) * signal
    gate_act = jax.nn.silu(z_part)
    mixed = (scanned * gate_act).astype(jnp.bfloat16)
    branch = jnp.dot(mixed, w_out, preferred_element_type=jnp.float32)
    result = (source + live_mask[:, None] * branch).astype(jnp.bfloat16)
    regathered = (
        lax.all_gather(norm_gain, "seq", axis=0, tiled=True),
        lax.all_gather(in_weight, "seq", axis=0, tiled=True),
        lax.all_gather(conv_weight, "seq", axis=0, tiled=True),
        lax.all_gather(conv_bias, "seq", axis=0, tiled=True),
        lax.all_gather(x_weight, "seq", axis=0, tiled=True),
        lax.all_gather(dt_weight, "seq", axis=0, tiled=True),
        lax.all_gather(dt_bias, "seq", axis=0, tiled=True),
        lax.all_gather(a_log, "seq", axis=0, tiled=True),
        lax.all_gather(skip_gain, "seq", axis=0, tiled=True),
        lax.all_gather(out_weight, "seq", axis=0, tiled=True),
    )
    gain_full, w_in, w_conv, b_conv, w_x, w_dt, b_dt, a_logs, w_skip, w_out = regathered
    gain_f = gain_full.astype(jnp.float32)
    conv_taps = w_conv.astype(jnp.float32)
    a_matrix = -jnp.exp(a_logs.astype(jnp.float32))
    cotangent = out_grad[0].astype(jnp.float32)
    g_branch = (live_mask[:, None] * cotangent).astype(jnp.bfloat16)
    g_mixed = lax.dot_general(g_branch, w_out, contract_last, preferred_element_type=jnp.float32)
    g_scan = g_mixed * gate_act
    g_zpart = g_mixed * scanned * silu_slope(z_part)
    g_skip_full = jnp.sum(g_scan * signal, 0)
    gscan_b = split_blocks(g_scan)

    def push_block(total, blk):
        dsum_blk, upto_blk, coutput_blk, gscan_blk = blk
        weight_blk = upto_blk[:, None, None] * jnp.exp(dsum_blk[:, :, None] * a_matrix[None])
        return (
            total + jnp.sum(weight_blk * gscan_blk[:, :, None] * coutput_blk[:, None, :], 0),
            None,
        )

    passed_local, _ = lax.scan(push_block, zero_state, (dsum_b, upto_b, coutput_b, gscan_b))
    leaving = entering_2(
        (group_prod, passed_local), "seq", combine_pair, (ones_state, zero_state), True
    )
    passed_in = leaving[1]
    start_rows = jnp.arange(n_blocks) * span_len
    start_alive = alive_before[start_rows]
    start_delta = delta_before[start_rows]
    block_starts = (
        local_starts
        + start_alive[:, None, None]
        * jnp.exp(start_delta[:, :, None] * a_matrix[None])
        * state_in[None]
    )

    def backward_step(carried, blk):
        passed, grad_amat = carried
        (
            start_state,
            delta_blk,
            drive_blk,
            binput_blk,
            coutput_blk,
            gscan_blk,
            keep_blk,
            dsum_blk,
            after_blk,
        ) = blk
        decays = decays_of(delta_blk, keep_blk, a_matrix)

        def ahead_step(state_tok, item):
            decay_now, drive_now, binput_now = item
            state_next = decay_now * state_tok + drive_now[:, None] * binput_now[None, :]
            return (state_next, state_next)

        _, states_blk = lax.scan(
            ahead_step, start_state, (decays, drive_blk, binput_blk), unroll=roll_by
        )
        before = jnp.concatenate([start_state[None], states_blk[:-1]], 0)

        def behind_step(passed_tok, item):
            decay_now, coutput_now, gscan_now = item
            adjoint = gscan_now[:, None] * coutput_now[None, :] + passed_tok
            return (decay_now * adjoint, adjoint)

        passed, adjoints_local = lax.scan(
            behind_step, passed, (decays, coutput_blk, gscan_blk), reverse=True, unroll=roll_by
        )
        reach = after_blk[:, None, None] * jnp.exp(
            (delta_total[None] - dsum_blk)[:, :, None] * a_matrix[None]
        )
        adjoints = adjoints_local + reach * passed_in[None]
        flow = adjoints * before * decays
        g_delta_decay = jnp.sum(flow * a_matrix[None], -1)
        grad_amat = grad_amat + jnp.sum(flow * delta_blk[:, :, None], 0)
        g_drive = jnp.einsum("qen,qn->qe", adjoints, binput_blk, precision=highest)
        g_binput = jnp.einsum("qen,qe->qn", adjoints, drive_blk, precision=highest)
        g_coutput = jnp.einsum("qen,qe->qn", states_blk, gscan_blk, precision=highest)
        return ((passed, grad_amat), (g_delta_decay, g_drive, g_binput, g_coutput))

    (_, grad_amat), pieces = lax.scan(
        backward_step,
        (zero_state, zero_state),
        (block_starts, delta_b, drive_b, binput_b, coutput_b, gscan_b, keep_b, dsum_b, after_b),
        reverse=True,
    )
    g_delta_decay = pieces[0].reshape(tokens, inner)
    g_drive = pieces[1].reshape(tokens, inner)
    g_binput = pieces[2].reshape(tokens, state)
    g_coutput = pieces[3].reshape(tokens, state)
    g_delta = g_delta_decay + g_drive * signal
    g_pre = (g_delta * jax.nn.sigmoid(dt_pre)).astype(jnp.bfloat16)
    g_dtlow = jnp.dot(g_pre, w_dt, preferred_element_type=jnp.float32)
    g_xdbl = jnp.concatenate([g_dtlow, g_binput, g_coutput], 1).astype(jnp.bfloat16)
    g_signal = (
        g_scan * w_skip.astype(jnp.float32)
        + g_drive * delta
        + lax.dot_general(g_xdbl, w_x, contract_last, preferred_element_type=jnp.float32)
    )
    g_conv = g_signal * silu_slope(conv_out)
    g_extended = sum(
        (
            jnp.pad(conv_taps[:, offset] * g_conv, ((offset, taps - 1 - offset), (0, 0)))
            for offset in range(taps)
        )
    )
    returned = passed_along(g_extended[: taps - 1], "seq", -1)
    g_xpart = g_extended[taps - 1 :] + jnp.pad(returned, ((tokens - (taps - 1), 0), (0, 0)))
    g_proj = jnp.concatenate([g_xpart, g_zpart], 1).astype(jnp.bfloat16)
    g_normed = lax.dot_general(g_proj, w_in, contract_last, preferred_element_type=jnp.float32)
    g_hat = g_normed * gain_f
    grad_source = (
        rscale * g_hat
        - source * rscale * rscale * rscale * jnp.mean(g_hat * source, axis=-1, keepdims=True)
        + cotangent
    )
    g_gain = jnp.sum(g_normed * scaled, 0)
    g_wconv = jnp.stack(
        [jnp.sum(g_conv * extended[offset : offset + tokens], 0) for offset in range(taps)], 1
    )
    g_bconv = jnp.sum(g_conv, 0)
    g_bdt = jnp.sum(g_pre.astype(jnp.float32), 0)
    g_alog = grad_amat * a_matrix
    weight_rows = lax.dot_general(
        normed, g_proj, contract_first, preferred_element_type=jnp.float32
    )
    g_win_rows, g_gain_rows = lax.psum_scatter(
        (weight_rows, g_gain), "seq", scatter_dimension=0, tiled=True
    )
    xw_rows = lax.dot_general(
        signal_low, g_xdbl, contract_first, preferred_element_type=jnp.float32
    )
    dtw_rows = lax.dot_general(g_pre, dt_low, contract_first, preferred_element_type=jnp.float32)
    outw_rows = lax.dot_general(mixed, g_branch, contract_first, preferred_element_type=jnp.float32)
    (
        g_wconv_rows,
        g_bconv_rows,
        g_wx_rows,
        g_wdt_rows,
        g_bdt_rows,
        g_alog_rows,
        g_skip_rows,
        g_wout_rows,
    ) = lax.psum_scatter(
        (g_wconv, g_bconv, xw_rows, dtw_rows, g_bdt, g_alog, g_skip_full, outw_rows),
        "seq",
        scatter_dimension=0,
        tiled=True,
    )
    totals = lax.psum(
        (
            g_gain_rows,
            g_win_rows,
            g_wconv_rows,
            g_bconv_rows,
            g_wx_rows,
            g_wdt_rows,
            g_bdt_rows,
            g_alog_rows,
            g_skip_rows,
            g_wout_rows,
        ),
        "ctx",
    )
    return (
        result[None],
        grad_source[None],
        totals[0],
        totals[1],
        totals[2],
        totals[3],
        totals[4],
        totals[5],
        totals[6],
        totals[7],
        totals[8],
        totals[9],
    )


MESH = pl.DeviceIdType.MESH
F32 = jnp.float32
BF16 = jnp.bfloat16
ROWS = 128
GROUPS = 8
LANES = 128
WIDE = 512
LOG2E = 1.4426950408889634


def place():
    seq = lax.axis_index("seq")
    return lax.axis_index("ctx"), seq, seq // 4, (seq // 2) % 2, seq % 2


def chip(z, y, x):
    return z * 4 + y * 2 + x


class Semaphores:
    def __init__(self, send, receive):
        self.send, self.receive = send, receive
        self.sends = self.receives = 0

    def new_send(self):
        self.sends += 1
        return self.send.at[self.sends - 1]

    def new_receive(self):
        self.receives += 1
        return self.receive.at[self.receives - 1]

    def copy(self, source, target, core, seq, send=None, receive=None):
        return pltpu.make_async_remote_copy(
            src_ref=source,
            dst_ref=target,
            send_sem=self.new_send() if send is None else send,
            recv_sem=self.new_receive() if receive is None else receive,
            device_id=(core, seq),
            device_id_type=MESH,
        )


def joint(region, copy_sems):
    c, _, z, y, x = place()
    send, receive = copy_sems
    return pltpu.make_async_remote_copy(
        src_ref=region,
        dst_ref=region,
        send_sem=send,
        recv_sem=receive,
        device_id=(c, chip(z, y, 1 - x)),
        device_id_type=MESH,
    )


def partner(z, j):
    return (z, z + 1 - 2 * (z % 2), (z + 2) % 4, 3 - z)[j]


class Gather:
    slots = 4

    def __init__(self, sems, buf, rows):
        c, _, z, y, x = place()
        rows = pl.ds(0, rows)
        own = self.slot(0)
        self.first = [
            sems.copy(buf.at[:, own, y, x, rows], buf.at[:, own, y, x, rows], c, chip(partner(z, j), y, x))
            for j in (1, 2, 3)
        ]
        send2, send3 = sems.new_send(), sems.new_send()
        self.second, self.second_all, self.third, self.third_all = [], [], [], []
        for j in range(self.slots):
            s = self.slot(j)
            got = sems.new_receive()
            self.second.append(
                [
                    sems.copy(buf.at[0, s, y, x, rows], buf.at[0, s, y, x, rows], c, chip(z, 1 - y, x), send2, got),
                    sems.copy(buf.at[1, s, y, x, rows], buf.at[1, s, y, x, rows], c, chip(z, y, 1 - x), send2, got),
                ]
            )
            self.second_all.append(joint(buf.at[:, s, y, x, rows], (send2, got)))
            got = sems.new_receive()
            self.third.append(
                [
                    sems.copy(buf.at[0, s, :, x, rows], buf.at[0, s, :, x, rows], c, chip(z, y, 1 - x), send3, got),
                    sems.copy(buf.at[1, s, y, :, rows], buf.at[1, s, y, :, rows], c, chip(z, 1 - y, x), send3, got),
                ]
            )
            self.third_all.append(joint(buf.at[:, s, :, x, rows], (send3, got)))
        self.second_sent = joint(buf.at[:, :, y, x, rows], (send2, got))
        self.third_sent = joint(buf.at[:, :, :, x, rows], (send3, got))

    def slot(self, j):
        return partner(place()[2], j)

    def start(self):
        for copy in self.first:
            copy.start()

    def arrived(self, j):
        if j > 0:
            self.first[j - 1].wait_recv()

    def relay(self, j):
        self.arrived(j)
        for copy in self.second[j]:
            copy.start()

    def cross(self, j):
        self.second_all[j].wait_recv()
        for copy in self.third[j]:
            copy.start()

    def slot_done(self, j):
        self.third_all[j].wait_recv()

    def done(self):
        for j in range(self.slots):
            self.slot_done(j)

    def sent(self):
        for copy in self.first:
            copy.wait_send()
        self.sent_rest()

    def sent_rest(self):
        self.second_sent.wait_send()
        self.third_sent.wait_send()


def is_active():
    c, _, z, _, _ = place()
    return z // 2 == c


def is_passive():
    return jnp.logical_not(is_active())


def half_slot(j):
    z = place()[2]
    return z % 2 if j == 0 else 1 - z % 2


class HalfGather(Gather):
    slots = 2

    def slot(self, j):
        return half_slot(j)

    def start(self):
        @pl.when(is_active())
        def _():
            for copy in self.first:
                copy.start()

    def arrived(self, j):
        if j == 1:

            @pl.when(is_active())
            def _():
                self.first[0].wait_recv()

        @pl.when(is_passive())
        def _():
            self.first[1 + j].wait_recv()

    def sent(self):
        @pl.when(is_active())
        def _():
            for copy in self.first:
                copy.wait_send()

        self.sent_rest()


def add_into(total, part):
    total[...] = total[...] + part[...]


class Scatter:
    order = (2, 3, 1, 0)

    def __init__(self, sems, grad, came1, came2, came3, rows):
        c, _, z, y, x = place()
        rows = self.rows = pl.ds(0, rows)
        self.grad, self.came1, self.came2, self.came3 = grad, came1, came2, came3
        send1, send2 = sems.new_send(), sems.new_send()
        self.first, self.first_all, self.second, self.second_all = [], [], [], []
        for j in range(len(self.order)):
            s = self.slot(j)
            got = sems.new_receive()
            self.first.append(
                [
                    sems.copy(grad.at[0, s, :, 1 - x, rows], came1.at[0, s], c, chip(z, y, 1 - x), send1, got),
                    sems.copy(grad.at[1, s, 1 - y, :, rows], came1.at[1, s], c, chip(z, 1 - y, x), send1, got),
                ]
            )
            self.first_all.append(joint(came1.at[:, s], (send1, got)))
            got = sems.new_receive()
            self.second.append(
                [
                    sems.copy(grad.at[0, s, 1 - y, x, rows], came2.at[0, s], c, chip(z, 1 - y, x), send2, got),
                    sems.copy(grad.at[1, s, y, 1 - x, rows], came2.at[1, s], c, chip(z, y, 1 - x), send2, got),
                ]
            )
            self.second_all.append(joint(came2.at[:, s], (send2, got)))
        self.first_sent = joint(came1, (send1, got))
        self.second_sent = joint(came2, (send2, got))
        got = sems.new_receive()
        self.third = [
            sems.copy(
                grad.at[:, self.slot(self.third_slot(j)), y, x, rows],
                came3.at[j - 1],
                c,
                chip(partner(z, j), y, x),
                None,
                got,
            )
            for j in (1, 2, 3)
        ]
        self.third_all = joint(came3, (send2, got))

    def slot(self, j):
        return partner(place()[2], j)

    def third_slot(self, j):
        return j

    def push1(self, j):
        for copy in self.first[j]:
            copy.start()

    def push2(self, j):
        _, _, _, y, x = place()
        s = self.slot(j)
        self.first_all[j].wait_recv()
        add_into(self.grad.at[0, s, 1 - y, x, self.rows], self.came1.at[0, s, 1 - y])
        self.second[j][0].start()
        add_into(self.grad.at[1, s, y, 1 - x, self.rows], self.came1.at[1, s, 1 - x])
        self.second[j][1].start()
        add_into(self.grad.at[0, s, y, x, self.rows], self.came1.at[0, s, y])
        add_into(self.grad.at[1, s, y, x, self.rows], self.came1.at[1, s, x])

    def push3(self, j):
        _, _, _, y, x = place()
        s = self.slot(j)
        self.second_all[j].wait_recv()
        for half in (0, 1):
            add_into(self.grad.at[half, s, y, x, self.rows], self.came2.at[half, s])
        self.send_on(j)

    def send_on(self, j):
        if j > 0:
            self.third[j - 1].start()

    def all1(self):
        for j in self.order:
            self.push1(j)

    def all2(self):
        for j in self.order:
            self.push2(j)

    def all3(self):
        for j in self.order:
            self.push3(j)

    def done(self):
        self.third_all.wait_recv()

    def sent(self):
        for copy in self.third:
            copy.wait_send()
        self.sent_rest()

    def sent_rest(self):
        self.first_sent.wait_send()
        self.second_sent.wait_send()

    def result(self, half):
        _, _, _, y, x = place()
        total = self.grad[half, self.slot(0), y, x, self.rows].astype(F32)
        for k in range(3):
            total = total + self.came3[k, half].astype(F32)
        return total


class HalfScatter(Scatter):
    order = (1, 0)

    def slot(self, j):
        return half_slot(j)

    def third_slot(self, j):
        return j % 2

    def send_on(self, j):
        if j == 1:

            @pl.when(is_active())
            def _():
                self.third[0].start()

        @pl.when(is_passive())
        def _():
            self.third[1 + j].start()

    def done(self):
        @pl.when(is_active())
        def _():
            self.third_all.wait_recv()

    def sent(self):
        @pl.when(is_active())
        def _():
            self.third[0].wait_send()

        @pl.when(is_passive())
        def _():
            self.third[1].wait_send()
            self.third[2].wait_send()

        self.sent_rest()


class AcrossGather:
    def __init__(self, sems, buf, first, count):
        c, _, z, y, x = place()
        rows = pl.ds(first, count)
        self.first = sems.copy(
            buf.at[:, z, y, x, rows], buf.at[:, z, y, x, rows], c, chip(z, y, 1 - x)
        )
        self.second = sems.copy(
            buf.at[:, z, y, :, rows], buf.at[:, z, y, :, rows], c, chip(z, 1 - y, x)
        )
        self.third = [
            sems.copy(
                buf.at[:, z, :, :, rows], buf.at[:, z, :, :, rows], c, chip(partner(z, j), y, x)
            )
            for j in (1, 2, 3)
        ]

    def start(self):
        self.first.start()

    def relay(self):
        self.first.wait_recv()
        self.second.start()

    def cross(self):
        self.second.wait_recv()
        for copy in self.third:
            copy.start()

    def done(self):
        for copy in self.third:
            copy.wait_recv()

    def sent(self):
        for copy in [self.first, self.second] + self.third:
            copy.wait_send()


class AcrossScatter:
    def __init__(self, sems, grad, came1, came2, came3, first, count):
        c, _, z, y, x = place()
        rows = self.rows = pl.ds(first, count)
        self.grad, self.came1, self.came2, self.came3 = grad, came1, came2, came3
        got = sems.new_receive()
        self.first = [
            sems.copy(
                grad.at[:, partner(z, j), :, :, rows],
                came1.at[j - 1],
                c,
                chip(partner(z, j), y, x),
                None,
                got,
            )
            for j in (1, 2, 3)
        ]
        self.first_all = joint(came1, (sems.new_send(), got))
        self.second = sems.copy(grad.at[:, z, 1 - y, :, rows], came2, c, chip(z, 1 - y, x))
        self.third = sems.copy(grad.at[:, z, y, 1 - x, rows], came3, c, chip(z, y, 1 - x))

    def push1(self):
        for copy in self.first:
            copy.start()

    def push2(self):
        _, _, z, y, _ = place()
        self.first_all.wait_recv()
        for row in (1 - y, y):
            for half in (0, 1):
                total = self.grad[half, z, row, :, self.rows].astype(F32)
                for k in range(3):
                    total = total + self.came1[k, half, row].astype(F32)
                self.grad[half, z, row, :, self.rows] = total.astype(BF16)
        self.second.start()

    def push3(self):
        _, _, z, y, _ = place()
        self.second.wait_recv()
        for half in (0, 1):
            add_into(self.grad.at[half, z, y, :, self.rows], self.came2.at[half])
        self.third.start()

    def done(self):
        self.third.wait_recv()

    def result(self, half):
        _, _, z, y, x = place()
        return self.grad[half, z, y, x, self.rows].astype(F32) + self.came3[half].astype(F32)

    def sent(self):
        for copy in self.first + [self.second, self.third]:
            copy.wait_send()


class Transpose:
    def __init__(self, sems, source, target):
        c, seq, _, _, _ = place()
        self.source, self.target = source, target
        pair = (sems.new_send(), sems.new_receive())
        self.copies = [
            sems.copy(source.at[(seq + k) % 16], target.at[seq], c, (seq + k) % 16, *pair)
            for k in range(1, 16)
        ]
        self.all = joint(target.at[pl.ds(0, 15)], pair)

    def start(self):
        _, seq, _, _, _ = place()
        for copy in self.copies:
            copy.start()
        self.target[seq] = self.source[seq]

    def done(self):
        self.all.wait_recv()

    def sent(self):
        self.all.wait_send()


def wide(tile, count=WIDE // LANES):
    return jnp.concatenate([tile] * count, axis=1)


def rows_of(ref, base):
    return jnp.broadcast_to(ref[pl.ds(base, 1), :], (16, LANES))


def spread(slab, j):
    return jnp.broadcast_to(slab[j : j + 1, :], (16, slab.shape[1]))


def put_partial(ref, j, value):
    folded = value[:8] + value[8:]
    for g in range(WIDE // LANES):
        ref[pl.ds(g * 64 + 8 * j, 8), :] = folded[:, g * LANES : (g + 1) * LANES]


def take_partial(ref):
    out = []
    for g in range(WIDE // LANES):
        total = ref[pl.ds(g * 64, 8, stride=8), :]
        for j in range(1, 8):
            total = total + ref[pl.ds(g * 64 + j, 8, stride=8), :]
        out.append(total)
    return jnp.concatenate(out, axis=1)


def fold_lanes(value):
    total = value[:, :LANES]
    for g in range(1, value.shape[1] // LANES):
        total = total + value[:, g * LANES : (g + 1) * LANES]
    return total


def dot_nn(a, b):
    return jnp.dot(a, b, preferred_element_type=F32)


def dot_nt(a, b):
    return lax.dot_general(a, b, contract_last, preferred_element_type=F32)


def dot_tn(a, b):
    return lax.dot_general(a, b, contract_first, preferred_element_type=F32)


def for_each(count, body):
    def step(i, carry):
        body(i)
        return carry

    lax.fori_loop(0, count, step, 0)


def lanes_at(i, width):
    return pl.ds(pl.multiple_of(i * width, width), width)


def fused_kernel(
    valid,
    hid_hbm,
    out_g_hbm,
    resets,
    in_w_hbm,
    out_w_hbm,
    x_w,
    dt_w,
    a_log,
    conv_w,
    vectors,
    o_out,
    o_gh,
    o_gin,
    o_gout,
    o_small,
    o_gain,
    hidb,
    gbr,
    kb,
    gain_b,
    nrm,
    nrm_t,
    xext,
    sig,
    delta,
    zz,
    gs,
    yy,
    bb,
    cb,
    a2,
    prm,
    hs,
    qb,
    qc,
    part1,
    part2,
    part3,
    gbc,
    low,
    mid,
    mid_t,
    gz,
    wx,
    wz,
    wo,
    wp,
    gx_w,
    gz_w,
    go_w,
    gp_w,
    x1,
    x2,
    x3,
    z1,
    z2,
    z3,
    o1,
    o2,
    o3,
    p1,
    p2,
    p3,
    c1,
    c2,
    c3,
    hp,
    hpr,
    hret,
    hin,
    lret,
    lin,
    lp,
    lpr,
    xd_out,
    xd_in,
    gext,
    gedge,
    rowx,
    rowx_in,
    fin,
    fin_in,
    fsm,
    in_w,
    out_g,
    load_sems,
    send_sems,
    recv_sems,
):
    c, seq, z, y, x = place()
    mate = 1 - c
    after = (seq + 1) % 16
    before = (seq + 15) % 16
    sems = Semaphores(send_sems, recv_sems)

    barrier = pltpu.get_barrier_semaphore()
    for k in range(1, 16):
        pl.semaphore_signal(
            barrier, inc=1, device_id=(c, (seq + k) % 16), device_id_type=MESH
        )
    pl.semaphore_signal(barrier, inc=1, device_id=(mate, seq), device_id_type=MESH)
    pl.semaphore_signal(barrier, inc=1, device_id=(mate, after), device_id_type=MESH)
    pl.semaphore_signal(barrier, inc=1, device_id=(mate, before), device_id_type=MESH)

    hid = hidb.at[c, pl.ds(16, ROWS), :]
    loads = [
        pltpu.make_async_copy(hid_hbm, hid, load_sems.at[0]),
        pltpu.make_async_copy(out_g_hbm, out_g, load_sems.at[1]),
    ]
    for half in (0, 1):
        for part, ref in ((0, wx), (1, wz)):
            at = pl.ds(pl.multiple_of(part * 2048 + c * 1024 + half * 512, 512), 512)
            loads.append(
                pltpu.make_async_copy(
                    in_w_hbm.at[:, at], ref.at[half, z, y, x], load_sems.at[2 + 2 * half + part]
                )
            )
    out_loads = [
        pltpu.make_async_copy(
            out_w_hbm.at[:, pl.ds(half * 512, 512)],
            wo.at[half, z % 2, y, x],
            load_sems.at[6 + half],
        )
        for half in (0, 1)
    ]
    in_load = pltpu.make_async_copy(in_w_hbm, in_w, load_sems.at[8])
    for load in loads:
        load.start()

    @pl.when(is_active())
    def _():
        for load in out_loads:
            load.start()

    in_load.start()

    @pl.when(z // 2 == c)
    def _():
        wp[0, z % 2, y, x] = x_w[...]
        wp[1, z % 2, y, x, 0:64, :] = dt_w[...]
        wp[1, z % 2, y, x, 64:80, :] = a_log[...]
        wp[1, z % 2, y, x, 80:96, :] = jnp.concatenate(
            [conv_w[...].astype(F32), vectors[0:3, :], jnp.zeros((9, LANES), F32)], axis=0
        ).astype(BF16)

    lane = lax.broadcasted_iota(jnp.int32, (8, LANES), 1)
    gain_mine = jnp.where(lane // 64 == x, jnp.broadcast_to(vectors[3:4, :], (8, LANES)), 0.0)
    gain_b[seq] = gain_mine
    kb[c] = jnp.transpose(
        jnp.broadcast_to(1.0 - resets[...].astype(F32), (ROWS, LANES))
    )
    row_place = seq * ROWS + lax.broadcasted_iota(jnp.int32, (ROWS, LANES), 0)
    live = (row_place < valid[0]).astype(F32)
    loads[1].wait()
    for g in range(GROUPS):
        at = slice(g * LANES, (g + 1) * LANES)
        gbr[c, :, at] = (live * out_g[:, at].astype(F32)).astype(BF16)

    loads[0].wait()
    for load in loads[2:]:
        load.wait()

    @pl.when(is_active())
    def _():
        for load in out_loads:
            load.wait()

    in_load.wait()
    pl.semaphore_wait(barrier, 18)

    gather_x = Gather(sems, wx, 64)
    gather_z = Gather(sems, wz, 48)
    across_z = AcrossGather(sems, wz, 48, 16)
    gather_o = HalfGather(sems, wo, 128)
    gather_p = HalfGather(sems, wp, 96)
    gain_sems = (sems.new_send(), sems.new_receive())
    gain_copies = [
        sems.copy(gain_b.at[seq], gain_b.at[seq], c, (seq + k) % 16, *gain_sems)
        for k in range(1, 16)
    ]
    gain_all = joint(gain_b.at[pl.ds(0, 15)], gain_sems)
    hid_copies = [
        sems.copy(hidb.at[c, pl.ds(16, ROWS), :], hidb.at[c, pl.ds(16, ROWS), :], mate, seq),
        sems.copy(hidb.at[c, pl.ds(128, 16), :], hidb.at[c, pl.ds(0, 16), :], c, after),
        sems.copy(hidb.at[c, pl.ds(128, 16), :], hidb.at[c, pl.ds(0, 16), :], mate, after),
        sems.copy(kb.at[c], kb.at[c], mate, seq),
    ]
    gbr_copy = sems.copy(gbr.at[c], gbr.at[c], mate, seq)
    for copy in hid_copies:
        copy.start()
    for copy in gain_copies:
        copy.start()
    across_z.start()
    gather_p.start()
    gather_x.start()
    gather_x.relay(0)

    for copy in hid_copies:
        copy.wait_recv()
    gather_p.relay(0)
    gather_p.relay(1)
    gain_all.wait_recv()
    gain_row = jnp.concatenate(
        [gain_b[2 * g][0:1, :] + gain_b[2 * g + 1][0:1, :] for g in range(GROUPS)], axis=1
    )
    for ctx in (0, 1):

        def norm_rows(i):
            at = pl.ds(pl.multiple_of(i * 16, 16), 16)
            rows = hidb[ctx, at, :].astype(F32)
            r = lax.rsqrt(jnp.mean(rows * rows, axis=1, keepdims=True) + epsilon)
            nrm[ctx, at, :] = (rows * r * gain_row).astype(BF16)

        for_each(9, norm_rows)
    gather_p.cross(0)
    gather_p.cross(1)
    gather_z.start()
    across_z.relay()
    for ctx in (0, 1):
        for g in range(GROUPS):
            at = slice(g * LANES, (g + 1) * LANES)
            nrm_t[at, ctx * ROWS : (ctx + 1) * ROWS] = jnp.transpose(
                nrm[ctx, 16:144, at].astype(F32)
            ).astype(BF16)

    gather_x.relay(1)
    gather_x.cross(0)
    gather_x.relay(2)
    gather_x.cross(1)
    gather_x.relay(3)
    gather_o.start()
    across_z.cross()
    gather_x.cross(2)
    gather_x.cross(3)
    gbr_copy.start()
    gather_z.relay(0)
    gather_x.done()
    gather_z.relay(1)
    gather_z.cross(0)
    first_chip = (seq > 0).astype(F32)
    for half in (0, 1):

        def x_columns(i):
            rows = nrm[...].reshape(288, 1024)
            w = wx[half, :, :, :, :, lanes_at(i, 256)].reshape(1024, 256)
            got = dot_nn(rows, w).astype(BF16).astype(F32)
            at = pl.ds(pl.multiple_of(half * 512 + i * 256, 256), 256)
            for ctx in (0, 1):
                xext[ctx, 0:16, at] = got[ctx * 144 : ctx * 144 + 16] * first_chip
                xext[ctx, 16:144, at] = got[ctx * 144 + 16 : ctx * 144 + 144]

        for_each(2, x_columns)

    gather_z.relay(2)
    gather_z.cross(1)
    gather_p.done()
    for j in range(GROUPS):
        prm[:, j * LANES : (j + 1) * LANES] = wp[
            1, j // 4, (j // 2) % 2, j % 2, 64:96, :
        ].astype(F32)
    a2[...] = -jnp.exp(prm[0:16, :]) * LOG2E

    def conv_rows(ctx, at):
        total = prm[20:21, at] + prm[16:17, at] * xext[ctx, 13:141, at]
        for k in range(1, 4):
            total = total + prm[16 + k : 17 + k, at] * xext[ctx, 13 + k : 141 + k, at]
        return total

    for ctx in (0, 1):

        def conv_columns(i):
            at = lanes_at(i, LANES)
            total = conv_rows(ctx, at)
            rows = slice(ctx * ROWS, (ctx + 1) * ROWS)
            sig[rows, at] = (total * jax.nn.sigmoid(total)).astype(BF16)

        for_each(GROUPS, conv_columns)

    total = jnp.zeros((256, 96), F32)
    for j in range(GROUPS):
        total = total + dot_nt(
            sig[:, j * LANES : (j + 1) * LANES], wp[0, j // 4, (j // 2) % 2, j % 2]
        )
    xd_out[:, 0:96] = total
    xd_out[:, 96:128] = jnp.zeros((256, 32), F32)
    xd_copy = sems.copy(xd_out, xd_in, mate, seq)
    xd_copy.start()
    gather_z.relay(3)
    gather_z.cross(2)
    xd_copy.wait()
    xd = xd_out[...] + xd_in[...]
    low[...] = xd[:, 0:64].astype(BF16)
    for n in range(16):
        bb[pl.ds(n, 256, stride=16), :] = jnp.broadcast_to(xd[:, 64 + n : 65 + n], (256, LANES))
        cb[pl.ds(n, 256, stride=16), :] = jnp.broadcast_to(xd[:, 80 + n : 81 + n], (256, LANES))
    for j in range(GROUPS):
        at = slice(j * LANES, (j + 1) * LANES)
        pre = dot_nn(low[...], wp[1, j // 4, (j // 2) % 2, j % 2, 0:64, :]) + prm[21:22, at]
        delta[:, at] = jnp.maximum(pre, 0.0) + jnp.log1p(jnp.exp(-jnp.abs(pre)))

    gather_z.cross(3)

    def decay(slab, j, a, base):
        return jnp.exp2(spread(slab, j) * a) * wide(rows_of(kb2, base))

    kb2 = kb.reshape(256, LANES)

    def tile16(ref, t):
        return ref[pl.ds(pl.multiple_of(t * 16, 16), 16), :]

    def forward_ends(q):
        ctx, block = q // 2, q % 2
        at = lanes_at(block, WIDE)
        a = a2[:, at]

        def eight(i, h):
            t0 = pl.multiple_of(ctx * ROWS + i * 8, 8)
            d = delta[pl.ds(t0, 8), at]
            u = d * slab_of(sig, t0, at)
            for j in range(8):
                h = decay(d, j, a, t0 + j) * h + spread(u, j) * wide(tile16(bb, t0 + j))
            return h

        h = lax.fori_loop(0, 16, eight, jnp.zeros((16, WIDE), F32))
        rows = pl.ds(pl.multiple_of(ctx * ROWS, ROWS), ROWS)
        summed = jnp.sum(delta[rows, at], axis=0, keepdims=True)
        kept = jnp.min(kb[ctx], axis=0, keepdims=True)
        decays = jnp.exp2(jnp.broadcast_to(summed, (16, WIDE)) * a) * wide(
            jnp.broadcast_to(kept, (16, LANES))
        )
        for g in range(4):
            piece = ctx * GROUPS + block * 4 + g
            hp[piece, 0] = h[:, g * LANES : (g + 1) * LANES]
            hp[piece, 1] = decays[:, g * LANES : (g + 1) * LANES]

    def slab_of(ref, t0, at):
        base = pl.multiple_of((t0 // 16) * 16, 16)
        both = ref[pl.ds(base, 16), at].astype(F32)
        return jnp.where(t0 % 16 == 0, both[:8], both[8:])

    for_each(4, forward_ends)
    send_ends = Transpose(sems, hp, hpr)
    send_ends.start()
    gather_o.relay(0)
    gather_o.relay(1)

    def z_columns(i):
        rows = nrm_rows()
        for half in (0, 1):
            w = wz[half, :, :, :, :, lanes_at(i, 256)].reshape(1024, 256)
            at = pl.ds(pl.multiple_of(half * 512 + i * 256, 256), 256)
            zz[:, at] = dot_nn(rows, w)

    def nrm_rows():
        return jnp.concatenate([nrm[0, 16:144, :], nrm[1, 16:144, :]], axis=0)

    send_ends.done()
    state = jnp.zeros((16, LANES), F32)
    for s in range(16):
        hret[s] = state
        state = hpr[s, 1] * state + hpr[s, 0]
    return_states = Transpose(sems, hret, hin)
    return_states.start()
    gather_o.cross(0)
    gather_o.cross(1)
    gather_z.done()
    across_z.done()
    for_each(2, z_columns)

    def forward(q):
        ctx, block = q // 2, q % 2
        at = lanes_at(block, WIDE)
        a = a2[:, at]
        h0 = jnp.concatenate([hin[ctx * GROUPS + block * 4 + g] for g in range(4)], axis=1)
        hs[ctx * 129, :, at] = h0

        def eight(i, h):
            t0 = pl.multiple_of(ctx * ROWS + i * 8, 8)
            d = delta[pl.ds(t0, 8), at]
            s8 = slab_of(sig, t0, at)
            u = d * s8
            for j in range(8):
                h = decay(d, j, a, t0 + j) * h + spread(u, j) * wide(tile16(bb, t0 + j))
                hs[t0 + ctx + j + 1, :, at] = h
                put_partial(part1, j, h * wide(tile16(cb, t0 + j)))
            yy[pl.ds(t0, 8), at] = take_partial(part1) + prm[22:23, at] * s8
            return h

        lax.fori_loop(0, 16, eight, h0)

    gbr_copy.wait_recv()

    def branch_back(i):
        branch = gbr[...].reshape(256, 1024)
        w0 = wo[0, i // 2, i % 2].reshape(256, 512)
        w1 = wo[1, i // 2, i % 2].reshape(256, 512)
        gm = dot_nt(branch[:, :512], w0) + dot_nt(branch[:, 512:], w1)
        at = lanes_at(i, 256)
        zv = zz[:, at]
        sigma = jax.nn.sigmoid(zv)
        gs[:, at] = gm * (zv * sigma)
        gz[:, at] = (gm * yy[:, at] * (sigma * (1.0 + zv * (1.0 - sigma)))).astype(BF16)

    def z_grads(i):
        d = pl.ds(pl.multiple_of(i * 128, 128), 128)
        for half in (0, 1):
            got = dot_nn(nrm_t[d, :], gz[:, half * 512 : (half + 1) * 512])
            gz_w[half, i // 2, i % 2] = got.astype(BF16).reshape(2, 64, 512)

    def backward_ends(q):
        ctx, block = q // 2, q % 2
        at = lanes_at(block, WIDE)
        a = a2[:, at]

        def eight(i, adj):
            t0 = pl.multiple_of(ctx * ROWS + (15 - i) * 8, 8)
            d = delta[pl.ds(t0, 8), at]
            u = gs[pl.ds(t0, 8), at]
            for j in range(7, -1, -1):
                adj = decay(d, j, a, t0 + j) * (adj + spread(u, j) * wide(tile16(cb, t0 + j)))
            return adj

        adj = lax.fori_loop(0, 16, eight, jnp.zeros((16, WIDE), F32))
        for g in range(4):
            lp[ctx * GROUPS + block * 4 + g] = adj[:, g * LANES : (g + 1) * LANES]

    return_states.done()
    for_each(4, forward)
    for ctx in (0, 1):
        for g in range(GROUPS):
            at = slice(g * LANES, (g + 1) * LANES)
            rows = slice(ctx * ROWS, (ctx + 1) * ROWS)
            zv = zz[rows, at]
            val = (yy[rows, at] * zv * jax.nn.sigmoid(zv)).astype(BF16)
            mid[rows, at] = val
            mid_t[at, rows] = jnp.transpose(val.astype(F32)).astype(BF16)

    def out_grads(i):
        e = pl.ds(pl.multiple_of(i * 256, 256), 256)
        branch = gbr[...].reshape(256, 1024)
        for half in (0, 1):
            got = dot_nn(mid_t[e, :], branch[:, half * 512 : (half + 1) * 512])
            go_w[half, i // 2, i % 2] = got.astype(BF16).reshape(2, 128, 512)

    for_each(4, out_grads)
    scatter_o = HalfScatter(sems, go_w, o1, o2, o3, 128)
    scatter_o.push1(1)

    for j in (0, 1):
        gather_o.slot_done(j)
        block = half_slot(j)
        branch_back(2 * block)
        branch_back(2 * block + 1)
        backward_ends(block)
        backward_ends(2 + block)
    send_adj = Transpose(sems, lp, lpr)
    send_adj.start()
    for_each(8, z_grads)
    scatter_z = Scatter(sems, gz_w, z1, z2, z3, 48)
    across_gz = AcrossScatter(sems, gz_w, c1, c2, c3, 48, 16)
    send_adj.done()
    state = jnp.zeros((16, LANES), F32)
    for s in range(15, -1, -1):
        lret[s] = state
        state = hpr[s, 1] * state + lpr[s]
    return_adj = Transpose(sems, lret, lin)
    return_adj.start()
    scatter_o.push1(0)
    across_gz.push1()
    scatter_z.push1(2)
    scatter_z.push1(3)
    for half in (0, 1):
        got = dot_nn(mid[...], wo[half].reshape(1024, 512))
        for ctx in (0, 1):
            rowx[ctx, :, half * 512 : (half + 1) * 512] = got[ctx * ROWS : (ctx + 1) * ROWS]
    rows_copy = sems.copy(rowx.at[mate], rowx_in.at[0], mate, seq)
    rows_copy.start()
    return_adj.done()

    sub = lax.broadcasted_iota(jnp.int32, (8, LANES), 0)
    pick_b = [(lane == 64 + 8 * k + sub).astype(F32) for k in (0, 1)]
    pick_c = [(lane == 80 + 8 * k + sub).astype(F32) for k in (0, 1)]
    all_ones = jnp.ones((LANES, LANES), BF16)
    def backward(ctx, block):
        at = slice(block * WIDE, (block + 1) * WIDE)
        a = a2[:, at]

        def eight(i, carry):
            adj, grad_a = carry
            t0 = pl.multiple_of(ctx * ROWS + (15 - i) * 8, 8)
            d = delta[pl.ds(t0, 8), at]
            g8 = gs[pl.ds(t0, 8), at]
            u = d * slab_of(sig, t0, at)
            h_next = hs[t0 + ctx + 8, :, at]
            for j in range(7, -1, -1):
                t = t0 + j
                dj = spread(d, j)
                gj = spread(g8, j)
                lam = adj + gj * wide(tile16(cb, t))
                adj = jnp.exp2(dj * a) * wide(rows_of(kb2, t)) * lam
                h_prev = hs[t + ctx, :, at]
                flow = adj * h_prev
                grad_a = grad_a + flow * dj
                put_partial(part1, j, flow * a)
                put_partial(part2, j, lam * wide(tile16(bb, t)))
                to = pl.ds(pl.multiple_of((t - ctx * ROWS) * 16, 16), 16)
                qb[block, to, :] = fold_lanes(lam * spread(u, j)).astype(BF16)
                qc[block, to, :] = fold_lanes(gj * h_next).astype(BF16)
                h_next = h_prev
            yy[pl.ds(t0, 8), at] = take_partial(part1) * (1.0 / LOG2E)
            zz[pl.ds(t0, 8), at] = take_partial(part2)
            return adj, grad_a

        adj0 = jnp.concatenate([lin[ctx * GROUPS + block * 4 + g] for g in range(4)], axis=1)
        _, grad_a = lax.fori_loop(0, 16, eight, (adj0, jnp.zeros((16, WIDE), F32)))
        hs[ctx * 129, :, at] = grad_a

    def sum_lanes(ctx, i):
        for k in range(2):
            t0 = pl.multiple_of(i * 32 + k * 16, 16)
            at = pl.ds(pl.multiple_of(t0 * 16, 256), 256)
            sum_b = dot_nn(qb[0, at, :], all_ones) + dot_nn(qb[1, at, :], all_ones)
            sum_c = dot_nn(qc[0, at, :], all_ones) + dot_nn(qc[1, at, :], all_ones)
            for j in range(16):
                got = sum_b[16 * j : 16 * j + 8] * pick_b[0]
                got = got + sum_b[16 * j + 8 : 16 * j + 16] * pick_b[1]
                got = got + sum_c[16 * j : 16 * j + 8] * pick_c[0]
                got = got + sum_c[16 * j + 8 : 16 * j + 16] * pick_c[1]
                part3[k * 128 + 8 * j : k * 128 + 8 * j + 8, :] = got
            for j in range(2):
                got = part3[pl.ds(k * 128 + j * 64, 8, stride=8), :]
                for n in range(1, 8):
                    got = got + part3[pl.ds(k * 128 + j * 64 + n, 8, stride=8), :]
                gbc[pl.ds(pl.multiple_of(ctx * ROWS + t0 + 8 * j, 8), 8), :] = got

    backward(0, 0)
    scatter_o.push2(1)
    scatter_z.push1(1)
    backward(0, 1)
    scatter_o.push2(0)
    scatter_z.push1(0)
    for_each(4, functools.partial(sum_lanes, 0))
    backward(1, 0)
    across_gz.push2()
    scatter_z.push2(2)
    backward(1, 1)
    scatter_o.push3(1)
    scatter_z.push2(3)
    for_each(4, functools.partial(sum_lanes, 1))

    ones = []
    for j in range(GROUPS):
        at = slice(j * LANES, (j + 1) * LANES)
        sv = sig[:, at].astype(F32)
        g_pre = ((yy[:, at] + zz[:, at] * sv) * (1.0 - jnp.exp(-delta[:, at]))).astype(BF16)
        mid[:, at] = g_pre
        ones.append(jnp.sum(g_pre.astype(F32), axis=0, keepdims=True))
    g_bdt = jnp.concatenate(ones, axis=1)

    total = jnp.zeros((256, 64), F32)
    for j in range(GROUPS):
        total = total + dot_nt(
            mid[:, j * LANES : (j + 1) * LANES], wp[1, j // 4, (j // 2) % 2, j % 2, 0:64, :]
        )
    xd_out[:, 0:64] = total
    xd_out[:, 64:128] = gbc[:, 64:128]
    gd_copy = sems.copy(xd_out, xd_in, mate, seq)
    rows_copy.wait()
    gd_copy.start()
    across_gz.push3()
    for g in range(GROUPS):
        at = slice(g * LANES, (g + 1) * LANES)
        o_out[:, at] = (
            hidb[c, 16:144, at].astype(F32) + live * (rowx[c, :, at] + rowx_in[0, :, at])
        ).astype(BF16)
    scatter_z.push2(1)
    gd_copy.wait()
    g_dbl = (xd_out[...] + xd_in[...]).astype(BF16)

    for ctx in (0, 1):
        for j in range(GROUPS):
            at = slice(j * LANES, (j + 1) * LANES)
            rows = slice(ctx * ROWS, (ctx + 1) * ROWS)
            back = dot_nn(g_dbl[rows, 0:96], wp[0, j // 4, (j // 2) % 2, j % 2])
            g_sig = gs[rows, at] * prm[22:23, at] + zz[rows, at] * delta[rows, at] + back
            v = conv_rows(ctx, at)
            sigma = jax.nn.sigmoid(v)
            gext[ctx, 0:128, at] = g_sig * (sigma * (1.0 + v * (1.0 - sigma)))
    edge_copies = [
        sems.copy(gext.at[ctx, pl.ds(0, 8), :], gedge.at[ctx], c, before) for ctx in (0, 1)
    ]
    for copy in edge_copies:
        copy.start()
    scatter_z.push2(0)
    scatter_o.push3(0)

    def small_grads():
        a_rows = -jnp.exp(prm[0:16, :])
        g_alog = (hs[0] + hs[129]) * a_rows
        g_t = jnp.transpose(g_dbl.astype(F32))[0:96].astype(BF16)
        low_t = jnp.transpose(
            jnp.concatenate([low[...].astype(F32), jnp.zeros((256, 64), F32)], axis=1)
        )[0:64].astype(BF16)
        for j in range(GROUPS):
            at = slice(j * LANES, (j + 1) * LANES)
            to = (j // 4, (j // 2) % 2, j % 2)
            sv = sig[:, at].astype(F32)
            gp_w[(0,) + to] = dot_nn(g_t, sig[:, at]).astype(BF16)
            g_dtw = dot_nn(low_t, mid[:, at])
            taps = []
            for k in range(4):
                term = jnp.zeros((1, LANES), F32)
                for ctx in (0, 1):
                    term = term + jnp.sum(
                        gext[ctx, 0:128, at] * xext[ctx, 13 + k : 141 + k, at],
                        axis=0,
                        keepdims=True,
                    )
                taps.append(term)
            bias = jnp.sum(gext[0, 0:128, at] + gext[1, 0:128, at], axis=0, keepdims=True)
            skip = jnp.sum(gs[:, at] * sv, axis=0, keepdims=True)
            rest = jnp.concatenate(
                [g_dtw, g_alog[:, at]]
                + taps
                + [bias, g_bdt[:, at], skip, jnp.zeros((9, LANES), F32)],
                axis=0,
            )
            gp_w[(1,) + to] = rest.astype(BF16)

    small_grads()
    scatter_p = HalfScatter(sems, gp_w, p1, p2, p3, 96)
    scatter_p.all1()

    for copy in edge_copies:
        copy.wait_recv()
    last_chip = (seq < 15).astype(F32)
    for ctx in (0, 1):
        gext[ctx, 128:136, :] = gedge[ctx] * last_chip

    for ctx in (0, 1):

        def x_back(i):
            at = lanes_at(i, LANES)
            total = prm[19:20, at] * gext[ctx, 0:128, at]
            for k in range(3):
                total = total + prm[16 + k : 17 + k, at] * gext[ctx, 3 - k : 131 - k, at]
            mid[ctx * ROWS : (ctx + 1) * ROWS, at] = total.astype(BF16)

        for_each(GROUPS, x_back)

    def x_grads(i):
        d = pl.ds(pl.multiple_of(i * 128, 128), 128)
        for half in (0, 1):
            got = dot_nn(nrm_t[d, :], mid[:, half * 512 : (half + 1) * 512])
            gx_w[half, i // 2, i % 2] = got.astype(BF16).reshape(2, 64, 512)

    scatter_x = Scatter(sems, gx_w, x1, x2, x3, 64)
    for j in scatter_x.order:
        zj = partner(z, j)
        x_grads(2 * zj)
        x_grads(2 * zj + 1)
        scatter_x.push1(j)
        scatter_z.push3(j)
    def normed_back(i):
        total = jnp.zeros((256, 128), F32)
        for half in (0, 1):
            at = slice(half * 512, (half + 1) * 512)
            total = total + dot_nt(mid[:, at], wx[half, i // 2, i % 2].reshape(128, 512))
            total = total + dot_nt(gz[:, at], wz[half, i // 2, i % 2].reshape(128, 512))
        to = lanes_at(i, 128)
        for ctx in (0, 1):
            rowx[ctx, :, to] = total[ctx * ROWS : (ctx + 1) * ROWS]

    for i in range(4):
        normed_back(i)
    scatter_p.all2()
    scatter_x.push2(2)
    for i in range(4, 8):
        normed_back(i)
    back_copy = sems.copy(rowx.at[mate], rowx_in.at[1], mate, seq)
    back_copy.start()
    scatter_x.push2(3)
    scatter_p.all3()
    scatter_x.push2(1)

    def hidden_rows(i):
        at = pl.ds(pl.multiple_of(i * 16, 16), 16)
        rows = hidb[c, pl.ds(pl.multiple_of(16 + i * 16, 16), 16), :].astype(F32)
        r = lax.rsqrt(jnp.mean(rows * rows, axis=1, keepdims=True) + epsilon)
        g_hat = (rowx[c, at, :] + rowx_in[1, at, :]) * gain_row
        inner = jnp.mean(g_hat * rows, axis=1, keepdims=True)
        o_gh[at, :] = r * g_hat - rows * (r * r * r * inner) + out_g[at, :].astype(F32)

    back_copy.wait()
    for_each(8, hidden_rows)
    scatter_x.push3(2)
    scatter_x.push2(0)
    scatter_x.push3(3)
    scatter_x.push3(1)
    scatter_x.push3(0)
    scatter_o.done()
    out_copy = sems.copy(o_gout, o_gout, mate, seq)

    @pl.when(is_active())
    def _():
        for half in (0, 1):
            o_gout[:, half * 512 : (half + 1) * 512] = scatter_o.result(half)
        out_copy.start()

    scatter_z.done()
    across_gz.done()
    for half in (0, 1):
        fin[2 + half, 0:48, :] = scatter_z.result(half)
        fin[2 + half, 48:64, :] = across_gz.result(half)
    z_copy = sems.copy(fin.at[pl.ds(2, 2)], fin_in.at[pl.ds(2, 2)], mate, seq)
    z_copy.start()
    scatter_p.done()
    small_copy = sems.copy(fsm, fsm, mate, seq)

    @pl.when(is_active())
    def _():
        for half in (0, 1):
            fsm[half * 96 : (half + 1) * 96, :] = scatter_p.result(half)
        small_copy.start()

    def weight_rows(part, gain_sum):
        for half in (0, 1):
            for core, ref in ((c, fin), (mate, fin_in)):
                at = pl.ds(pl.multiple_of(part * 2048 + core * 1024 + half * 512, 512), 512)
                rows = ref[part * 2 + half]
                o_gin[:, at] = rows
                gain_sum = gain_sum + fold_lanes(rows * in_w[:, at].astype(F32))
        return gain_sum

    z_copy.wait()
    gain_sum = weight_rows(1, jnp.zeros((64, LANES), F32))
    for group in (gather_x, gather_z, gather_o, gather_p, scatter_z, scatter_o):
        group.sent()
    for group in (across_z, across_gz, send_ends, return_states, send_adj, return_adj):
        group.sent()
    for copy in hid_copies + edge_copies + [gbr_copy, gain_all]:
        copy.wait_send()

    scatter_x.done()
    for half in (0, 1):
        fin[half] = scatter_x.result(half)
    x_copy = sems.copy(fin.at[pl.ds(0, 2)], fin_in.at[pl.ds(0, 2)], mate, seq)
    x_copy.start()

    @pl.when(is_active())
    def _():
        out_copy.wait_send()
        small_copy.wait_send()

    @pl.when(is_passive())
    def _():
        out_copy.wait_recv()
        small_copy.wait_recv()

    o_small[...] = fsm[...]
    scatter_x.sent()
    scatter_p.sent()
    x_copy.wait()
    o_gain[...] = weight_rows(0, gain_sum)


def fused_shards(
    hidden,
    out_grad,
    resets,
    valid,
    norm_gain,
    in_weight,
    conv_weight,
    conv_bias,
    x_weight,
    dt_weight,
    dt_bias,
    a_log,
    skip_gain,
    out_weight,
):
    norm_row = norm_gain.astype(F32)
    vectors = jnp.stack(
        [
            conv_bias.astype(F32),
            dt_bias.astype(F32),
            skip_gain.astype(F32),
            jnp.concatenate([norm_row, norm_row]),
        ]
    )
    vmem = pltpu.VMEM
    sends, receives = 71, 92
    scratch = [
        vmem((2, 144, 1024), BF16),
        vmem((2, 128, 1024), BF16),
        vmem((2, 128, LANES), F32),
        vmem((16, 8, LANES), F32),
        vmem((2, 144, 1024), BF16),
        vmem((1024, 256), BF16),
        vmem((2, 144, 1024), F32),
        vmem((256, 1024), BF16),
        vmem((256, 1024), F32),
        vmem((256, 1024), F32),
        vmem((256, 1024), F32),
        vmem((256, 1024), F32),
        vmem((4096, LANES), F32),
        vmem((4096, LANES), F32),
        vmem((16, 1024), F32),
        vmem((32, 1024), F32),
        vmem((258, 16, 1024), F32),
        vmem((2, 2048, LANES), BF16),
        vmem((2, 2048, LANES), BF16),
        vmem((256, LANES), F32),
        vmem((256, LANES), F32),
        vmem((256, LANES), F32),
        vmem((256, LANES), F32),
        vmem((256, 64), BF16),
        vmem((256, 1024), BF16),
        vmem((1024, 256), BF16),
        vmem((256, 1024), BF16),
        vmem((2, 4, 2, 2, 64, 512), BF16),
        vmem((2, 4, 2, 2, 64, 512), BF16),
        vmem((2, 2, 2, 2, 128, 512), BF16),
        vmem((2, 2, 2, 2, 96, LANES), BF16),
        vmem((2, 4, 2, 2, 64, 512), BF16),
        vmem((2, 4, 2, 2, 64, 512), BF16),
        vmem((2, 2, 2, 2, 128, 512), BF16),
        vmem((2, 2, 2, 2, 96, LANES), BF16),
    ]
    for z_count, rows, columns in ((4, 64, 512), (4, 48, 512), (2, 128, 512)):
        scratch += [
            vmem((2, z_count, 2, rows, columns), BF16),
            vmem((2, z_count, rows, columns), BF16),
            vmem((3, 2, rows, columns), BF16),
        ]
    scratch += [
        vmem((2, 2, 2, 96, LANES), BF16),
        vmem((2, 2, 96, LANES), BF16),
        vmem((3, 2, 96, LANES), BF16),
        vmem((3, 2, 2, 2, 16, 512), BF16),
        vmem((2, 2, 16, 512), BF16),
        vmem((2, 16, 512), BF16),
        vmem((16, 2, 16, LANES), F32),
        vmem((16, 2, 16, LANES), F32),
        vmem((16, 16, LANES), F32),
        vmem((16, 16, LANES), F32),
        vmem((16, 16, LANES), F32),
        vmem((16, 16, LANES), F32),
        vmem((16, 16, LANES), F32),
        vmem((16, 16, LANES), F32),
        vmem((256, LANES), F32),
        vmem((256, LANES), F32),
        vmem((2, 136, 1024), F32),
        vmem((2, 8, 1024), F32),
        vmem((2, 128, 1024), F32),
        vmem((2, 128, 1024), F32),
        vmem((4, 64, 512), F32),
        vmem((4, 64, 512), F32),
        vmem((192, LANES), F32),
        vmem((64, 4096), BF16),
        vmem((128, 1024), BF16),
        pltpu.SemaphoreType.DMA((9,)),
        pltpu.SemaphoreType.DMA((sends,)),
        pltpu.SemaphoreType.DMA((receives,)),
    ]
    whole = pl.BlockSpec(memory_space=pltpu.VMEM)
    hbm = pl.BlockSpec(memory_space=pl.ANY)
    parts = pl.pallas_call(
        fused_kernel,
        out_shape=(
            jax.ShapeDtypeStruct((128, 1024), BF16),
            jax.ShapeDtypeStruct((128, 1024), F32),
            jax.ShapeDtypeStruct((64, 4096), F32),
            jax.ShapeDtypeStruct((128, 1024), F32),
            jax.ShapeDtypeStruct((192, LANES), F32),
            jax.ShapeDtypeStruct((64, LANES), F32),
        ),
        in_specs=[pl.BlockSpec(memory_space=pltpu.SMEM), hbm, hbm, whole, hbm, hbm] + [whole] * 5,
        out_specs=(whole,) * 6,
        scratch_shapes=scratch,
        compiler_params=pltpu.CompilerParams(
            collective_id=0, has_side_effects=True, vmem_limit_bytes=64 * 2**20
        ),
    )(
        valid,
        hidden[0],
        out_grad[0],
        resets,
        in_weight,
        out_weight,
        x_weight.T,
        dt_weight.T,
        a_log.T,
        conv_weight.T,
        vectors,
    )
    got = pl.pallas_call(
        place_outputs,
        out_shape=tuple(
            jax.ShapeDtypeStruct(shape, dtype)
            for shape, dtype in (
                ((128, 1024), BF16),
                ((128, 1024), F32),
                ((1, 64), F32),
                ((64, 4096), F32),
                ((4, LANES), F32),
                ((1, LANES), F32),
                ((96, LANES), F32),
                ((64, LANES), F32),
                ((1, LANES), F32),
                ((16, LANES), F32),
                ((1, LANES), F32),
                ((128, 1024), F32),
            )
        ),
        in_specs=[whole] * 7,
        out_specs=(whole,) * 12,
        compiler_params=pltpu.CompilerParams(vmem_limit_bytes=64 * 2**20),
    )(*parts, vectors)
    return (
        got[0][None],
        got[1][None],
        got[2][0],
        got[3],
        got[4].T,
        got[5][0],
        got[6].T,
        got[7].T,
        got[8][0],
        got[9].T,
        got[10][0],
        got[11],
    )


def place_outputs(
    out,
    g_hidden,
    g_in,
    g_out,
    small,
    gain,
    vectors,
    o_out,
    o_hidden,
    o_gain,
    o_in,
    o_taps,
    o_bias,
    o_xw,
    o_dtw,
    o_dtb,
    o_alog,
    o_skip,
    o_outw,
):
    o_out[...] = out[...]
    o_hidden[...] = g_hidden[...]
    o_in[...] = g_in[...]
    o_outw[...] = g_out[...]
    o_xw[...] = small[0:96, :]
    o_dtw[...] = small[96:160, :]
    o_alog[...] = small[160:176, :]
    o_taps[...] = small[176:180, :]
    o_bias[...] = small[180:181, :]
    o_dtb[...] = small[181:182, :]
    o_skip[...] = small[182:183, :]
    turned = jnp.transpose(jnp.concatenate([gain[...], jnp.zeros((64, LANES), F32)], axis=0))
    o_gain[...] = (jnp.sum(turned, axis=0, keepdims=True) / vectors[3:4, :])[:, 0:64]


def solution(mesh):
    sizes = dict(mesh.shape)
    body = fused_shards if sizes == {"ctx": 2, "seq": 16} else shards
    return jax.shard_map(
        body,
        mesh=mesh,
        in_specs=(
            P("ctx", "seq", None),
            P("ctx", "seq", None),
            P("ctx", "seq"),
            P("ctx"),
            P("seq"),
            P("seq", None),
            P("seq", None),
            P("seq"),
            P("seq", None),
            P("seq", None),
            P("seq"),
            P("seq", None),
            P("seq"),
            P("seq", None),
        ),
        out_specs=(
            P("ctx", "seq", None),
            P("ctx", "seq", None),
            P("seq"),
            P("seq", None),
            P("seq", None),
            P("seq"),
            P("seq", None),
            P("seq", None),
            P("seq"),
            P("seq", None),
            P("seq"),
            P("seq", None),
        ),
        check_vma=False,
    )
```

```python
import functools

import jax
import jax.numpy as jnp
from jax import lax
from jax.experimental import pallas as pl
from jax.experimental.pallas import tpu as pltpu
from jax.sharding import PartitionSpec as P

epsilon = 1e-05
highest = lax.Precision.HIGHEST
contract_last = (((1,), (1,)), ((), ()))
contract_first = (((0,), (0,)), ((), ()))


def passed_along(block, axis, distance):
    devices = range(lax.axis_size(axis))
    route = [(i - distance, i) for i in devices if i - distance in devices]
    return lax.ppermute(block, axis, route)


def entering_2(part, axis, combine, identity, reverse):
    count = lax.axis_size(axis)
    place = lax.axis_index(axis)
    ahead = count - 1 - place if reverse else place
    gathered = jax.tree.map(lambda a: lax.all_gather(a, axis), part)
    state = jax.tree.map(lambda a, e: jnp.zeros_like(a) + jnp.asarray(e, a.dtype), part, identity)

    def one(hop, state):
        source = count - 1 - hop if reverse else hop
        return combine(
            state, jax.tree.map(lambda a: lax.dynamic_index_in_dim(a, source, 0, False), gathered)
        )

    return lax.fori_loop(0, ahead, one, state)


def silu_slope(value):
    sigma = jax.nn.sigmoid(value)
    return sigma * (1.0 + value * (1.0 - sigma))


def combine_pair(earlier, later):
    return (earlier[0] * later[0], later[0] * earlier[1] + later[1])


def decays_of(delta_blk, keep_blk, a_matrix):
    return keep_blk[:, None, None] * jnp.exp(delta_blk[:, :, None] * a_matrix[None])


def shards(
    hidden,
    out_grad,
    resets,
    valid,
    norm_gain,
    in_weight,
    conv_weight,
    conv_bias,
    x_weight,
    dt_weight,
    dt_bias,
    a_log,
    skip_gain,
    out_weight,
):
    gathered = (
        lax.all_gather(norm_gain, "seq", axis=0, tiled=True),
        lax.all_gather(in_weight, "seq", axis=0, tiled=True),
        lax.all_gather(conv_weight, "seq", axis=0, tiled=True),
        lax.all_gather(conv_bias, "seq", axis=0, tiled=True),
        lax.all_gather(x_weight, "seq", axis=0, tiled=True),
        lax.all_gather(dt_weight, "seq", axis=0, tiled=True),
        lax.all_gather(dt_bias, "seq", axis=0, tiled=True),
        lax.all_gather(a_log, "seq", axis=0, tiled=True),
        lax.all_gather(skip_gain, "seq", axis=0, tiled=True),
        lax.all_gather(out_weight, "seq", axis=0, tiled=True),
    )
    gain_full, w_in, w_conv, b_conv, w_x, w_dt, b_dt, a_logs, w_skip, w_out = gathered
    tokens = hidden.shape[1]
    inner = w_out.shape[0]
    rank = w_dt.shape[1]
    state = a_logs.shape[1]
    taps = w_conv.shape[1]
    places = lax.axis_index("seq") * tokens + jnp.arange(tokens, dtype=jnp.int32)
    live_mask = (places < valid[0]).astype(jnp.float32)
    reset_f = resets[0].astype(jnp.float32)
    keep_mask = 1.0 - reset_f
    source = hidden[0].astype(jnp.float32)
    rscale = lax.rsqrt(jnp.mean(source * source, axis=-1, keepdims=True) + epsilon)
    scaled = source * rscale
    gain_f = gain_full.astype(jnp.float32)
    normed = (scaled * gain_f).astype(jnp.bfloat16)
    projected = jnp.dot(normed, w_in, preferred_element_type=jnp.float32)
    x_part = projected[:, :inner].astype(jnp.bfloat16)
    z_part = projected[:, inner:]
    rim_rows = passed_along(x_part[tokens - (taps - 1) :], "seq", 1)
    extended = jnp.concatenate([rim_rows, x_part], 0).astype(jnp.float32)
    conv_taps = w_conv.astype(jnp.float32)
    conv_out = b_conv.astype(jnp.float32) + sum(
        (conv_taps[:, offset] * extended[offset : offset + tokens] for offset in range(taps))
    )
    signal_low = jax.nn.silu(conv_out).astype(jnp.bfloat16)
    signal = signal_low.astype(jnp.float32)
    x_dbl = jnp.dot(signal_low, w_x, preferred_element_type=jnp.float32)
    dt_low = x_dbl[:, :rank].astype(jnp.bfloat16)
    b_input = x_dbl[:, rank : rank + state]
    c_output = x_dbl[:, rank + state :]
    dt_pre = lax.dot_general(
        dt_low, w_dt, contract_last, preferred_element_type=jnp.float32
    ) + b_dt.astype(jnp.float32)
    delta = jax.nn.softplus(dt_pre)
    a_matrix = -jnp.exp(a_logs.astype(jnp.float32))
    drive = delta * signal
    reset_count = jnp.cumsum(reset_f)
    reset_before = reset_count - reset_f
    delta_sum = jnp.cumsum(delta, 0)
    delta_before = delta_sum - delta
    reset_total = reset_count[-1]
    delta_total = delta_sum[-1]
    alive_upto = (reset_count == 0.0).astype(jnp.float32)
    alive_before = (reset_before == 0.0).astype(jnp.float32)
    alive_after = (reset_total - reset_count == 0.0).astype(jnp.float32)
    span_len = min(64, tokens)
    n_blocks = tokens // span_len
    roll_by = min(16, span_len)

    def split_blocks(value):
        return value.reshape((n_blocks, span_len) + value.shape[1:])

    delta_b = split_blocks(delta)
    drive_b = split_blocks(drive)
    binput_b = split_blocks(b_input)
    coutput_b = split_blocks(c_output)
    keep_b = split_blocks(keep_mask)
    dsum_b = split_blocks(delta_sum)
    upto_b = split_blocks(alive_upto)
    after_b = split_blocks(alive_after)
    ones_state = jnp.ones((inner, state), jnp.float32)
    zero_state = jnp.zeros((inner, state), jnp.float32)
    group_prod = (reset_total == 0.0).astype(jnp.float32) * jnp.exp(delta_total[:, None] * a_matrix)

    def forward_step(state_now, blk):
        delta_blk, drive_blk, binput_blk, coutput_blk, keep_blk = blk
        decays = decays_of(delta_blk, keep_blk, a_matrix)

        def token_step(state_tok, item):
            decay_now, drive_now, binput_now, coutput_now = item
            state_next = decay_now * state_tok + drive_now[:, None] * binput_now[None, :]
            return (state_next, jnp.sum(state_next * coutput_now[None, :], -1))

        state_end, outputs = lax.scan(
            token_step, state_now, (decays, drive_blk, binput_blk, coutput_blk), unroll=roll_by
        )
        return (state_end, (state_now, outputs))

    group_state, (local_starts, scan_local) = lax.scan(
        forward_step, zero_state, (delta_b, drive_b, binput_b, coutput_b, keep_b)
    )
    entering = entering_2(
        (group_prod, group_state), "seq", combine_pair, (ones_state, zero_state), False
    )
    state_in = entering[1]

    def lift_block(blk):
        dsum_blk, upto_blk, coutput_blk = blk
        lifted = (
            upto_blk[:, None, None]
            * jnp.exp(dsum_blk[:, :, None] * a_matrix[None])
            * state_in[None]
        )
        return jnp.sum(lifted * coutput_blk[:, None, :], -1)

    lifted_out = lax.map(lift_block, (dsum_b, upto_b, coutput_b))
    scanned = (scan_local + lifted_out).reshape(tokens, inner) + w_skip.astype(jnp.float32) * signal
    gate_act = jax.nn.silu(z_part)
    mixed = (scanned * gate_act).astype(jnp.bfloat16)
    branch = jnp.dot(mixed, w_out, preferred_element_type=jnp.float32)
    result = (source + live_mask[:, None] * branch).astype(jnp.bfloat16)
    regathered = (
        lax.all_gather(norm_gain, "seq", axis=0, tiled=True),
        lax.all_gather(in_weight, "seq", axis=0, tiled=True),
        lax.all_gather(conv_weight, "seq", axis=0, tiled=True),
        lax.all_gather(conv_bias, "seq", axis=0, tiled=True),
        lax.all_gather(x_weight, "seq", axis=0, tiled=True),
        lax.all_gather(dt_weight, "seq", axis=0, tiled=True),
        lax.all_gather(dt_bias, "seq", axis=0, tiled=True),
        lax.all_gather(a_log, "seq", axis=0, tiled=True),
        lax.all_gather(skip_gain, "seq", axis=0, tiled=True),
        lax.all_gather(out_weight, "seq", axis=0, tiled=True),
    )
    gain_full, w_in, w_conv, b_conv, w_x, w_dt, b_dt, a_logs, w_skip, w_out = regathered
    gain_f = gain_full.astype(jnp.float32)
    conv_taps = w_conv.astype(jnp.float32)
    a_matrix = -jnp.exp(a_logs.astype(jnp.float32))
    cotangent = out_grad[0].astype(jnp.float32)
    g_branch = (live_mask[:, None] * cotangent).astype(jnp.bfloat16)
    g_mixed = lax.dot_general(g_branch, w_out, contract_last, preferred_element_type=jnp.float32)
    g_scan = g_mixed * gate_act
    g_zpart = g_mixed * scanned * silu_slope(z_part)
    g_skip_full = jnp.sum(g_scan * signal, 0)
    gscan_b = split_blocks(g_scan)

    def push_block(total, blk):
        dsum_blk, upto_blk, coutput_blk, gscan_blk = blk
        weight_blk = upto_blk[:, None, None] * jnp.exp(dsum_blk[:, :, None] * a_matrix[None])
        return (
            total + jnp.sum(weight_blk * gscan_blk[:, :, None] * coutput_blk[:, None, :], 0),
            None,
        )

    passed_local, _ = lax.scan(push_block, zero_state, (dsum_b, upto_b, coutput_b, gscan_b))
    leaving = entering_2(
        (group_prod, passed_local), "seq", combine_pair, (ones_state, zero_state), True
    )
    passed_in = leaving[1]
    start_rows = jnp.arange(n_blocks) * span_len
    start_alive = alive_before[start_rows]
    start_delta = delta_before[start_rows]
    block_starts = (
        local_starts
        + start_alive[:, None, None]
        * jnp.exp(start_delta[:, :, None] * a_matrix[None])
        * state_in[None]
    )

    def backward_step(carried, blk):
        passed, grad_amat = carried
        (
            start_state,
            delta_blk,
            drive_blk,
            binput_blk,
            coutput_blk,
            gscan_blk,
            keep_blk,
            dsum_blk,
            after_blk,
        ) = blk
        decays = decays_of(delta_blk, keep_blk, a_matrix)

        def ahead_step(state_tok, item):
            decay_now, drive_now, binput_now = item
            state_next = decay_now * state_tok + drive_now[:, None] * binput_now[None, :]
            return (state_next, state_next)

        _, states_blk = lax.scan(
            ahead_step, start_state, (decays, drive_blk, binput_blk), unroll=roll_by
        )
        before = jnp.concatenate([start_state[None], states_blk[:-1]], 0)

        def behind_step(passed_tok, item):
            decay_now, coutput_now, gscan_now = item
            adjoint = gscan_now[:, None] * coutput_now[None, :] + passed_tok
            return (decay_now * adjoint, adjoint)

        passed, adjoints_local = lax.scan(
            behind_step, passed, (decays, coutput_blk, gscan_blk), reverse=True, unroll=roll_by
        )
        reach = after_blk[:, None, None] * jnp.exp(
            (delta_total[None] - dsum_blk)[:, :, None] * a_matrix[None]
        )
        adjoints = adjoints_local + reach * passed_in[None]
        flow = adjoints * before * decays
        g_delta_decay = jnp.sum(flow * a_matrix[None], -1)
        grad_amat = grad_amat + jnp.sum(flow * delta_blk[:, :, None], 0)
        g_drive = jnp.einsum("qen,qn->qe", adjoints, binput_blk, precision=highest)
        g_binput = jnp.einsum("qen,qe->qn", adjoints, drive_blk, precision=highest)
        g_coutput = jnp.einsum("qen,qe->qn", states_blk, gscan_blk, precision=highest)
        return ((passed, grad_amat), (g_delta_decay, g_drive, g_binput, g_coutput))

    (_, grad_amat), pieces = lax.scan(
        backward_step,
        (zero_state, zero_state),
        (block_starts, delta_b, drive_b, binput_b, coutput_b, gscan_b, keep_b, dsum_b, after_b),
        reverse=True,
    )
    g_delta_decay = pieces[0].reshape(tokens, inner)
    g_drive = pieces[1].reshape(tokens, inner)
    g_binput = pieces[2].reshape(tokens, state)
    g_coutput = pieces[3].reshape(tokens, state)
    g_delta = g_delta_decay + g_drive * signal
    g_pre = (g_delta * jax.nn.sigmoid(dt_pre)).astype(jnp.bfloat16)
    g_dtlow = jnp.dot(g_pre, w_dt, preferred_element_type=jnp.float32)
    g_xdbl = jnp.concatenate([g_dtlow, g_binput, g_coutput], 1).astype(jnp.bfloat16)
    g_signal = (
        g_scan * w_skip.astype(jnp.float32)
        + g_drive * delta
        + lax.dot_general(g_xdbl, w_x, contract_last, preferred_element_type=jnp.float32)
    )
    g_conv = g_signal * silu_slope(conv_out)
    g_extended = sum(
        (
            jnp.pad(conv_taps[:, offset] * g_conv, ((offset, taps - 1 - offset), (0, 0)))
            for offset in range(taps)
        )
    )
    returned = passed_along(g_extended[: taps - 1], "seq", -1)
    g_xpart = g_extended[taps - 1 :] + jnp.pad(returned, ((tokens - (taps - 1), 0), (0, 0)))
    g_proj = jnp.concatenate([g_xpart, g_zpart], 1).astype(jnp.bfloat16)
    g_normed = lax.dot_general(g_proj, w_in, contract_last, preferred_element_type=jnp.float32)
    g_hat = g_normed * gain_f
    grad_source = (
        rscale * g_hat
        - source * rscale * rscale * rscale * jnp.mean(g_hat * source, axis=-1, keepdims=True)
        + cotangent
    )
    g_gain = jnp.sum(g_normed * scaled, 0)
    g_wconv = jnp.stack(
        [jnp.sum(g_conv * extended[offset : offset + tokens], 0) for offset in range(taps)], 1
    )
    g_bconv = jnp.sum(g_conv, 0)
    g_bdt = jnp.sum(g_pre.astype(jnp.float32), 0)
    g_alog = grad_amat * a_matrix
    weight_rows = lax.dot_general(
        normed, g_proj, contract_first, preferred_element_type=jnp.float32
    )
    g_win_rows, g_gain_rows = lax.psum_scatter(
        (weight_rows, g_gain), "seq", scatter_dimension=0, tiled=True
    )
    xw_rows = lax.dot_general(
        signal_low, g_xdbl, contract_first, preferred_element_type=jnp.float32
    )
    dtw_rows = lax.dot_general(g_pre, dt_low, contract_first, preferred_element_type=jnp.float32)
    outw_rows = lax.dot_general(mixed, g_branch, contract_first, preferred_element_type=jnp.float32)
    (
        g_wconv_rows,
        g_bconv_rows,
        g_wx_rows,
        g_wdt_rows,
        g_bdt_rows,
        g_alog_rows,
        g_skip_rows,
        g_wout_rows,
    ) = lax.psum_scatter(
        (g_wconv, g_bconv, xw_rows, dtw_rows, g_bdt, g_alog, g_skip_full, outw_rows),
        "seq",
        scatter_dimension=0,
        tiled=True,
    )
    totals = lax.psum(
        (
            g_gain_rows,
            g_win_rows,
            g_wconv_rows,
            g_bconv_rows,
            g_wx_rows,
            g_wdt_rows,
            g_bdt_rows,
            g_alog_rows,
            g_skip_rows,
            g_wout_rows,
        ),
        "ctx",
    )
    return (
        result[None],
        grad_source[None],
        totals[0],
        totals[1],
        totals[2],
        totals[3],
        totals[4],
        totals[5],
        totals[6],
        totals[7],
        totals[8],
        totals[9],
    )


MESH = pl.DeviceIdType.MESH
F32 = jnp.float32
BF16 = jnp.bfloat16
ROWS = 128
GROUPS = 8
LANES = 128
WIDE = 512
LOG2E = 1.4426950408889634


def place():
    seq = lax.axis_index("seq")
    return lax.axis_index("ctx"), seq, seq // 4, (seq // 2) % 2, seq % 2


def chip(z, y, x):
    return z * 4 + y * 2 + x


class Semaphores:
    def __init__(self, send, receive):
        self.send, self.receive = send, receive
        self.sends = self.receives = 0

    def new_send(self):
        self.sends += 1
        return self.send.at[self.sends - 1]

    def new_receive(self):
        self.receives += 1
        return self.receive.at[self.receives - 1]

    def copy(self, source, target, core, seq, send=None, receive=None):
        return pltpu.make_async_remote_copy(
            src_ref=source,
            dst_ref=target,
            send_sem=self.new_send() if send is None else send,
            recv_sem=self.new_receive() if receive is None else receive,
            device_id=(core, seq),
            device_id_type=MESH,
        )


def joint(region, copy_sems):
    c, _, z, y, x = place()
    send, receive = copy_sems
    return pltpu.make_async_remote_copy(
        src_ref=region,
        dst_ref=region,
        send_sem=send,
        recv_sem=receive,
        device_id=(c, chip(z, y, 1 - x)),
        device_id_type=MESH,
    )


def partner(z, j):
    return (z, z + 1 - 2 * (z % 2), (z + 2) % 4, 3 - z)[j]


class Gather:
    slots = 4

    def __init__(self, sems, buf, rows):
        c, _, z, y, x = place()
        rows = pl.ds(0, rows)
        own = self.slot(0)
        self.first = [
            sems.copy(buf.at[:, own, y, x, rows], buf.at[:, own, y, x, rows], c, chip(partner(z, j), y, x))
            for j in (1, 2, 3)
        ]
        send2, send3 = sems.new_send(), sems.new_send()
        self.second, self.second_all, self.third, self.third_all = [], [], [], []
        for j in range(self.slots):
            s = self.slot(j)
            got = sems.new_receive()
            self.second.append(
                [
                    sems.copy(buf.at[0, s, y, x, rows], buf.at[0, s, y, x, rows], c, chip(z, 1 - y, x), send2, got),
                    sems.copy(buf.at[1, s, y, x, rows], buf.at[1, s, y, x, rows], c, chip(z, y, 1 - x), send2, got),
                ]
            )
            self.second_all.append(joint(buf.at[:, s, y, x, rows], (send2, got)))
            got = sems.new_receive()
            self.third.append(
                [
                    sems.copy(buf.at[0, s, :, x, rows], buf.at[0, s, :, x, rows], c, chip(z, y, 1 - x), send3, got),
                    sems.copy(buf.at[1, s, y, :, rows], buf.at[1, s, y, :, rows], c, chip(z, 1 - y, x), send3, got),
                ]
            )
            self.third_all.append(joint(buf.at[:, s, :, x, rows], (send3, got)))
        self.second_sent = joint(buf.at[:, :, y, x, rows], (send2, got))
        self.third_sent = joint(buf.at[:, :, :, x, rows], (send3, got))

    def slot(self, j):
        return partner(place()[2], j)

    def start(self):
        for copy in self.first:
            copy.start()

    def arrived(self, j):
        if j > 0:
            self.first[j - 1].wait_recv()

    def relay(self, j):
        self.arrived(j)
        for copy in self.second[j]:
            copy.start()

    def cross(self, j):
        self.second_all[j].wait_recv()
        for copy in self.third[j]:
            copy.start()

    def slot_done(self, j):
        self.third_all[j].wait_recv()

    def done(self):
        for j in range(self.slots):
            self.slot_done(j)

    def sent(self):
        for copy in self.first:
            copy.wait_send()
        self.sent_rest()

    def sent_rest(self):
        self.second_sent.wait_send()
        self.third_sent.wait_send()


def is_active():
    c, _, z, _, _ = place()
    return z // 2 == c


def is_passive():
    return jnp.logical_not(is_active())


def half_slot(j):
    z = place()[2]
    return z % 2 if j == 0 else 1 - z % 2


class HalfGather(Gather):
    slots = 2

    def slot(self, j):
        return half_slot(j)

    def start(self):
        @pl.when(is_active())
        def _():
            for copy in self.first:
                copy.start()

    def arrived(self, j):
        if j == 1:

            @pl.when(is_active())
            def _():
                self.first[0].wait_recv()

        @pl.when(is_passive())
        def _():
            self.first[1 + j].wait_recv()

    def sent(self):
        @pl.when(is_active())
        def _():
            for copy in self.first:
                copy.wait_send()

        self.sent_rest()


def add_into(total, part):
    total[...] = total[...] + part[...]


class Scatter:
    order = (2, 3, 1, 0)

    def __init__(self, sems, grad, came1, came2, came3, rows):
        c, _, z, y, x = place()
        rows = self.rows = pl.ds(0, rows)
        self.grad, self.came1, self.came2, self.came3 = grad, came1, came2, came3
        send1, send2 = sems.new_send(), sems.new_send()
        self.first, self.first_all, self.second, self.second_all = [], [], [], []
        for j in range(len(self.order)):
            s = self.slot(j)
            got = sems.new_receive()
            self.first.append(
                [
                    sems.copy(grad.at[0, s, :, 1 - x, rows], came1.at[0, s], c, chip(z, y, 1 - x), send1, got),
                    sems.copy(grad.at[1, s, 1 - y, :, rows], came1.at[1, s], c, chip(z, 1 - y, x), send1, got),
                ]
            )
            self.first_all.append(joint(came1.at[:, s], (send1, got)))
            got = sems.new_receive()
            self.second.append(
                [
                    sems.copy(grad.at[0, s, 1 - y, x, rows], came2.at[0, s], c, chip(z, 1 - y, x), send2, got),
                    sems.copy(grad.at[1, s, y, 1 - x, rows], came2.at[1, s], c, chip(z, y, 1 - x), send2, got),
                ]
            )
            self.second_all.append(joint(came2.at[:, s], (send2, got)))
        self.first_sent = joint(came1, (send1, got))
        self.second_sent = joint(came2, (send2, got))
        got = sems.new_receive()
        self.third = [
            sems.copy(
                grad.at[:, self.slot(self.third_slot(j)), y, x, rows],
                came3.at[j - 1],
                c,
                chip(partner(z, j), y, x),
                None,
                got,
            )
            for j in (1, 2, 3)
        ]
        self.third_all = joint(came3, (send2, got))

    def slot(self, j):
        return partner(place()[2], j)

    def third_slot(self, j):
        return j

    def push1(self, j):
        for copy in self.first[j]:
            copy.start()

    def push2(self, j):
        _, _, _, y, x = place()
        s = self.slot(j)
        self.first_all[j].wait_recv()
        add_into(self.grad.at[0, s, 1 - y, x, self.rows], self.came1.at[0, s, 1 - y])
        self.second[j][0].start()
        add_into(self.grad.at[1, s, y, 1 - x, self.rows], self.came1.at[1, s, 1 - x])
        self.second[j][1].start()
        add_into(self.grad.at[0, s, y, x, self.rows], self.came1.at[0, s, y])
        add_into(self.grad.at[1, s, y, x, self.rows], self.came1.at[1, s, x])

    def push3(self, j):
        _, _, _, y, x = place()
        s = self.slot(j)
        self.second_all[j].wait_recv()
        for half in (0, 1):
            add_into(self.grad.at[half, s, y, x, self.rows], self.came2.at[half, s])
        self.send_on(j)

    def send_on(self, j):
        if j > 0:
            self.third[j - 1].start()

    def all1(self):
        for j in self.order:
            self.push1(j)

    def all2(self):
        for j in self.order:
            self.push2(j)

    def all3(self):
        for j in self.order:
            self.push3(j)

    def done(self):
        self.third_all.wait_recv()

    def sent(self):
        for copy in self.third:
            copy.wait_send()
        self.sent_rest()

    def sent_rest(self):
        self.first_sent.wait_send()
        self.second_sent.wait_send()

    def result(self, half):
        _, _, _, y, x = place()
        total = self.grad[half, self.slot(0), y, x, self.rows].astype(F32)
        for k in range(3):
            total = total + self.came3[k, half].astype(F32)
        return total


class HalfScatter(Scatter):
    order = (1, 0)

    def slot(self, j):
        return half_slot(j)

    def third_slot(self, j):
        return j % 2

    def send_on(self, j):
        if j == 1:

            @pl.when(is_active())
            def _():
                self.third[0].start()

        @pl.when(is_passive())
        def _():
            self.third[1 + j].start()

    def done(self):
        @pl.when(is_active())
        def _():
            self.third_all.wait_recv()

    def sent(self):
        @pl.when(is_active())
        def _():
            self.third[0].wait_send()

        @pl.when(is_passive())
        def _():
            self.third[1].wait_send()
            self.third[2].wait_send()

        self.sent_rest()


class AcrossGather:
    def __init__(self, sems, buf, first, count):
        c, _, z, y, x = place()
        rows = pl.ds(first, count)
        self.first = sems.copy(
            buf.at[:, z, y, x, rows], buf.at[:, z, y, x, rows], c, chip(z, y, 1 - x)
        )
        self.second = sems.copy(
            buf.at[:, z, y, :, rows], buf.at[:, z, y, :, rows], c, chip(z, 1 - y, x)
        )
        self.third = [
            sems.copy(
                buf.at[:, z, :, :, rows], buf.at[:, z, :, :, rows], c, chip(partner(z, j), y, x)
            )
            for j in (1, 2, 3)
        ]

    def start(self):
        self.first.start()

    def relay(self):
        self.first.wait_recv()
        self.second.start()

    def cross(self):
        self.second.wait_recv()
        for copy in self.third:
            copy.start()

    def done(self):
        for copy in self.third:
            copy.wait_recv()

    def sent(self):
        for copy in [self.first, self.second] + self.third:
            copy.wait_send()


class AcrossScatter:
    def __init__(self, sems, grad, came1, came2, came3, first, count):
        c, _, z, y, x = place()
        rows = self.rows = pl.ds(first, count)
        self.grad, self.came1, self.came2, self.came3 = grad, came1, came2, came3
        got = sems.new_receive()
        self.first = [
            sems.copy(
                grad.at[:, partner(z, j), :, :, rows],
                came1.at[j - 1],
                c,
                chip(partner(z, j), y, x),
                None,
                got,
            )
            for j in (1, 2, 3)
        ]
        self.first_all = joint(came1, (sems.new_send(), got))
        self.second = sems.copy(grad.at[:, z, 1 - y, :, rows], came2, c, chip(z, 1 - y, x))
        self.third = sems.copy(grad.at[:, z, y, 1 - x, rows], came3, c, chip(z, y, 1 - x))

    def push1(self):
        for copy in self.first:
            copy.start()

    def push2(self):
        _, _, z, y, _ = place()
        self.first_all.wait_recv()
        for row in (1 - y, y):
            for half in (0, 1):
                total = self.grad[half, z, row, :, self.rows].astype(F32)
                for k in range(3):
                    total = total + self.came1[k, half, row].astype(F32)
                self.grad[half, z, row, :, self.rows] = total.astype(BF16)
        self.second.start()

    def push3(self):
        _, _, z, y, _ = place()
        self.second.wait_recv()
        for half in (0, 1):
            add_into(self.grad.at[half, z, y, :, self.rows], self.came2.at[half])
        self.third.start()

    def done(self):
        self.third.wait_recv()

    def result(self, half):
        _, _, z, y, x = place()
        return self.grad[half, z, y, x, self.rows].astype(F32) + self.came3[half].astype(F32)

    def sent(self):
        for copy in self.first + [self.second, self.third]:
            copy.wait_send()


class Transpose:
    def __init__(self, sems, source, target):
        c, seq, _, _, _ = place()
        self.source, self.target = source, target
        pair = (sems.new_send(), sems.new_receive())
        self.copies = [
            sems.copy(source.at[(seq + k) % 16], target.at[seq], c, (seq + k) % 16, *pair)
            for k in range(1, 16)
        ]
        self.all = joint(target.at[pl.ds(0, 15)], pair)

    def start(self):
        _, seq, _, _, _ = place()
        for copy in self.copies:
            copy.start()
        self.target[seq] = self.source[seq]

    def done(self):
        self.all.wait_recv()

    def sent(self):
        self.all.wait_send()


def wide(tile, count=WIDE // LANES):
    return jnp.concatenate([tile] * count, axis=1)


def rows_of(ref, base):
    return jnp.broadcast_to(ref[pl.ds(base, 1), :], (16, LANES))


def spread(slab, j):
    return jnp.broadcast_to(slab[j : j + 1, :], (16, slab.shape[1]))


def put_partial(ref, j, value):
    folded = value[:8] + value[8:]
    for g in range(WIDE // LANES):
        ref[pl.ds(g * 64 + 8 * j, 8), :] = folded[:, g * LANES : (g + 1) * LANES]


def take_partial(ref):
    out = []
    for g in range(WIDE // LANES):
        total = ref[pl.ds(g * 64, 8, stride=8), :]
        for j in range(1, 8):
            total = total + ref[pl.ds(g * 64 + j, 8, stride=8), :]
        out.append(total)
    return jnp.concatenate(out, axis=1)


def fold_lanes(value):
    total = value[:, :LANES]
    for g in range(1, value.shape[1] // LANES):
        total = total + value[:, g * LANES : (g + 1) * LANES]
    return total


def dot_nn(a, b):
    return jnp.dot(a, b, preferred_element_type=F32)


def dot_nt(a, b):
    return lax.dot_general(a, b, contract_last, preferred_element_type=F32)


def dot_tn(a, b):
    return lax.dot_general(a, b, contract_first, preferred_element_type=F32)


def for_each(count, body):
    def step(i, carry):
        body(i)
        return carry

    lax.fori_loop(0, count, step, 0)


def lanes_at(i, width):
    return pl.ds(pl.multiple_of(i * width, width), width)


def fused_kernel(
    valid,
    hid_hbm,
    out_g_hbm,
    resets,
    in_w_hbm,
    out_w_hbm,
    x_w,
    dt_w,
    a_log,
    conv_w,
    vectors,
    o_out,
    o_gh,
    o_gin,
    o_gout,
    o_small,
    o_gain,
    hidb,
    gbr,
    kb,
    gain_b,
    nrm,
    nrm_t,
    xext,
    sig,
    delta,
    zz,
    gs,
    yy,
    bb,
    cb,
    a2,
    prm,
    hs,
    qb,
    qc,
    part1,
    part2,
    part3,
    gbc,
    low,
    mid,
    mid_t,
    gz,
    wx,
    wz,
    wo,
    wp,
    gx_w,
    gz_w,
    go_w,
    gp_w,
    x1,
    x2,
    x3,
    z1,
    z2,
    z3,
    o1,
    o2,
    o3,
    p1,
    p2,
    p3,
    c1,
    c2,
    c3,
    hp,
    hpr,
    hret,
    hin,
    lret,
    lin,
    lp,
    lpr,
    xd_out,
    xd_in,
    gext,
    gedge,
    rowx,
    rowx_in,
    fin,
    fin_in,
    fsm,
    in_w,
    out_g,
    load_sems,
    send_sems,
    recv_sems,
):
    c, seq, z, y, x = place()
    mate = 1 - c
    after = (seq + 1) % 16
    before = (seq + 15) % 16
    sems = Semaphores(send_sems, recv_sems)

    barrier = pltpu.get_barrier_semaphore()
    for k in range(1, 16):
        pl.semaphore_signal(
            barrier, inc=1, device_id=(c, (seq + k) % 16), device_id_type=MESH
        )
    pl.semaphore_signal(barrier, inc=1, device_id=(mate, seq), device_id_type=MESH)
    pl.semaphore_signal(barrier, inc=1, device_id=(mate, after), device_id_type=MESH)
    pl.semaphore_signal(barrier, inc=1, device_id=(mate, before), device_id_type=MESH)

    hid = hidb.at[c, pl.ds(16, ROWS), :]
    loads = [
        pltpu.make_async_copy(hid_hbm, hid, load_sems.at[0]),
        pltpu.make_async_copy(out_g_hbm, out_g, load_sems.at[1]),
    ]
    for half in (0, 1):
        for part, ref in ((0, wx), (1, wz)):
            at = pl.ds(pl.multiple_of(part * 2048 + c * 1024 + half * 512, 512), 512)
            loads.append(
                pltpu.make_async_copy(
                    in_w_hbm.at[:, at], ref.at[half, z, y, x], load_sems.at[2 + 2 * half + part]
                )
            )
    out_loads = [
        pltpu.make_async_copy(
            out_w_hbm.at[:, pl.ds(half * 512, 512)],
            wo.at[half, z % 2, y, x],
            load_sems.at[6 + half],
        )
        for half in (0, 1)
    ]
    in_load = pltpu.make_async_copy(in_w_hbm, in_w, load_sems.at[8])
    for load in loads:
        load.start()

    @pl.when(is_active())
    def _():
        for load in out_loads:
            load.start()

    in_load.start()

    @pl.when(z // 2 == c)
    def _():
        wp[0, z % 2, y, x] = x_w[...]
        wp[1, z % 2, y, x, 0:64, :] = dt_w[...]
        wp[1, z % 2, y, x, 64:80, :] = a_log[...]
        wp[1, z % 2, y, x, 80:96, :] = jnp.concatenate(
            [conv_w[...].astype(F32), vectors[0:3, :], jnp.zeros((9, LANES), F32)], axis=0
        ).astype(BF16)

    lane = lax.broadcasted_iota(jnp.int32, (8, LANES), 1)
    gain_mine = jnp.where(lane // 64 == x, jnp.broadcast_to(vectors[3:4, :], (8, LANES)), 0.0)
    gain_b[seq] = gain_mine
    kb[c] = jnp.transpose(
        jnp.broadcast_to(1.0 - resets[...].astype(F32), (ROWS, LANES))
    )
    row_place = seq * ROWS + lax.broadcasted_iota(jnp.int32, (ROWS, LANES), 0)
    live = (row_place < valid[0]).astype(F32)
    loads[1].wait()
    for g in range(GROUPS):
        at = slice(g * LANES, (g + 1) * LANES)
        gbr[c, :, at] = (live * out_g[:, at].astype(F32)).astype(BF16)

    loads[0].wait()
    for load in loads[2:]:
        load.wait()

    @pl.when(is_active())
    def _():
        for load in out_loads:
            load.wait()

    in_load.wait()
    pl.semaphore_wait(barrier, 18)

    gather_x = Gather(sems, wx, 64)
    gather_z = Gather(sems, wz, 48)
    across_z = AcrossGather(sems, wz, 48, 16)
    gather_o = HalfGather(sems, wo, 128)
    gather_p = HalfGather(sems, wp, 96)
    gain_sems = (sems.new_send(), sems.new_receive())
    gain_copies = [
        sems.copy(gain_b.at[seq], gain_b.at[seq], c, (seq + k) % 16, *gain_sems)
        for k in range(1, 16)
    ]
    gain_all = joint(gain_b.at[pl.ds(0, 15)], gain_sems)
    hid_copies = [
        sems.copy(hidb.at[c, pl.ds(16, ROWS), :], hidb.at[c, pl.ds(16, ROWS), :], mate, seq),
        sems.copy(hidb.at[c, pl.ds(128, 16), :], hidb.at[c, pl.ds(0, 16), :], c, after),
        sems.copy(hidb.at[c, pl.ds(128, 16), :], hidb.at[c, pl.ds(0, 16), :], mate, after),
        sems.copy(kb.at[c], kb.at[c], mate, seq),
    ]
    gbr_copy = sems.copy(gbr.at[c], gbr.at[c], mate, seq)
    for copy in hid_copies:
        copy.start()
    for copy in gain_copies:
        copy.start()
    across_z.start()
    gather_p.start()
    gather_x.start()
    gather_x.relay(0)

    for copy in hid_copies:
        copy.wait_recv()
    gather_p.relay(0)
    gather_p.relay(1)
    gain_all.wait_recv()
    gain_row = jnp.concatenate(
        [gain_b[2 * g][0:1, :] + gain_b[2 * g + 1][0:1, :] for g in range(GROUPS)], axis=1
    )
    for ctx in (0, 1):

        def norm_rows(i):
            at = pl.ds(pl.multiple_of(i * 16, 16), 16)
            rows = hidb[ctx, at, :].astype(F32)
            r = lax.rsqrt(jnp.mean(rows * rows, axis=1, keepdims=True) + epsilon)
            nrm[ctx, at, :] = (rows * r * gain_row).astype(BF16)

        for_each(9, norm_rows)
    gather_p.cross(0)
    gather_p.cross(1)
    gather_z.start()
    across_z.relay()
    for ctx in (0, 1):
        for g in range(GROUPS):
            at = slice(g * LANES, (g + 1) * LANES)
            nrm_t[at, ctx * ROWS : (ctx + 1) * ROWS] = jnp.transpose(
                nrm[ctx, 16:144, at].astype(F32)
            ).astype(BF16)

    gather_x.relay(1)
    gather_x.cross(0)
    gather_x.relay(2)
    gather_x.cross(1)
    gather_x.relay(3)
    gather_o.start()
    across_z.cross()
    gather_x.cross(2)
    gather_x.cross(3)
    gbr_copy.start()
    gather_z.relay(0)
    gather_x.done()
    gather_z.relay(1)
    gather_z.cross(0)
    first_chip = (seq > 0).astype(F32)
    for half in (0, 1):

        def x_columns(i):
            rows = nrm[...].reshape(288, 1024)
            w = wx[half, :, :, :, :, lanes_at(i, 256)].reshape(1024, 256)
            got = dot_nn(rows, w).astype(BF16).astype(F32)
            at = pl.ds(pl.multiple_of(half * 512 + i * 256, 256), 256)
            for ctx in (0, 1):
                xext[ctx, 0:16, at] = got[ctx * 144 : ctx * 144 + 16] * first_chip
                xext[ctx, 16:144, at] = got[ctx * 144 + 16 : ctx * 144 + 144]

        for_each(2, x_columns)

    gather_z.relay(2)
    gather_z.cross(1)
    gather_p.done()
    for j in range(GROUPS):
        prm[:, j * LANES : (j + 1) * LANES] = wp[
            1, j // 4, (j // 2) % 2, j % 2, 64:96, :
        ].astype(F32)
    a2[...] = -jnp.exp(prm[0:16, :]) * LOG2E

    def conv_rows(ctx, at):
        total = prm[20:21, at] + prm[16:17, at] * xext[ctx, 13:141, at]
        for k in range(1, 4):
            total = total + prm[16 + k : 17 + k, at] * xext[ctx, 13 + k : 141 + k, at]
        return total

    for ctx in (0, 1):

        def conv_columns(i):
            at = lanes_at(i, LANES)
            total = conv_rows(ctx, at)
            rows = slice(ctx * ROWS, (ctx + 1) * ROWS)
            sig[rows, at] = (total * jax.nn.sigmoid(total)).astype(BF16)

        for_each(GROUPS, conv_columns)

    total = jnp.zeros((256, 96), F32)
    for j in range(GROUPS):
        total = total + dot_nt(
            sig[:, j * LANES : (j + 1) * LANES], wp[0, j // 4, (j // 2) % 2, j % 2]
        )
    xd_out[:, 0:96] = total
    xd_out[:, 96:128] = jnp.zeros((256, 32), F32)
    xd_copy = sems.copy(xd_out, xd_in, mate, seq)
    xd_copy.start()
    gather_z.relay(3)
    gather_z.cross(2)
    xd_copy.wait()
    xd = xd_out[...] + xd_in[...]
    low[...] = xd[:, 0:64].astype(BF16)
    for n in range(16):
        bb[pl.ds(n, 256, stride=16), :] = jnp.broadcast_to(xd[:, 64 + n : 65 + n], (256, LANES))
        cb[pl.ds(n, 256, stride=16), :] = jnp.broadcast_to(xd[:, 80 + n : 81 + n], (256, LANES))
    for j in range(GROUPS):
        at = slice(j * LANES, (j + 1) * LANES)
        pre = dot_nn(low[...], wp[1, j // 4, (j // 2) % 2, j % 2, 0:64, :]) + prm[21:22, at]
        decay_of = jnp.exp(-jnp.abs(pre))
        small_log = decay_of * (1.0 - decay_of * (0.5 - decay_of * (1.0 / 3.0)))
        delta[:, at] = jnp.maximum(pre, 0.0) + jnp.where(
            decay_of < 0.01, small_log, jnp.log1p(decay_of)
        )

    gather_z.cross(3)

    def decay(slab, j, a, base):
        return jnp.exp2(spread(slab, j) * a) * wide(rows_of(kb2, base))

    kb2 = kb.reshape(256, LANES)

    def tile16(ref, t):
        return ref[pl.ds(pl.multiple_of(t * 16, 16), 16), :]

    def forward_ends(q):
        ctx, block = q // 2, q % 2
        at = lanes_at(block, WIDE)
        a = a2[:, at]

        def eight(i, h):
            t0 = pl.multiple_of(ctx * ROWS + i * 8, 8)
            d = delta[pl.ds(t0, 8), at]
            u = d * slab_of(sig, t0, at)
            for j in range(8):
                h = decay(d, j, a, t0 + j) * h + spread(u, j) * wide(tile16(bb, t0 + j))
            return h

        h = lax.fori_loop(0, 16, eight, jnp.zeros((16, WIDE), F32))
        rows = pl.ds(pl.multiple_of(ctx * ROWS, ROWS), ROWS)
        summed = jnp.sum(delta[rows, at], axis=0, keepdims=True)
        kept = jnp.min(kb[ctx], axis=0, keepdims=True)
        decays = jnp.exp2(jnp.broadcast_to(summed, (16, WIDE)) * a) * wide(
            jnp.broadcast_to(kept, (16, LANES))
        )
        for g in range(4):
            piece = ctx * GROUPS + block * 4 + g
            hp[piece, 0] = h[:, g * LANES : (g + 1) * LANES]
            hp[piece, 1] = decays[:, g * LANES : (g + 1) * LANES]

    def slab_of(ref, t0, at):
        base = pl.multiple_of((t0 // 16) * 16, 16)
        both = ref[pl.ds(base, 16), at].astype(F32)
        return jnp.where(t0 % 16 == 0, both[:8], both[8:])

    for_each(4, forward_ends)
    send_ends = Transpose(sems, hp, hpr)
    send_ends.start()
    gather_o.relay(0)
    gather_o.relay(1)

    def z_columns(i):
        rows = nrm_rows()
        for half in (0, 1):
            w = wz[half, :, :, :, :, lanes_at(i, 256)].reshape(1024, 256)
            at = pl.ds(pl.multiple_of(half * 512 + i * 256, 256), 256)
            zz[:, at] = dot_nn(rows, w)

    def nrm_rows():
        return jnp.concatenate([nrm[0, 16:144, :], nrm[1, 16:144, :]], axis=0)

    send_ends.done()
    state = jnp.zeros((16, LANES), F32)
    for s in range(16):
        hret[s] = state
        state = hpr[s, 1] * state + hpr[s, 0]
    return_states = Transpose(sems, hret, hin)
    return_states.start()
    gather_o.cross(0)
    gather_o.cross(1)
    gather_z.done()
    across_z.done()
    for_each(2, z_columns)

    def forward(q):
        ctx, block = q // 2, q % 2
        at = lanes_at(block, WIDE)
        a = a2[:, at]
        h0 = jnp.concatenate([hin[ctx * GROUPS + block * 4 + g] for g in range(4)], axis=1)
        hs[ctx * 129, :, at] = h0

        def eight(i, h):
            t0 = pl.multiple_of(ctx * ROWS + i * 8, 8)
            d = delta[pl.ds(t0, 8), at]
            s8 = slab_of(sig, t0, at)
            u = d * s8
            for j in range(8):
                h = decay(d, j, a, t0 + j) * h + spread(u, j) * wide(tile16(bb, t0 + j))
                hs[t0 + ctx + j + 1, :, at] = h
                put_partial(part1, j, h * wide(tile16(cb, t0 + j)))
            yy[pl.ds(t0, 8), at] = take_partial(part1) + prm[22:23, at] * s8
            return h

        lax.fori_loop(0, 16, eight, h0)

    gbr_copy.wait_recv()

    def branch_back(i):
        branch = gbr[...].reshape(256, 1024)
        w0 = wo[0, i // 2, i % 2].reshape(256, 512)
        w1 = wo[1, i // 2, i % 2].reshape(256, 512)
        gm = dot_nt(branch[:, :512], w0) + dot_nt(branch[:, 512:], w1)
        at = lanes_at(i, 256)
        zv = zz[:, at]
        sigma = jax.nn.sigmoid(zv)
        gs[:, at] = gm * (zv * sigma)
        gz[:, at] = (gm * yy[:, at] * (sigma * (1.0 + zv * (1.0 - sigma)))).astype(BF16)

    def z_grads(i):
        d = pl.ds(pl.multiple_of(i * 128, 128), 128)
        for half in (0, 1):
            got = dot_nn(nrm_t[d, :], gz[:, half * 512 : (half + 1) * 512])
            gz_w[half, i // 2, i % 2] = got.astype(BF16).reshape(2, 64, 512)

    def backward_ends(q):
        ctx, block = q // 2, q % 2
        at = lanes_at(block, WIDE)
        a = a2[:, at]

        def eight(i, adj):
            t0 = pl.multiple_of(ctx * ROWS + (15 - i) * 8, 8)
            d = delta[pl.ds(t0, 8), at]
            u = gs[pl.ds(t0, 8), at]
            for j in range(7, -1, -1):
                adj = decay(d, j, a, t0 + j) * (adj + spread(u, j) * wide(tile16(cb, t0 + j)))
            return adj

        adj = lax.fori_loop(0, 16, eight, jnp.zeros((16, WIDE), F32))
        for g in range(4):
            lp[ctx * GROUPS + block * 4 + g] = adj[:, g * LANES : (g + 1) * LANES]

    return_states.done()
    for_each(4, forward)
    for ctx in (0, 1):
        for g in range(GROUPS):
            at = slice(g * LANES, (g + 1) * LANES)
            rows = slice(ctx * ROWS, (ctx + 1) * ROWS)
            zv = zz[rows, at]
            val = (yy[rows, at] * zv * jax.nn.sigmoid(zv)).astype(BF16)
            mid[rows, at] = val
            mid_t[at, rows] = jnp.transpose(val.astype(F32)).astype(BF16)

    def out_grads(i):
        e = pl.ds(pl.multiple_of(i * 256, 256), 256)
        branch = gbr[...].reshape(256, 1024)
        for half in (0, 1):
            got = dot_nn(mid_t[e, :], branch[:, half * 512 : (half + 1) * 512])
            go_w[half, i // 2, i % 2] = got.astype(BF16).reshape(2, 128, 512)

    for_each(4, out_grads)
    scatter_o = HalfScatter(sems, go_w, o1, o2, o3, 128)
    scatter_o.push1(1)

    for j in (0, 1):
        gather_o.slot_done(j)
        block = half_slot(j)
        branch_back(2 * block)
        branch_back(2 * block + 1)
        backward_ends(block)
        backward_ends(2 + block)
    send_adj = Transpose(sems, lp, lpr)
    send_adj.start()
    for_each(8, z_grads)
    scatter_z = Scatter(sems, gz_w, z1, z2, z3, 48)
    across_gz = AcrossScatter(sems, gz_w, c1, c2, c3, 48, 16)
    send_adj.done()
    state = jnp.zeros((16, LANES), F32)
    for s in range(15, -1, -1):
        lret[s] = state
        state = hpr[s, 1] * state + lpr[s]
    return_adj = Transpose(sems, lret, lin)
    return_adj.start()
    scatter_o.push1(0)
    across_gz.push1()
    scatter_z.push1(2)
    scatter_z.push1(3)
    for half in (0, 1):
        got = dot_nn(mid[...], wo[half].reshape(1024, 512))
        for ctx in (0, 1):
            rowx[ctx, :, half * 512 : (half + 1) * 512] = got[ctx * ROWS : (ctx + 1) * ROWS]
    rows_copy = sems.copy(rowx.at[mate], rowx_in.at[0], mate, seq)
    rows_copy.start()
    return_adj.done()

    sub = lax.broadcasted_iota(jnp.int32, (8, LANES), 0)
    pick_b = [(lane == 64 + 8 * k + sub).astype(F32) for k in (0, 1)]
    pick_c = [(lane == 80 + 8 * k + sub).astype(F32) for k in (0, 1)]
    all_ones = jnp.ones((LANES, LANES), BF16)
    def backward(ctx, block):
        at = slice(block * WIDE, (block + 1) * WIDE)
        a = a2[:, at]

        def eight(i, carry):
            adj, grad_a = carry
            t0 = pl.multiple_of(ctx * ROWS + (15 - i) * 8, 8)
            d = delta[pl.ds(t0, 8), at]
            g8 = gs[pl.ds(t0, 8), at]
            u = d * slab_of(sig, t0, at)
            h_next = hs[t0 + ctx + 8, :, at]
            for j in range(7, -1, -1):
                t = t0 + j
                dj = spread(d, j)
                gj = spread(g8, j)
                lam = adj + gj * wide(tile16(cb, t))
                adj = jnp.exp2(dj * a) * wide(rows_of(kb2, t)) * lam
                h_prev = hs[t + ctx, :, at]
                flow = adj * h_prev
                grad_a = grad_a + flow * dj
                put_partial(part1, j, flow * a)
                put_partial(part2, j, lam * wide(tile16(bb, t)))
                to = pl.ds(pl.multiple_of((t - ctx * ROWS) * 16, 16), 16)
                qb[block, to, :] = fold_lanes(lam * spread(u, j)).astype(BF16)
                qc[block, to, :] = fold_lanes(gj * h_next).astype(BF16)
                h_next = h_prev
            yy[pl.ds(t0, 8), at] = take_partial(part1) * (1.0 / LOG2E)
            zz[pl.ds(t0, 8), at] = take_partial(part2)
            return adj, grad_a

        adj0 = jnp.concatenate([lin[ctx * GROUPS + block * 4 + g] for g in range(4)], axis=1)
        _, grad_a = lax.fori_loop(0, 16, eight, (adj0, jnp.zeros((16, WIDE), F32)))
        hs[ctx * 129, :, at] = grad_a

    def sum_lanes(ctx, i):
        for k in range(2):
            t0 = pl.multiple_of(i * 32 + k * 16, 16)
            at = pl.ds(pl.multiple_of(t0 * 16, 256), 256)
            sum_b = dot_nn(qb[0, at, :], all_ones) + dot_nn(qb[1, at, :], all_ones)
            sum_c = dot_nn(qc[0, at, :], all_ones) + dot_nn(qc[1, at, :], all_ones)
            for j in range(16):
                got = sum_b[16 * j : 16 * j + 8] * pick_b[0]
                got = got + sum_b[16 * j + 8 : 16 * j + 16] * pick_b[1]
                got = got + sum_c[16 * j : 16 * j + 8] * pick_c[0]
                got = got + sum_c[16 * j + 8 : 16 * j + 16] * pick_c[1]
                part3[k * 128 + 8 * j : k * 128 + 8 * j + 8, :] = got
            for j in range(2):
                got = part3[pl.ds(k * 128 + j * 64, 8, stride=8), :]
                for n in range(1, 8):
                    got = got + part3[pl.ds(k * 128 + j * 64 + n, 8, stride=8), :]
                gbc[pl.ds(pl.multiple_of(ctx * ROWS + t0 + 8 * j, 8), 8), :] = got

    backward(0, 0)
    scatter_o.push2(1)
    scatter_z.push1(1)
    backward(0, 1)
    scatter_o.push2(0)
    scatter_z.push1(0)
    for_each(4, functools.partial(sum_lanes, 0))
    backward(1, 0)
    across_gz.push2()
    scatter_z.push2(2)
    backward(1, 1)
    scatter_o.push3(1)
    scatter_z.push2(3)
    for_each(4, functools.partial(sum_lanes, 1))

    ones = []
    for j in range(GROUPS):
        at = slice(j * LANES, (j + 1) * LANES)
        sv = sig[:, at].astype(F32)
        step = delta[:, at]
        small_sigmoid = step * (1.0 - step * (0.5 - step * (1.0 / 6.0 - step * (1.0 / 24.0))))
        sigma = jnp.where(step < 0.125, small_sigmoid, 1.0 - jnp.exp(-step))
        g_pre = ((yy[:, at] + zz[:, at] * sv) * sigma).astype(BF16)
        mid[:, at] = g_pre
        ones.append(jnp.sum(g_pre.astype(F32), axis=0, keepdims=True))
    g_bdt = jnp.concatenate(ones, axis=1)

    total = jnp.zeros((256, 64), F32)
    for j in range(GROUPS):
        total = total + dot_nt(
            mid[:, j * LANES : (j + 1) * LANES], wp[1, j // 4, (j // 2) % 2, j % 2, 0:64, :]
        )
    xd_out[:, 0:64] = total
    xd_out[:, 64:128] = gbc[:, 64:128]
    gd_copy = sems.copy(xd_out, xd_in, mate, seq)
    rows_copy.wait()
    gd_copy.start()
    across_gz.push3()
    for g in range(GROUPS):
        at = slice(g * LANES, (g + 1) * LANES)
        o_out[:, at] = (
            hidb[c, 16:144, at].astype(F32) + live * (rowx[c, :, at] + rowx_in[0, :, at])
        ).astype(BF16)
    scatter_z.push2(1)
    gd_copy.wait()
    g_dbl = (xd_out[...] + xd_in[...]).astype(BF16)

    for ctx in (0, 1):
        for j in range(GROUPS):
            at = slice(j * LANES, (j + 1) * LANES)
            rows = slice(ctx * ROWS, (ctx + 1) * ROWS)
            back = dot_nn(g_dbl[rows, 0:96], wp[0, j // 4, (j // 2) % 2, j % 2])
            g_sig = gs[rows, at] * prm[22:23, at] + zz[rows, at] * delta[rows, at] + back
            v = conv_rows(ctx, at)
            sigma = jax.nn.sigmoid(v)
            gext[ctx, 0:128, at] = g_sig * (sigma * (1.0 + v * (1.0 - sigma)))
    edge_copies = [
        sems.copy(gext.at[ctx, pl.ds(0, 8), :], gedge.at[ctx], c, before) for ctx in (0, 1)
    ]
    for copy in edge_copies:
        copy.start()
    scatter_z.push2(0)
    scatter_o.push3(0)

    def small_grads():
        a_rows = -jnp.exp(prm[0:16, :])
        g_alog = (hs[0] + hs[129]) * a_rows
        g_t = jnp.transpose(g_dbl.astype(F32))[0:96].astype(BF16)
        low_t = jnp.transpose(
            jnp.concatenate([low[...].astype(F32), jnp.zeros((256, 64), F32)], axis=1)
        )[0:64].astype(BF16)
        for j in range(GROUPS):
            at = slice(j * LANES, (j + 1) * LANES)
            to = (j // 4, (j // 2) % 2, j % 2)
            sv = sig[:, at].astype(F32)
            gp_w[(0,) + to] = dot_nn(g_t, sig[:, at]).astype(BF16)
            g_dtw = dot_nn(low_t, mid[:, at])
            taps = []
            for k in range(4):
                term = jnp.zeros((1, LANES), F32)
                for ctx in (0, 1):
                    term = term + jnp.sum(
                        gext[ctx, 0:128, at] * xext[ctx, 13 + k : 141 + k, at],
                        axis=0,
                        keepdims=True,
                    )
                taps.append(term)
            bias = jnp.sum(gext[0, 0:128, at] + gext[1, 0:128, at], axis=0, keepdims=True)
            skip = jnp.sum(gs[:, at] * sv, axis=0, keepdims=True)
            rest = jnp.concatenate(
                [g_dtw, g_alog[:, at]]
                + taps
                + [bias, g_bdt[:, at], skip, jnp.zeros((9, LANES), F32)],
                axis=0,
            )
            gp_w[(1,) + to] = rest.astype(BF16)

    small_grads()
    scatter_p = HalfScatter(sems, gp_w, p1, p2, p3, 96)
    scatter_p.all1()

    for copy in edge_copies:
        copy.wait_recv()
    last_chip = (seq < 15).astype(F32)
    for ctx in (0, 1):
        gext[ctx, 128:136, :] = gedge[ctx] * last_chip

    for ctx in (0, 1):

        def x_back(i):
            at = lanes_at(i, LANES)
            total = prm[19:20, at] * gext[ctx, 0:128, at]
            for k in range(3):
                total = total + prm[16 + k : 17 + k, at] * gext[ctx, 3 - k : 131 - k, at]
            mid[ctx * ROWS : (ctx + 1) * ROWS, at] = total.astype(BF16)

        for_each(GROUPS, x_back)

    def x_grads(i):
        d = pl.ds(pl.multiple_of(i * 128, 128), 128)
        for half in (0, 1):
            got = dot_nn(nrm_t[d, :], mid[:, half * 512 : (half + 1) * 512])
            gx_w[half, i // 2, i % 2] = got.astype(BF16).reshape(2, 64, 512)

    scatter_x = Scatter(sems, gx_w, x1, x2, x3, 64)
    for j in scatter_x.order:
        zj = partner(z, j)
        x_grads(2 * zj)
        x_grads(2 * zj + 1)
        scatter_x.push1(j)
        scatter_z.push3(j)
    def normed_back(i):
        total = jnp.zeros((256, 128), F32)
        for half in (0, 1):
            at = slice(half * 512, (half + 1) * 512)
            total = total + dot_nt(mid[:, at], wx[half, i // 2, i % 2].reshape(128, 512))
            total = total + dot_nt(gz[:, at], wz[half, i // 2, i % 2].reshape(128, 512))
        to = lanes_at(i, 128)
        for ctx in (0, 1):
            rowx[ctx, :, to] = total[ctx * ROWS : (ctx + 1) * ROWS]

    for i in range(4):
        normed_back(i)
    scatter_p.all2()
    scatter_x.push2(2)
    for i in range(4, 8):
        normed_back(i)
    back_copy = sems.copy(rowx.at[mate], rowx_in.at[1], mate, seq)
    back_copy.start()
    scatter_x.push2(3)
    scatter_p.all3()
    scatter_x.push2(1)

    def hidden_rows(i):
        at = pl.ds(pl.multiple_of(i * 16, 16), 16)
        rows = hidb[c, pl.ds(pl.multiple_of(16 + i * 16, 16), 16), :].astype(F32)
        r = lax.rsqrt(jnp.mean(rows * rows, axis=1, keepdims=True) + epsilon)
        g_hat = (rowx[c, at, :] + rowx_in[1, at, :]) * gain_row
        inner = jnp.mean(g_hat * rows, axis=1, keepdims=True)
        o_gh[at, :] = r * g_hat - rows * (r * r * r * inner) + out_g[at, :].astype(F32)

    back_copy.wait()
    for_each(8, hidden_rows)
    scatter_x.push3(2)
    scatter_x.push2(0)
    scatter_x.push3(3)
    scatter_x.push3(1)
    scatter_x.push3(0)
    scatter_o.done()
    out_copy = sems.copy(o_gout, o_gout, mate, seq)

    @pl.when(is_active())
    def _():
        for half in (0, 1):
            o_gout[:, half * 512 : (half + 1) * 512] = scatter_o.result(half)
        out_copy.start()

    scatter_z.done()
    across_gz.done()
    for half in (0, 1):
        fin[2 + half, 0:48, :] = scatter_z.result(half)
        fin[2 + half, 48:64, :] = across_gz.result(half)
    z_copy = sems.copy(fin.at[pl.ds(2, 2)], fin_in.at[pl.ds(2, 2)], mate, seq)
    z_copy.start()
    scatter_p.done()
    small_copy = sems.copy(fsm, fsm, mate, seq)

    @pl.when(is_active())
    def _():
        for half in (0, 1):
            fsm[half * 96 : (half + 1) * 96, :] = scatter_p.result(half)
        small_copy.start()

    def weight_rows(part, gain_sum):
        for half in (0, 1):
            for core, ref in ((c, fin), (mate, fin_in)):
                at = pl.ds(pl.multiple_of(part * 2048 + core * 1024 + half * 512, 512), 512)
                rows = ref[part * 2 + half]
                o_gin[:, at] = rows
                gain_sum = gain_sum + fold_lanes(rows * in_w[:, at].astype(F32))
        return gain_sum

    z_copy.wait()
    gain_sum = weight_rows(1, jnp.zeros((64, LANES), F32))
    for group in (gather_x, gather_z, gather_o, gather_p, scatter_z, scatter_o):
        group.sent()
    for group in (across_z, across_gz, send_ends, return_states, send_adj, return_adj):
        group.sent()
    for copy in hid_copies + edge_copies + [gbr_copy, gain_all]:
        copy.wait_send()

    scatter_x.done()
    for half in (0, 1):
        fin[half] = scatter_x.result(half)
    x_copy = sems.copy(fin.at[pl.ds(0, 2)], fin_in.at[pl.ds(0, 2)], mate, seq)
    x_copy.start()

    @pl.when(is_active())
    def _():
        out_copy.wait_send()
        small_copy.wait_send()

    @pl.when(is_passive())
    def _():
        out_copy.wait_recv()
        small_copy.wait_recv()

    o_small[...] = fsm[...]
    scatter_x.sent()
    scatter_p.sent()
    x_copy.wait()
    o_gain[...] = weight_rows(0, gain_sum)


def fused_shards(
    hidden,
    out_grad,
    resets,
    valid,
    norm_gain,
    in_weight,
    conv_weight,
    conv_bias,
    x_weight,
    dt_weight,
    dt_bias,
    a_log,
    skip_gain,
    out_weight,
):
    norm_row = norm_gain.astype(F32)
    vectors = jnp.stack(
        [
            conv_bias.astype(F32),
            dt_bias.astype(F32),
            skip_gain.astype(F32),
            jnp.concatenate([norm_row, norm_row]),
        ]
    )
    vmem = pltpu.VMEM
    sends, receives = 71, 92
    scratch = [
        vmem((2, 144, 1024), BF16),
        vmem((2, 128, 1024), BF16),
        vmem((2, 128, LANES), F32),
        vmem((16, 8, LANES), F32),
        vmem((2, 144, 1024), BF16),
        vmem((1024, 256), BF16),
        vmem((2, 144, 1024), F32),
        vmem((256, 1024), BF16),
        vmem((256, 1024), F32),
        vmem((256, 1024), F32),
        vmem((256, 1024), F32),
        vmem((256, 1024), F32),
        vmem((4096, LANES), F32),
        vmem((4096, LANES), F32),
        vmem((16, 1024), F32),
        vmem((32, 1024), F32),
        vmem((258, 16, 1024), F32),
        vmem((2, 2048, LANES), BF16),
        vmem((2, 2048, LANES), BF16),
        vmem((256, LANES), F32),
        vmem((256, LANES), F32),
        vmem((256, LANES), F32),
        vmem((256, LANES), F32),
        vmem((256, 64), BF16),
        vmem((256, 1024), BF16),
        vmem((1024, 256), BF16),
        vmem((256, 1024), BF16),
        vmem((2, 4, 2, 2, 64, 512), BF16),
        vmem((2, 4, 2, 2, 64, 512), BF16),
        vmem((2, 2, 2, 2, 128, 512), BF16),
        vmem((2, 2, 2, 2, 96, LANES), BF16),
        vmem((2, 4, 2, 2, 64, 512), BF16),
        vmem((2, 4, 2, 2, 64, 512), BF16),
        vmem((2, 2, 2, 2, 128, 512), BF16),
        vmem((2, 2, 2, 2, 96, LANES), BF16),
    ]
    for z_count, rows, columns in ((4, 64, 512), (4, 48, 512), (2, 128, 512)):
        scratch += [
            vmem((2, z_count, 2, rows, columns), BF16),
            vmem((2, z_count, rows, columns), BF16),
            vmem((3, 2, rows, columns), BF16),
        ]
    scratch += [
        vmem((2, 2, 2, 96, LANES), BF16),
        vmem((2, 2, 96, LANES), BF16),
        vmem((3, 2, 96, LANES), BF16),
        vmem((3, 2, 2, 2, 16, 512), BF16),
        vmem((2, 2, 16, 512), BF16),
        vmem((2, 16, 512), BF16),
        vmem((16, 2, 16, LANES), F32),
        vmem((16, 2, 16, LANES), F32),
        vmem((16, 16, LANES), F32),
        vmem((16, 16, LANES), F32),
        vmem((16, 16, LANES), F32),
        vmem((16, 16, LANES), F32),
        vmem((16, 16, LANES), F32),
        vmem((16, 16, LANES), F32),
        vmem((256, LANES), F32),
        vmem((256, LANES), F32),
        vmem((2, 136, 1024), F32),
        vmem((2, 8, 1024), F32),
        vmem((2, 128, 1024), F32),
        vmem((2, 128, 1024), F32),
        vmem((4, 64, 512), F32),
        vmem((4, 64, 512), F32),
        vmem((192, LANES), F32),
        vmem((64, 4096), BF16),
        vmem((128, 1024), BF16),
        pltpu.SemaphoreType.DMA((9,)),
        pltpu.SemaphoreType.DMA((sends,)),
        pltpu.SemaphoreType.DMA((receives,)),
    ]
    whole = pl.BlockSpec(memory_space=pltpu.VMEM)
    hbm = pl.BlockSpec(memory_space=pl.ANY)
    parts = pl.pallas_call(
        fused_kernel,
        out_shape=(
            jax.ShapeDtypeStruct((128, 1024), BF16),
            jax.ShapeDtypeStruct((128, 1024), F32),
            jax.ShapeDtypeStruct((64, 4096), F32),
            jax.ShapeDtypeStruct((128, 1024), F32),
            jax.ShapeDtypeStruct((192, LANES), F32),
            jax.ShapeDtypeStruct((64, LANES), F32),
        ),
        in_specs=[pl.BlockSpec(memory_space=pltpu.SMEM), hbm, hbm, whole, hbm, hbm] + [whole] * 5,
        out_specs=(whole,) * 6,
        scratch_shapes=scratch,
        compiler_params=pltpu.CompilerParams(
            collective_id=0, has_side_effects=True, vmem_limit_bytes=64 * 2**20
        ),
    )(
        valid,
        hidden[0],
        out_grad[0],
        resets,
        in_weight,
        out_weight,
        x_weight.T,
        dt_weight.T,
        a_log.T,
        conv_weight.T,
        vectors,
    )
    got = pl.pallas_call(
        place_outputs,
        out_shape=tuple(
            jax.ShapeDtypeStruct(shape, dtype)
            for shape, dtype in (
                ((128, 1024), BF16),
                ((128, 1024), F32),
                ((1, 64), F32),
                ((64, 4096), F32),
                ((4, LANES), F32),
                ((1, LANES), F32),
                ((96, LANES), F32),
                ((64, LANES), F32),
                ((1, LANES), F32),
                ((16, LANES), F32),
                ((1, LANES), F32),
                ((128, 1024), F32),
            )
        ),
        in_specs=[whole] * 7,
        out_specs=(whole,) * 12,
        compiler_params=pltpu.CompilerParams(vmem_limit_bytes=64 * 2**20),
    )(*parts, vectors)
    return (
        got[0][None],
        got[1][None],
        got[2][0],
        got[3],
        got[4].T,
        got[5][0],
        got[6].T,
        got[7].T,
        got[8][0],
        got[9].T,
        got[10][0],
        got[11],
    )


def place_outputs(
    out,
    g_hidden,
    g_in,
    g_out,
    small,
    gain,
    vectors,
    o_out,
    o_hidden,
    o_gain,
    o_in,
    o_taps,
    o_bias,
    o_xw,
    o_dtw,
    o_dtb,
    o_alog,
    o_skip,
    o_outw,
):
    o_out[...] = out[...]
    o_hidden[...] = g_hidden[...]
    o_in[...] = g_in[...]
    o_outw[...] = g_out[...]
    o_xw[...] = small[0:96, :]
    o_dtw[...] = small[96:160, :]
    o_alog[...] = small[160:176, :]
    o_taps[...] = small[176:180, :]
    o_bias[...] = small[180:181, :]
    o_dtb[...] = small[181:182, :]
    o_skip[...] = small[182:183, :]
    turned = jnp.transpose(jnp.concatenate([gain[...], jnp.zeros((64, LANES), F32)], axis=0))
    o_gain[...] = (jnp.sum(turned, axis=0, keepdims=True) / vectors[3:4, :])[:, 0:64]


def solution(mesh):
    sizes = dict(mesh.shape)
    body = fused_shards if sizes == {"ctx": 2, "seq": 16} else shards
    return jax.shard_map(
        body,
        mesh=mesh,
        in_specs=(
            P("ctx", "seq", None),
            P("ctx", "seq", None),
            P("ctx", "seq"),
            P("ctx"),
            P("seq"),
            P("seq", None),
            P("seq", None),
            P("seq"),
            P("seq", None),
            P("seq", None),
            P("seq"),
            P("seq", None),
            P("seq"),
            P("seq", None),
        ),
        out_specs=(
            P("ctx", "seq", None),
            P("ctx", "seq", None),
            P("seq"),
            P("seq", None),
            P("seq", None),
            P("seq"),
            P("seq", None),
            P("seq", None),
            P("seq"),
            P("seq", None),
            P("seq"),
            P("seq", None),
        ),
        check_vma=False,
    )
```
